32 devices in a mesh: dp: 16 (over z, x, core), tensor: 2 (over y).
Axes of the slice: x: 2, y: 2, z: 4, core: 2. Of those that a mesh axis runs over, the one named last changes fastest.
Arguments:
- tokens: bfloat16 [16, 1376, 1024], P('dp', 'tensor'), may hold values from -16 to 16
- cotangent: bfloat16 [16, 1376, 1024], P('dp', 'tensor'), may hold values from -6 to 6
- lengths: int32 [16], P('dp'), may hold values from 0 to 1370, as said below
- adapter_ids: int32 [16], P('dp'), may hold values from 0 to 7
- gain_one: float32 [1024], replicated, may hold values from 0.25 to 1.75
- gain_two: float32 [1024], replicated, may hold values from 0.25 to 1.75
- scale_one: float32 [1024], replicated, may hold values from 0.5 to 2
- scale_two: float32 [1024], replicated, may hold values from 0.5 to 2
- w_qkv: bfloat16 [1024, 3, 1024], P(None, None, 'tensor'), may hold values from -0.1875 to 0.1875
- w_out: bfloat16 [1024, 1024], P('tensor'), may hold values from -1 to 1
- w_up: bfloat16 [1024, 4096], P(None, 'tensor'), may hold values from -0.1875 to 0.1875
- w_down: bfloat16 [4096, 1024], P('tensor'), may hold values from -0.09375 to 0.09375
- qkv_a: bfloat16 [8, 16, 1024], replicated, may hold values from -0.1875 to 0.1875
- qkv_b: bfloat16 [8, 3, 1024, 16], P(None, None, 'tensor'), may hold values from -1.5 to 1.5
- out_a: bfloat16 [8, 16, 1024], P(None, None, 'tensor'), may hold values from -1 to 1
- out_b: bfloat16 [8, 1024, 16], replicated, may hold values from -1.5 to 1.5
- up_a: bfloat16 [8, 16, 1024], replicated, may hold values from -0.1875 to 0.1875
- up_b: bfloat16 [8, 4096, 16], P(None, 'tensor'), may hold values from -1.5 to 1.5
- down_a: bfloat16 [8, 16, 4096], P(None, None, 'tensor'), may hold values from -0.09375 to 0.09375
- down_b: bfloat16 [8, 1024, 16], replicated, may hold values from -1.5 to 1.5
Outputs:
- layer_out: bfloat16 [16, 1376, 1024], P('dp', 'tensor')
- grad_tokens: float32 [16, 1376, 1024], P('dp', 'tensor')
- grad_qkv_a: float32 [8, 16, 1024], replicated
- grad_qkv_b: float32 [8, 3, 1024, 16], P(None, None, 'tensor')
- grad_out_a: float32 [8, 16, 1024], P(None, None, 'tensor')
- grad_out_b: float32 [8, 1024, 16], replicated
- grad_up_a: float32 [8, 16, 1024], replicated
- grad_up_b: float32 [8, 4096, 16], P(None, 'tensor')
- grad_down_a: float32 [8, 16, 4096], P(None, None, 'tensor')
- grad_down_b: float32 [8, 1024, 16], replicated
The draws below stay inside these ranges and needn't reach their ends.
Inputs may be any that keep to these rules, and one draw needn't show every extreme that they name: `lengths`: slots g * 1 to g + 1 - 1 belong to group g of the dp axis; the first c of them hold images, with c from (2) // 2 to 1, each of 685 to 1370 valid tokens, and the others are empty with length 0.
All inputs are finite; a program needn't handle non-finite values.
Results may differ from the reference program's by a relative error of at most 0.014.
The reference program's roundings to bfloat16 on the way count: a program that leaves them out, or rounds other values in their place, can miss the bound.
Values may be sent and summed in bfloat16 or wider, within the bound.
No kernel may reach another device: no remote copies, remote signals or barrier semaphores. Data moves between devices by JAX's collectives and lax.ppermute only.
A program may use at most 384 MiB of HBM per device.

```python
import math
import jax
import jax.numpy as jnp
from jax import lax

D = 1024
HEADS = 16
HD = 64
FF = 4096
RANK = 16
ADAPTERS = 8
SEQ = 1376
VALID = 1370
SLOT_DEV = 1
SLOTS = 16


def draw_tokens(key, part):
    key_noise, key_rows, key_cols, key_offset = jax.random.split(key, 4)
    noise = jax.random.normal(key_noise, (SLOTS, SEQ, D), jnp.float32)
    row_scale = jnp.exp(jax.random.uniform(key_rows, (SLOTS, SEQ, 1), jnp.float32, math.log(0.4), math.log(4.0)))
    col_scale = jnp.exp(jax.random.uniform(key_cols, (1, 1, D), jnp.float32, math.log(0.5), math.log(2.0)))
    row_offset = jax.random.uniform(key_offset, (SLOTS, SEQ, 1), jnp.float32, -1.0, 1.0)
    return jnp.clip(row_scale * (noise * col_scale + row_offset), -16.0, 16.0).astype(jnp.bfloat16)


def draw_lengths(key, part):
    key_count, key_len = jax.random.split(jax.random.fold_in(key, 7))
    groups = SLOTS // SLOT_DEV
    fewest = (SLOT_DEV + 1) // 2
    counts = jax.random.randint(key_count, (groups,), fewest, SLOT_DEV + 1)
    counts = counts.at[groups - 1].set(fewest).at[0].set(SLOT_DEV)
    lengths_all = jax.random.randint(key_len, (groups, SLOT_DEV), VALID // 2, VALID + 1)
    lengths_all = lengths_all.at[0, 0].set(VALID)
    slot_pos = jnp.arange(SLOT_DEV, dtype=jnp.int32)
    filled = jnp.where(slot_pos[None, :] < counts[:, None], lengths_all, 0)
    return filled.reshape(SLOTS).astype(jnp.int32)


def set_ends(result, rng, smallest, high):
    index_at = [jax.random.randint(jax.random.fold_in(rng, axis), (), 0, length) for axis, length in enumerate(result.shape)]
    widest = result.shape.index(max(result.shape))
    neighbour = index_at[:widest] + [(index_at[widest] + 1) % result.shape[widest]] + index_at[widest + 1:]
    return result.at[tuple(index_at)].set(smallest).at[tuple(neighbour)].set(high)


def shard_levels(rng, extent, pieces, least, high):
    loudness, own = 1.0, jax.random.fold_in(rng, 6)
    for axis_at, shards_of in pieces:
        draws = jnp.exp(jax.random.uniform(jax.random.fold_in(own, axis_at), (shards_of,), jnp.float32, least / len(pieces), high / len(pieces)))
        loudness = loudness * jnp.repeat(draws, extent[axis_at] // shards_of).reshape([-1 if axis == axis_at else 1 for axis in range(len(extent))])
    return loudness


def scatter_about(key, dims, scale, bound, pieces=(), kind=jnp.bfloat16):
    drawn = scale * jax.random.normal(key, dims, jnp.float32)
    if pieces:
        drawn = drawn * shard_levels(key, dims, pieces, -0.22, 0.18)
    return jnp.clip(drawn, -bound, bound).astype(kind)


def setup_inputs(seed: int = 0) -> dict:
    key_of = jax.random.split(jax.random.key(seed), 21)
    return {
        "tokens": draw_tokens(jax.random.fold_in(key_of[20], 71), 0),
        "cotangent": scatter_about(key_of[1], (SLOTS, SEQ, D), 1.0, 6.0, ((0, 16), (1, 2))),
        "lengths": draw_lengths(jax.random.fold_in(key_of[20], 71), 0),
        "adapter_ids": set_ends(jax.random.randint(key_of[3], (SLOTS,), 0, ADAPTERS), jax.random.fold_in(key_of[3], 1), 0, ADAPTERS - 1).astype(jnp.int32),
        "gain_one": jnp.clip(1.0 + 0.15 * jax.random.normal(key_of[4], (D,), jnp.float32), 0.25, 1.75),
        "gain_two": jnp.clip(1.0 + 0.15 * jax.random.normal(key_of[5], (D,), jnp.float32), 0.25, 1.75),
        "scale_one": jnp.clip(jnp.exp(jax.random.uniform(key_of[6], (D,), jnp.float32, math.log(0.5), math.log(2.0))), 0.5, 2.0),
        "scale_two": jnp.clip(jnp.exp(jax.random.uniform(key_of[7], (D,), jnp.float32, math.log(0.5), math.log(2.0))), 0.5, 2.0),
        "w_qkv": scatter_about(key_of[8], (D, 3, D), D ** -0.5, 0.1875, ((2, 2),)),
        "w_out": scatter_about(key_of[9], (D, D), (D // 32) ** -0.5, 1.0, ((0, 2),)),
        "w_up": scatter_about(key_of[10], (D, FF), D ** -0.5, 0.1875, ((1, 2),)),
        "w_down": scatter_about(key_of[11], (FF, D), FF ** -0.5, 0.09375, ((0, 2),)),
        "qkv_a": scatter_about(key_of[12], (ADAPTERS, RANK, D), D ** -0.5, 0.1875),
        "qkv_b": scatter_about(key_of[13], (ADAPTERS, 3, D, RANK), RANK ** -0.5, 1.5, ((2, 2),)),
        "out_a": scatter_about(key_of[14], (ADAPTERS, RANK, D), (D // 32) ** -0.5, 1.0, ((2, 2),)),
        "out_b": scatter_about(key_of[15], (ADAPTERS, D, RANK), RANK ** -0.5, 1.5),
        "up_a": scatter_about(key_of[16], (ADAPTERS, RANK, D), D ** -0.5, 0.1875),
        "up_b": scatter_about(key_of[17], (ADAPTERS, FF, RANK), RANK ** -0.5, 1.5, ((1, 2),)),
        "down_a": scatter_about(key_of[18], (ADAPTERS, RANK, FF), FF ** -0.5, 0.09375, ((2, 2),)),
        "down_b": scatter_about(key_of[19], (ADAPTERS, D, RANK), RANK ** -0.5, 1.5),
    }


@jax.custom_vjp
def low(v):
    return lax.optimization_barrier(v.astype(jnp.bfloat16)).astype(jnp.float32)

@jax.custom_vjp
def low_back(v):
    return v

def low_keep(v):
    return (low(v), None)

def low_pass(kept, grad):
    return (grad,)

def back_keep(v):
    return (v, None)

def back_low(kept, grad):
    return (low(grad),)
low.defvjp(low_keep, low_pass)
low_back.defvjp(back_keep, back_low)
epsilon = 1e-06
masked_score = -1e+30
HIGHEST = lax.Precision.HIGHEST

def matmul(left, right):
    return jnp.dot(left, right, precision=HIGHEST)

def norm_rows(values, gain_vec):
    average = lax.optimization_barrier(jnp.mean(values, axis=-1, keepdims=True))
    centred = values - average
    variance = lax.optimization_barrier(jnp.mean(centred * centred, axis=-1, keepdims=True))
    return centred * lax.rsqrt(variance + epsilon) * gain_vec

def forward_slot(token_rows, qkv_a, qkv_b, out_a, out_b, up_a, up_b, down_a, down_b, frozen, key_valid, row_valid):
    gain_one, gain_two, scale_one, scale_two, w_qkv, w_out, w_up, w_down = frozen
    seq_len = token_rows.shape[0]
    normed_one = low(norm_rows(token_rows, gain_one))
    rank_qkv = low(matmul(normed_one, qkv_a.T))
    projected = jnp.einsum('td,dcf->ctf', normed_one, w_qkv, precision=HIGHEST)
    projected = projected + jnp.einsum('tr,cfr->ctf', rank_qkv, qkv_b, precision=HIGHEST)
    projected = low(low_back(projected))
    split_heads = projected.reshape(3, seq_len, HEADS, HD)
    scores = jnp.einsum('qhe,khe->hqk', split_heads[0], split_heads[1], precision=HIGHEST) * HD ** (-0.5)
    scores = low_back(scores)
    scores = jnp.where(key_valid[None, None, :], scores, masked_score)
    soft_low = low(jax.nn.softmax(scores, axis=-1))
    mixed = jnp.einsum('hqk,khe->qhe', soft_low, split_heads[2], precision=HIGHEST)
    mixed = low(low_back(mixed.reshape(seq_len, HEADS * HD)))
    rank_out = low_back(matmul(mixed, out_a.T))
    attn_branch = low_back(matmul(mixed, w_out) + matmul(rank_out, out_b.T))
    residual = token_rows + scale_one * attn_branch
    normed_two = low(norm_rows(residual, gain_two))
    rank_up = low(matmul(normed_two, up_a.T))
    preact = low_back(matmul(normed_two, w_up) + matmul(rank_up, up_b.T))
    hidden = low(jax.nn.gelu(preact, approximate=False))
    rank_down = low_back(matmul(hidden, down_a.T))
    mlp_branch = low_back(matmul(hidden, w_down) + matmul(rank_down, down_b.T))
    return (residual + scale_two * mlp_branch) * row_valid[:, None]

def reference(tokens, cotangent, lengths, adapter_ids, gain_one, gain_two, scale_one, scale_two, w_qkv, w_out, w_up, w_down, qkv_a, qkv_b, out_a, out_b, up_a, up_b, down_a, down_b):
    frozen = (gain_one.astype(jnp.float32), gain_two.astype(jnp.float32), scale_one.astype(jnp.float32), scale_two.astype(jnp.float32), w_qkv.astype(jnp.float32), w_out.astype(jnp.float32), w_up.astype(jnp.float32), w_down.astype(jnp.float32))
    tables = tuple((table.astype(jnp.float32) for table in (qkv_a, qkv_b, out_a, out_b, up_a, up_b, down_a, down_b)))
    positions = jnp.arange(SEQ, dtype=jnp.int32)

    def one_slot(totals, slot_items):
        token_rows, grad_rows, length, adapter = slot_items
        key_valid = positions < jnp.maximum(length, 1)
        row_valid = (positions < length).astype(jnp.float32)
        chosen = tuple((table[adapter] for table in tables))

        def slot_forward(rows, *picked):
            return forward_slot(rows, *picked, frozen, key_valid, row_valid)
        output, pullback = jax.vjp(slot_forward, token_rows.astype(jnp.float32), *chosen)
        gradients = pullback(grad_rows.astype(jnp.float32))
        totals = tuple((total.at[adapter].add(grad) for total, grad in zip(totals, gradients[1:])))
        return (totals, (output.astype(jnp.bfloat16), gradients[0]))
    initial = tuple((jnp.zeros_like(table) for table in tables))
    totals, (outputs, grad_tokens) = lax.scan(one_slot, initial, (tokens, cotangent, lengths, adapter_ids))
    return (outputs, grad_tokens, totals[0], totals[1], totals[2], totals[3], totals[4], totals[5], totals[6], totals[7])
```

```python
import functools

import jax
import jax.numpy as jnp
from jax import lax
from jax.experimental import pallas as pl
from jax.experimental.pallas import tpu as pltpu
from jax.sharding import Mesh
from jax.sharding import PartitionSpec as P

HD = 64
ADAPTERS = 8


epsilon = 1e-06
masked_score = -1e30
HIGHEST = lax.Precision.HIGHEST


def product(form, left, right):
    return jnp.einsum(form, left, right, preferred_element_type=jnp.float32)


def precise(form, left, right):
    return jnp.einsum(form, left.astype(jnp.float32), right.astype(jnp.float32), precision=HIGHEST)


def select_rows(onehot, table):
    return product("sn,n...->s...", onehot, table).astype(table.dtype)


def norm_rows(values, gain_vec):
    average = jnp.mean(values, axis=-1, keepdims=True)
    centred = values - average
    variance = jnp.mean(centred * centred, axis=-1, keepdims=True)
    return centred * lax.rsqrt(variance + epsilon) * gain_vec


def norm_back(values, gain_vec, grad_normed):
    normed, pullback = jax.vjp(lambda rows: norm_rows(rows, gain_vec), values)
    return pullback(grad_normed)[0]


def gelu_slope(values):
    return (
        0.5 * (1.0 + lax.erf(values * 0.7071067811865476))
        + values * jnp.exp(-0.5 * values * values) * 0.3989422804014327
    )


def ffn_forward(rows_low, up_mat, down_mat, up_a_sel, up_b_sel, down_a_sel, down_b_sel):
    rank_up = product("std,srd->str", rows_low, up_a_sel).astype(jnp.bfloat16)
    preact = product("std,dh->sth", rows_low, up_mat) + product("str,shr->sth", rank_up, up_b_sel)
    hidden = jax.nn.gelu(preact, approximate=False).astype(jnp.bfloat16)
    rank_down = product("sth,srh->str", hidden, down_a_sel)
    terms = product("sth,hd->std", hidden, down_mat) + precise(
        "str,sdr->std", rank_down, down_b_sel
    )
    return (rank_up, preact, hidden, rank_down, terms)


def ffn_backward(
    rows_low,
    grad_rows,
    up_mat,
    down_mat,
    up_a_sel,
    up_b_sel,
    down_a_sel,
    down_b_sel,
    rank_up,
    preact,
    hidden,
    rank_down,
):
    grad_rank_down = product("std,sdr->str", grad_rows, down_b_sel).astype(jnp.bfloat16)
    grad_hidden = product("std,hd->sth", grad_rows, down_mat) + product(
        "str,srh->sth", grad_rank_down, down_a_sel
    )
    grad_preact = (grad_hidden * gelu_slope(preact)).astype(jnp.bfloat16)
    grad_up_b = product("sth,str->shr", grad_preact, rank_up)
    grad_rank_up = product("sth,shr->str", grad_preact, up_b_sel)
    grad_rows_in = product("sth,dh->std", grad_preact, up_mat) + precise(
        "str,srd->std", grad_rank_up, up_a_sel
    )
    grad_up_a = precise("str,std->srd", grad_rank_up, rows_low)
    grad_down_a = product("str,sth->srh", grad_rank_down, hidden)
    grad_down_b = precise("std,str->sdr", grad_rows, rank_down)
    return (grad_rows_in, (grad_up_a, grad_up_b, grad_down_a, grad_down_b))


def plain_body(
    tokens,
    cotangent,
    lengths,
    adapter_ids,
    gain_one,
    gain_two,
    scale_one,
    scale_two,
    w_qkv,
    w_out,
    w_up,
    w_down,
    qkv_a,
    qkv_b,
    out_a,
    out_b,
    up_a,
    up_b,
    down_a,
    down_b,
):
    shard_rows = tokens.shape[1]
    seq_len = shard_rows * lax.axis_size("tensor")
    heads_local = w_qkv.shape[2] // HD
    scale_attn = HD ** (-0.5)
    first_row = lax.axis_index("tensor") * shard_rows
    positions = jnp.arange(seq_len, dtype=jnp.int32)
    key_valid = positions[None, :] < jnp.maximum(lengths, 1)[:, None]
    local_rows = first_row + jnp.arange(shard_rows, dtype=jnp.int32)
    row_valid = (local_rows[None, :] < lengths[:, None]).astype(jnp.float32)[:, :, None]
    adapters = jnp.arange(ADAPTERS, dtype=jnp.int32)
    onehot = (adapter_ids[:, None] == adapters[None, :]).astype(jnp.bfloat16)
    qkv_a_sel = select_rows(onehot, qkv_a)
    qkv_b_sel = select_rows(onehot, qkv_b)
    out_a_sel = select_rows(onehot, out_a)
    out_b_sel = select_rows(onehot, out_b)
    up_a_sel = select_rows(onehot, up_a)
    down_b_sel = select_rows(onehot, down_b)
    inputs = tokens.astype(jnp.float32)
    normed_one = norm_rows(inputs, gain_one).astype(jnp.bfloat16)
    full_one = lax.all_gather(normed_one, "tensor", axis=1, tiled=True)
    rank_qkv = product("std,srd->str", full_one, qkv_a_sel).astype(jnp.bfloat16)
    projected = (
        product("std,dcf->sctf", full_one, w_qkv) + product("str,scfr->sctf", rank_qkv, qkv_b_sel)
    ).astype(jnp.bfloat16)

    def split_heads(rows):
        return rows.reshape(seq_len, heads_local, HD)

    def masked_scores(queries, keyrows, valid_keys):
        scores = product("qhe,khe->hqk", queries, keyrows) * scale_attn
        return jnp.where(valid_keys[None, None, :], scores, masked_score)

    def attend(slot_items):
        slot_block, valid_keys = slot_items
        queries = split_heads(slot_block[0])
        keyrows = split_heads(slot_block[1])
        values = split_heads(slot_block[2])
        scores = masked_scores(queries, keyrows, valid_keys)
        row_max = jnp.max(scores, axis=-1, keepdims=True)
        exponent = jnp.exp(scores - row_max)
        row_total = jnp.sum(exponent, axis=-1, keepdims=True)
        soft_low = (exponent / row_total).astype(jnp.bfloat16)
        mixed_rows = (
            product("hqk,khe->qhe", soft_low, values).astype(jnp.bfloat16).reshape(seq_len, -1)
        )
        return (mixed_rows, (row_max + jnp.log(row_total))[:, :, 0])

    mixed, log_total = lax.map(attend, (projected, key_valid))
    rank_out = product("stf,srf->str", mixed, out_a_sel)
    attn_terms = product("stf,fd->std", mixed, w_out) + precise("str,sdr->std", rank_out, out_b_sel)
    attn_branch = lax.psum_scatter(attn_terms, "tensor", scatter_dimension=1, tiled=True)
    residual = inputs + scale_one * attn_branch
    normed_two = norm_rows(residual, gain_two).astype(jnp.bfloat16)
    up_mat, down_mat, up_b_all, down_a_all = (
        lax.all_gather(w_up, "tensor", axis=1, tiled=True),
        lax.all_gather(w_down, "tensor", axis=0, tiled=True),
        lax.all_gather(up_b, "tensor", axis=1, tiled=True),
        lax.all_gather(down_a, "tensor", axis=2, tiled=True),
    )
    up_b_sel = select_rows(onehot, up_b_all)
    down_a_sel = select_rows(onehot, down_a_all)
    rank_up, preact, hidden, rank_down, ffn_terms = ffn_forward(
        normed_two, up_mat, down_mat, up_a_sel, up_b_sel, down_a_sel, down_b_sel
    )
    layer_out = ((residual + scale_two * ffn_terms) * row_valid).astype(jnp.bfloat16)
    grad_out = cotangent.astype(jnp.float32) * row_valid
    grad_mlp = (scale_two * grad_out).astype(jnp.bfloat16)
    ffn_grad_in, ffn_grads = ffn_backward(
        normed_two,
        grad_mlp,
        up_mat,
        down_mat,
        up_a_sel,
        up_b_sel,
        down_a_sel,
        down_b_sel,
        rank_up,
        preact,
        hidden,
        rank_down,
    )
    grad_residual = grad_out + norm_back(residual, gain_two, ffn_grad_in)
    grad_attn = (scale_one * grad_residual).astype(jnp.bfloat16)
    full_grad_attn = lax.all_gather(grad_attn, "tensor", axis=1, tiled=True)
    grad_rank_out = product("std,sdr->str", full_grad_attn, out_b_sel).astype(jnp.bfloat16)
    grad_mixed = (
        product("std,fd->stf", full_grad_attn, w_out)
        + product("str,srf->stf", grad_rank_out, out_a_sel)
    ).astype(jnp.bfloat16)
    grad_out_a = product("str,stf->srf", grad_rank_out, mixed)
    grad_out_b = precise("std,str->sdr", full_grad_attn, rank_out)

    def attend_back(slot_items):
        slot_block, valid_keys, log_rows, grad_rows = slot_items
        queries = split_heads(slot_block[0])
        keyrows = split_heads(slot_block[1])
        values = split_heads(slot_block[2])
        scores = masked_scores(queries, keyrows, valid_keys)
        soft = jnp.exp(scores - log_rows[:, :, None])
        soft_low = soft.astype(jnp.bfloat16)
        grad_heads = split_heads(grad_rows)
        grad_soft = product("qhe,khe->hqk", grad_heads, values)
        grad_values = product("hqk,qhe->khe", soft_low, grad_heads)
        grad_scores = (
            soft * (grad_soft - jnp.sum(soft * grad_soft, axis=-1, keepdims=True))
        ).astype(jnp.bfloat16)
        grad_queries = product("hqk,khe->qhe", grad_scores, keyrows) * scale_attn
        grad_keys = product("hqk,qhe->khe", grad_scores, queries) * scale_attn
        return (
            jnp.stack([grad_queries, grad_keys, grad_values])
            .reshape(3, seq_len, -1)
            .astype(jnp.bfloat16)
        )

    grad_projected = lax.map(attend_back, (projected, key_valid, log_total, grad_mixed))
    grad_qkv_b = product("sctf,str->scfr", grad_projected, rank_qkv)
    grad_rank_qkv = product("sctf,scfr->str", grad_projected, qkv_b_sel)
    grad_one_terms = product("sctf,dcf->std", grad_projected, w_qkv) + precise(
        "str,srd->std", grad_rank_qkv, qkv_a_sel
    )
    grad_qkv_a = precise("str,std->srd", grad_rank_qkv, full_one)
    grad_normed_one = lax.psum_scatter(grad_one_terms, "tensor", scatter_dimension=1, tiled=True)
    grad_tokens = grad_residual + norm_back(inputs, gain_one, grad_normed_one)
    onehot_wide = onehot.astype(jnp.float32)

    def stack_slots(slot_grads):
        return jnp.einsum("sn,s...->n...", onehot_wide, slot_grads, precision=HIGHEST)

    grad_up_a, grad_up_b, grad_down_a, grad_down_b = ffn_grads
    sum_qkv_b, sum_out_a = lax.psum((stack_slots(grad_qkv_b), stack_slots(grad_out_a)), "dp")
    joint_sums = lax.psum(
        (
            stack_slots(grad_qkv_a),
            stack_slots(grad_out_b),
            stack_slots(grad_up_a),
            stack_slots(grad_up_b),
            stack_slots(grad_down_a),
            stack_slots(grad_down_b),
        ),
        ("dp", "tensor"),
    )
    sum_qkv_a, sum_out_b, sum_up_a, up_b_whole, down_a_whole, sum_down_b = joint_sums
    width_local = w_up.shape[1]
    first_col = lax.axis_index("tensor") * width_local
    sum_up_b = lax.dynamic_slice_in_dim(up_b_whole, first_col, width_local, 1)
    sum_down_a = lax.dynamic_slice_in_dim(down_a_whole, first_col, width_local, 2)
    return (
        layer_out,
        grad_tokens,
        sum_qkv_a,
        sum_qkv_b,
        sum_out_a,
        sum_out_b,
        sum_up_a,
        sum_up_b,
        sum_down_a,
        sum_down_b,
    )


F32 = jnp.float32
BF = jnp.bfloat16
LOG2E = 1.4426950408889634
PARTS = 8
PAD = 128
FLIP = [(0, 1), (1, 0)]
SWAP = [(0, 0), (1, 2), (2, 1), (3, 3)]


def dotg(a, b, ca, cb):
    return lax.dot_general(a, b, (((ca,), (cb,)), ((), ())), preferred_element_type=F32)


def pad_rows(table):
    rank, width = table.shape
    return jnp.concatenate([table, jnp.zeros((PAD - rank, width), table.dtype)], axis=0)


def pad_twice(table):
    rank, width = table.shape
    return jnp.concatenate([table, table, jnp.zeros((PAD - 2 * rank, width), table.dtype)], axis=0)


def two_terms(wide, rank):
    high = wide.astype(BF).astype(F32)
    return (high + pltpu.roll(wide - high, rank, 1)).astype(BF)


def three_terms(wide):
    high = wide.astype(BF)
    rest = wide - high.astype(F32)
    middle = rest.astype(BF)
    return high, middle, (rest - middle.astype(F32)).astype(BF)


def whole():
    return pl.BlockSpec(memory_space=pltpu.VMEM)


def in_place():
    return pl.BlockSpec(memory_space=pl.ANY)


def scalars():
    return pl.BlockSpec(memory_space=pltpu.SMEM)


def params(mib=58, **more):
    return pltpu.CompilerParams(vmem_limit_bytes=mib * 2**20, **more)


def cost(flops, nbytes):
    return pl.CostEstimate(flops=int(flops), bytes_accessed=int(nbytes), transcendentals=0)


def norm_stats(values):
    average = jnp.mean(values, axis=-1, keepdims=True)
    centred = values - average
    scale = lax.rsqrt(jnp.mean(centred * centred, axis=-1, keepdims=True) + epsilon)
    return centred * scale, scale


def norm_grad(unit, scale, grad):
    return scale * (
        grad
        - jnp.mean(grad, axis=-1, keepdims=True)
        - unit * jnp.mean(grad * unit, axis=-1, keepdims=True)
    )


def row_mask(scal, rows):
    at = lax.broadcasted_iota(jnp.int32, (rows, 1), 0) + scal[1] * rows
    return (at < scal[0]).astype(F32)


def fetch(parts, target, sem, part_at, axis, size):
    copies = []
    for near, part in enumerate(parts):
        first = pl.multiple_of((part_at ^ near) * size, size)
        place = target.at[:, pl.ds(first, size)] if axis == 1 else target.at[pl.ds(first, size)]
        copies.append(pltpu.make_async_copy(part, place, sem.at[near]))
    for copy in copies:
        copy.start()
    return copies


def qkv_local_kernel(tok, gain, w, qa, qb, n1, rank, out, low):
    @pl.when(pl.program_id(0) == 0)
    def _():
        unit, _ = norm_stats(tok[...].astype(F32))
        normed = (unit * gain[...]).astype(BF)
        n1[...] = normed
        ranked = dotg(normed, pad_rows(qa[...]), 1, 1).astype(BF)
        rank[...] = ranked
        low[...] = ranked

    out[0] = (dotg(n1[...], w[0], 1, 0) + dotg(low[...], pad_rows(qb[0]), 1, 0)).astype(BF)


def qkv_local(tok, gain, w, qa, qb):
    rows, width = tok.shape
    third = w.shape[2]
    rank = qa.shape[0]
    fixed = lambda c: (0, 0)
    turn = lambda c: ((c + 1) % 3, 0, 0)
    return pl.pallas_call(
        qkv_local_kernel,
        grid=(3,),
        in_specs=[
            pl.BlockSpec((rows, width), fixed),
            pl.BlockSpec((1, width), fixed),
            pl.BlockSpec((1, width, third), turn),
            pl.BlockSpec((rank, width), fixed),
            pl.BlockSpec((1, rank, third), turn),
        ],
        out_specs=[
            pl.BlockSpec((rows, width), fixed),
            pl.BlockSpec((rows, PAD), fixed),
            pl.BlockSpec((1, rows, third), turn),
        ],
        out_shape=[
            jax.ShapeDtypeStruct((rows, width), BF),
            jax.ShapeDtypeStruct((rows, PAD), BF),
            jax.ShapeDtypeStruct((3, rows, third), BF),
        ],
        scratch_shapes=[pltpu.VMEM((rows, PAD), BF)],
        compiler_params=params(dimension_semantics=("arbitrary",)),
        cost_estimate=cost(2 * rows * width * 3 * third, 8e6),
        name="qkv_local",
    )(tok, gain, w, qa, qb)


def qkv_other_kernel(scal, n1, rank, pack, *rest):
    parts, (out, w), (sem,) = rest[:PARTS], rest[PARTS : PARTS + 2], rest[PARTS + 2 :]
    third = w.shape[2]
    copies = fetch(parts, w, sem, scal[2], 1, parts[0].shape[1])
    for copy in copies:
        copy.wait()
    for c in (1, 2, 0):
        qb = pack[:, c * third : (c + 1) * third]
        out[c] = (dotg(n1[...], w[c], 1, 0) + dotg(rank[...], pad_rows(qb), 1, 0)).astype(BF)


def qkv_other(scal, n1, rank, pack, parts):
    rows, width = n1.shape
    third = parts[0].shape[2]
    return pl.pallas_call(
        qkv_other_kernel,
        in_specs=[scalars(), whole(), whole(), whole()] + [in_place()] * PARTS,
        out_specs=[whole(), whole()],
        out_shape=[
            jax.ShapeDtypeStruct((3, rows, third), BF),
            jax.ShapeDtypeStruct((3, width, third), BF),
        ],
        scratch_shapes=[pltpu.SemaphoreType.DMA((PARTS,))],
        compiler_params=params(),
        cost_estimate=cost(2 * rows * width * 3 * third, 10e6),
        name="qkv_other",
    )(scal, n1, rank, pack, *parts)


def head_lanes(rows, head):
    lanes = lax.broadcasted_iota(jnp.int32, (rows, 2 * HD), 1)
    return lanes, (lanes < HD) if head == 0 else (lanes >= HD), HD if head == 0 else 0


def key_bias(scal, rows, other):
    side = 1 - scal[1] if other else scal[1]
    at = lax.broadcasted_iota(jnp.int32, (rows, 2 * HD), 0) + side * rows
    return jnp.where(at < jnp.maximum(scal[0], 1), 0.0, masked_score).astype(BF)


def scaled_queries(queries):
    wide = queries.astype(F32) * (HD**-0.5 * LOG2E)
    high = wide.astype(BF)
    return high, (wide - high.astype(F32)).astype(BF)


def attend_kernel(scal, q_ref, k_ref, v_ref, ko_ref, vo_ref, out, log_out, qx, kx, vt):
    rows = q_ref.shape[1]
    queries = q_ref[0]
    zero = jnp.zeros_like(queries)
    one = jnp.ones_like(queries)
    high, low = scaled_queries(queries)
    for head in range(2):
        lanes, own, spare = head_lanes(rows, head)
        qx[head, :, 0:128] = jnp.where(own, high, jnp.where(lanes == spare, one, zero))
        qx[head, :, 128:256] = low
        for side, ref in enumerate((k_ref, ko_ref)):
            at = slice(side * rows, (side + 1) * rows)
            bias = key_bias(scal, rows, side == 1)
            kx[head, at, 0:128] = jnp.where(own, ref[0], jnp.where(lanes == spare, bias, zero))
            kx[head, at, 128:256] = jnp.where(own, ref[0], zero)
    for side, ref in enumerate((v_ref, vo_ref)):
        at = slice(side * rows, (side + 1) * rows)
        turned = ref[0].T
        for head in range(2):
            vt[head, 0:HD, at] = turned[head * HD : (head + 1) * HD]
            vt[head, HD : HD + 16, at] = jnp.ones((16, rows), BF)

    def scores(head):
        return dotg(kx[head], qx[head], 1, 1)

    ahead = scores(0)
    mixed = []
    for head in range(2):
        now = ahead
        if head == 0:
            ahead = scores(1)
        top = jnp.max(now, axis=0, keepdims=True)
        soft = jnp.exp2(now - top).astype(BF)
        terms = dotg(vt[head], soft, 1, 0)
        total = terms[HD : HD + 1]
        mixed.append(terms[0:HD] / total)
        log_out[0, head : head + 1, :] = top + jnp.log2(total)
    out[...] = jnp.concatenate(mixed, axis=0).T.astype(BF)


def attend(scal, own, other):
    _, rows, width = own.shape
    pairs = width // (2 * HD)
    take = lambda c: pl.BlockSpec((1, rows, 2 * HD), lambda p: (c, 0, p))
    return pl.pallas_call(
        attend_kernel,
        grid=(pairs,),
        in_specs=[scalars(), take(0), take(1), take(2), take(0), take(1)],
        out_specs=[
            pl.BlockSpec((rows, 2 * HD), lambda p: (0, p)),
            pl.BlockSpec((1, 8, rows), lambda p: (p, 0, 0)),
        ],
        out_shape=[
            jax.ShapeDtypeStruct((rows, width), BF),
            jax.ShapeDtypeStruct((pairs, 8, rows), F32),
        ],
        scratch_shapes=[
            pltpu.VMEM((2, rows, 256), BF),
            pltpu.VMEM((2, 2 * rows, 256), BF),
            pltpu.VMEM((2, HD + 16, 2 * rows), BF),
        ],
        compiler_params=params(dimension_semantics=("arbitrary",)),
        cost_estimate=cost(16e-6 * 1e15, 6e6),
        name="attend",
    )(scal, own, own, own, other, other)


def attend_back_kernel(
    scal, q_ref, k_ref, v_ref, ko_ref, vo_ref, mixed_ref, grad_ref, log_ref, own_out, other_out,
    qx, gx, qm, gm, kx, vx, kt,
):
    rows = q_ref.shape[1]
    queries, grad = q_ref[0], grad_ref[...]
    zero = jnp.zeros_like(queries)
    one = jnp.ones_like(queries)
    high, low = scaled_queries(queries)
    weighed = grad.astype(F32) * mixed_ref[...].astype(F32)
    logs = log_ref[0].T
    for head in range(2):
        lanes, own, spare = head_lanes(rows, head)

        def spread(columns):
            filled = zero
            for step, column in enumerate(columns):
                filled = jnp.where(lanes == spare + step, column, filled)
            return filled

        row_sum = jnp.sum(jnp.where(own, weighed, 0.0), axis=1, keepdims=True)
        log_terms = three_terms(-logs[:, head : head + 1])
        qx[head, :, 0:128] = jnp.where(
            own, high, spread(log_terms + (jnp.ones_like(log_terms[0]),))
        )
        qx[head, :, 128:256] = jnp.where(own, low, zero)
        gx[head] = jnp.where(own, grad, spread(three_terms(-row_sum)))
        qm[head] = jnp.where(own, queries, zero)
        gm[head] = jnp.where(own, grad, zero)
        extra = (lanes >= spare) & (lanes < spare + 3)
        for side, (key_ref, value_ref) in enumerate(((k_ref, v_ref), (ko_ref, vo_ref))):
            at = slice(side * rows, (side + 1) * rows)
            bias = key_bias(scal, rows, side == 1)
            fill = jnp.where(extra, one, jnp.where(lanes == spare + 3, bias, zero))
            kx[head, at, 0:128] = jnp.where(own, key_ref[0], fill)
            kx[head, at, 128:256] = jnp.where(own, key_ref[0], zero)
            vx[head, at, :] = jnp.where(own, value_ref[0], jnp.where(extra, one, zero))
    for side, ref in enumerate((k_ref, ko_ref)):
        kt[:, side * rows : (side + 1) * rows] = ref[0].T
    steps = [(side, head) for side in range(2) for head in range(2)]

    def first(side, head):
        at = slice(side * rows, (side + 1) * rows)
        return dotg(kx[head, at], qx[head], 1, 1), dotg(vx[head, at], gx[head], 1, 1)

    ahead = first(*steps[0])
    grad_queries = [0.0, 0.0]
    kept = None
    for number, (side, head) in enumerate(steps):
        scores, grad_soft = ahead
        if number + 1 < len(steps):
            ahead = first(*steps[number + 1])
        soft = jnp.exp2(scores)
        grad_scores = (soft * grad_soft).astype(BF)
        values = dotg(soft.astype(BF), gm[head], 1, 0)
        keys = dotg(grad_scores, qm[head], 1, 0)
        at = slice(side * rows, (side + 1) * rows)
        grad_queries[head] += dotg(kt[head * HD : (head + 1) * HD, at], grad_scores, 1, 0)
        if head == 0:
            kept = (keys, values)
        else:
            keys = ((kept[0] + keys) * HD**-0.5).astype(BF)
            values = (kept[1] + values).astype(BF)
            if side == 0:
                own_out[1], own_out[2] = keys, values
            else:
                other_out[0], other_out[1] = keys, values
    own_out[0] = (jnp.concatenate(grad_queries, axis=0).T * HD**-0.5).astype(BF)


def attend_back(scal, own, other, mixed, grad, logs):
    _, rows, width = own.shape
    pairs = width // (2 * HD)
    take = lambda c: pl.BlockSpec((1, rows, 2 * HD), lambda p: (c, 0, p))
    flat = pl.BlockSpec((rows, 2 * HD), lambda p: (0, p))
    return pl.pallas_call(
        attend_back_kernel,
        grid=(pairs,),
        in_specs=[scalars(), take(0), take(1), take(2), take(0), take(1), flat, flat]
        + [pl.BlockSpec((1, 8, rows), lambda p: (p, 0, 0))],
        out_specs=[
            pl.BlockSpec((3, rows, 2 * HD), lambda p: (0, 0, p)),
            pl.BlockSpec((2, rows, 2 * HD), lambda p: (0, 0, p)),
        ],
        out_shape=[
            jax.ShapeDtypeStruct((3, rows, width), BF),
            jax.ShapeDtypeStruct((2, rows, width), BF),
        ],
        scratch_shapes=[
            pltpu.VMEM((2, rows, 256), BF),
            pltpu.VMEM((2, rows, 128), BF),
            pltpu.VMEM((2, rows, 128), BF),
            pltpu.VMEM((2, rows, 128), BF),
            pltpu.VMEM((2, 2 * rows, 256), BF),
            pltpu.VMEM((2, 2 * rows, 128), BF),
            pltpu.VMEM((2 * HD, 2 * rows), BF),
        ],
        compiler_params=params(dimension_semantics=("arbitrary",)),
        cost_estimate=cost(27e-6 * 1e15, 9e6),
        name="attend_back",
    )(scal, own, own, own, other, other, mixed, grad, logs)


def branch_kernel(
    scal, mix_a, mix_b, tok, w_a, oa_a, oa_b, ob, scale_one, gain_two, scale_two, ua, db, cot, *rest
):
    parts = rest[:PARTS]
    residual, n2, rank_out, rank_up, grad_mlp, grad_rank, w_b, sem = rest[PARTS:]
    rows = tok.shape[0]
    rank = oa_a.shape[0]
    copies = fetch(parts, w_b, sem, scal[2], 0, parts[0].shape[0])
    grad_low = (scale_two[...] * (cot[...].astype(F32) * row_mask(scal, rows))).astype(BF)
    grad_mlp[...] = grad_low
    grad_rank[...] = dotg(grad_low, pad_rows(db[...]), 1, 1).astype(BF)
    ranked = dotg(mix_a[...], pad_rows(oa_a[...]), 1, 1) + dotg(mix_b[...], pad_rows(oa_b[...]), 1, 1)
    ranked = two_terms(ranked, rank)
    rank_out[...] = ranked
    for copy in copies:
        copy.wait()
    branch = dotg(mix_a[...], w_a[...], 1, 0) + dotg(mix_b[...], w_b[...], 1, 0)
    branch = branch + dotg(ranked, pad_twice(ob[...]), 1, 0)
    total = tok[...].astype(F32) + scale_one[...] * branch
    residual[...] = total
    unit, _ = norm_stats(total)
    normed = (unit * gain_two[...]).astype(BF)
    n2[...] = normed
    rank_up[...] = dotg(normed, pad_rows(ua[...]), 1, 1).astype(BF)


def branch(scal, mix_a, mix_b, tok, w_a, parts, oa_a, oa_b, ob, scale_one, gain_two, scale_two, ua, db, cot):
    rows, width = tok.shape
    low = jax.ShapeDtypeStruct((rows, width), BF)
    ranked = jax.ShapeDtypeStruct((rows, PAD), BF)
    return pl.pallas_call(
        branch_kernel,
        in_specs=[scalars()] + [whole()] * 13 + [in_place()] * PARTS,
        out_specs=[whole()] * 7,
        out_shape=[jax.ShapeDtypeStruct((rows, width), F32), low, ranked, ranked, low, ranked]
        + [jax.ShapeDtypeStruct(w_a.shape, BF)],
        scratch_shapes=[pltpu.SemaphoreType.DMA((PARTS,))],
        compiler_params=params(),
        cost_estimate=cost(2 * rows * width * width, 16e6),
        name="branch",
    )(scal, mix_a, mix_b, tok, w_a, oa_a, oa_b, ob, scale_one, gain_two, scale_two, ua, db, cot, *parts)


def mlp_kernel(count, step, more, *refs):
    scal, n2, rank_up, grad_mlp, grad_rank, ub, da = refs[:7]
    ups, downs = refs[7 : 7 + count], refs[7 + count : 7 + 2 * count]
    rest = refs[7 + 2 * count :]
    earlier = ()
    if more:
        earlier, rest = rest[:4], rest[4:]
    m_out, g_out, rd_out, gru_out, gub_out, gda_out = rest[:6]
    wu, wd, ubs, das, hidden, grad_pre, sem, early_sem = rest[6:]
    width = wu.shape[1]
    rank = ub.shape[0]
    size = width // PARTS
    chunks = width // step
    waits = [[] for _ in range(chunks)]
    for near in range(PARTS):
        at = pl.ds(near * size, size)
        if count == 1:
            sources = ups[0].at[:, at], downs[0].at[at]
        else:
            sources = ups[near], downs[near]
        for which, (source, target) in enumerate(zip(sources, (wu.at[:, at], wd.at[at]))):
            copy = pltpu.make_async_copy(source, target, sem.at[which, near])
            copy.start()
            waits[near * size // step].append(copy)
    if more:
        early = [
            pltpu.make_async_copy(earlier[0], m_out, early_sem.at[0]),
            pltpu.make_async_copy(earlier[1], g_out, early_sem.at[1]),
        ]
        for copy in early:
            copy.start()

    def place(near):
        if count == 1:
            return pl.ds(near * size, size)
        return pl.ds(pl.multiple_of((scal[2] ^ near) * size, size), size)

    ubs[...] = jnp.zeros_like(ubs)
    das[...] = jnp.zeros_like(das)
    for near in range(PARTS):
        at = slice(near * size, (near + 1) * size)
        ubs[0:rank, at] = ub[:, place(near)]
        das[0:rank, at] = da[:, place(near)]
    up_turned = rank_up[...].T[0:rank]
    grad_turned = grad_rank[...].T[0:rank]

    def first(k):
        for copy in waits[k]:
            copy.wait()
        at = slice(k * step, (k + 1) * step)
        return (
            dotg(n2[...], wu[:, at], 1, 0) + dotg(rank_up[...], ubs[:, at], 1, 0),
            dotg(grad_mlp[...], wd[at, :], 1, 1) + dotg(grad_rank[...], das[:, at], 1, 0),
        )

    ahead = first(0)
    for k in range(chunks):
        at = slice(k * step, (k + 1) * step)
        preact, grad_hidden = ahead
        if k + 1 < chunks:
            ahead = first(k + 1)
        cdf = 0.5 * (1.0 + lax.erf(preact * 0.7071067811865476))
        hidden[:, at] = (preact * cdf).astype(BF)
        slope = cdf + preact * jnp.exp(-0.5 * preact * preact) * 0.3989422804014327
        grad_pre[:, at] = (grad_hidden * slope).astype(BF)
    ranked = dotg(hidden[...], das[...], 1, 1)
    grad_ranked = dotg(grad_pre[...], ubs[...], 1, 1)
    if more:
        ranked, grad_ranked = ranked + earlier[2][...], grad_ranked + earlier[3][...]
    rd_out[...] = ranked
    gru_out[...] = grad_ranked
    for near in range(PARTS):
        at = slice(near * size, (near + 1) * size)
        gub_out[:, place(near)] = dotg(up_turned, grad_pre[:, at], 1, 0)
        gda_out[:, place(near)] = dotg(grad_turned, hidden[:, at], 1, 0)
    if more:
        for copy in early:
            copy.wait()
    for at in (slice(k, k + step) for k in range(0, wu.shape[0], step)):
        terms = dotg(hidden[...], wd[:, at], 1, 0)
        grad_terms = dotg(grad_pre[...], wu[at, :], 1, 1)
        if more:
            m_out[:, at] += terms
            g_out[:, at] += grad_terms
        else:
            m_out[:, at] = terms
            g_out[:, at] = grad_terms


def mlp(scal, n2, rank_up, grad_mlp, grad_rank, ub, da, ups, downs, earlier=()):
    rows, width = n2.shape
    half = ub.shape[1]
    rank = ub.shape[0]
    count = len(ups)
    step = half // 4
    sums = jax.ShapeDtypeStruct((rows, width), F32)
    ranked = jax.ShapeDtypeStruct((rows, PAD), F32)
    table = jax.ShapeDtypeStruct((rank, half), F32)
    return pl.pallas_call(
        functools.partial(mlp_kernel, count, step, bool(earlier)),
        in_specs=[scalars()]
        + [whole()] * 6
        + [in_place()] * (2 * count)
        + ([in_place()] * 2 + [whole()] * 2 if earlier else []),
        out_specs=[whole()] * 6,
        out_shape=[sums, sums, ranked, ranked, table, table],
        scratch_shapes=[
            pltpu.VMEM((width, half), BF),
            pltpu.VMEM((half, width), BF),
            pltpu.VMEM((PAD, half), BF),
            pltpu.VMEM((PAD, half), BF),
            pltpu.VMEM((rows, half), BF),
            pltpu.VMEM((rows, half), BF),
            pltpu.SemaphoreType.DMA((2, PARTS)),
            pltpu.SemaphoreType.DMA((2,)),
        ],
        compiler_params=params(),
        cost_estimate=cost(28e-6 * 1e15, 20e6),
        name="mlp",
    )(scal, n2, rank_up, grad_mlp, grad_rank, ub, da, *ups, *downs, *earlier)


def middle_kernel(
    scal, residual, m_in, g_in, rd, gru, db, ua, scale_two, gain_two, scale_one, cot, w_a, w_b,
    oa_a, oa_b, ob, mix_a, mix_b, rank_out, n2, grad_mlp,
    layer, grad_res, grad_a, grad_b, goa_a, goa_b, gob, gua, gdb,
):
    rows = residual.shape[0]
    rank = db.shape[0]
    valid = row_mask(scal, rows)
    down = two_terms(rd[...], rank)
    up = two_terms(gru[...], rank)

    def turned(terms, right):
        both = dotg(terms.T[0 : 2 * rank], right, 1, 0)
        return both[0:rank] + both[rank : 2 * rank]

    branch_out = m_in[...] + dotg(down, pad_twice(db[...]), 1, 0)
    layer[...] = ((residual[...] + scale_two[...] * branch_out) * valid).astype(BF)
    gua[...] = turned(up, n2[...])
    gdb[...] = turned(down, grad_mlp[...])
    unit, scale = norm_stats(residual[...])
    grad_normed = (g_in[...] + dotg(up, pad_twice(ua[...]), 1, 0)) * gain_two[...]
    grad_total = cot[...].astype(F32) * valid + norm_grad(unit, scale, grad_normed)
    grad_res[...] = grad_total
    grad_attn = (scale_one[...] * grad_total).astype(BF)
    grad_rank = dotg(grad_attn, pad_rows(ob[...]), 1, 1).astype(BF)
    grad_a[...] = (
        dotg(grad_attn, w_a[...], 1, 1) + dotg(grad_rank, pad_rows(oa_a[...]), 1, 0)
    ).astype(BF)
    grad_b[...] = (
        dotg(grad_attn, w_b[...], 1, 1) + dotg(grad_rank, pad_rows(oa_b[...]), 1, 0)
    ).astype(BF)
    rank_turned = grad_rank.T[0:rank]
    goa_a[...] = dotg(rank_turned, mix_a[...], 1, 0)
    goa_b[...] = dotg(rank_turned, mix_b[...], 1, 0)
    gob[...] = turned(rank_out[...], grad_attn)


def middle(*args):
    rows, width = args[1].shape
    half = args[12].shape[0]
    rank = args[6].shape[0]
    part = jax.ShapeDtypeStruct((rows, half), BF)
    table = jax.ShapeDtypeStruct((rank, width), F32)
    half_table = jax.ShapeDtypeStruct((rank, half), F32)
    return pl.pallas_call(
        middle_kernel,
        in_specs=[scalars()] + [whole()] * (len(args) - 1),
        out_specs=[whole()] * 9,
        out_shape=[jax.ShapeDtypeStruct((rows, width), BF), jax.ShapeDtypeStruct((rows, width), F32)]
        + [part, part, half_table, half_table, table, table, table],
        compiler_params=params(),
        cost_estimate=cost(8e-6 * 1e15, 20e6),
        name="middle",
    )(*args)


def qkv_tables_kernel(own_a, got_a, own_b, got_b, qb_a, qb_b, n1, rank_in, sum_a, sum_b, rank_out, gqb_a, gqb_b, gqa):
    rank = qb_a.shape[1]
    rank_turned = rank_in[...].T[0:rank]
    ranked = None
    for own, got, qb, total, table in ((own_a, got_a, qb_a, sum_a, gqb_a), (own_b, got_b, qb_b, sum_b, gqb_b)):
        for c in range(3):
            grad = own[c] if c == 0 else (own[c].astype(F32) + got[c - 1].astype(F32)).astype(BF)
            total[c] = grad
            table[c] = dotg(rank_turned, grad, 1, 0)
            terms = dotg(grad, pad_rows(qb[c]), 1, 1)
            ranked = terms if ranked is None else ranked + terms
    ranked = two_terms(ranked, rank)
    rank_out[...] = ranked
    both = dotg(ranked.T[0 : 2 * rank], n1[...], 1, 0)
    gqa[...] = both[0:rank] + both[rank : 2 * rank]


def qkv_tables(own_a, got_a, own_b, got_b, qb_a, qb_b, n1, rank_in):
    rows, width = n1.shape
    _, rank, third = qb_a.shape
    return pl.pallas_call(
        qkv_tables_kernel,
        in_specs=[whole()] * 8,
        out_specs=[whole()] * 6,
        out_shape=[jax.ShapeDtypeStruct((3, rows, third), BF)] * 2
        + [jax.ShapeDtypeStruct((rows, PAD), BF)]
        + [jax.ShapeDtypeStruct((3, rank, third), F32)] * 2
        + [jax.ShapeDtypeStruct((rank, width), F32)],
        compiler_params=params(),
        cost_estimate=cost(5e-6 * 1e15, 14e6),
        name="qkv_tables",
    )(own_a, got_a, own_b, got_b, qb_a, qb_b, n1, rank_in)


def qkv_rows_kernel(grad_a, grad_b, w_a, w_b, ranked, qa, tok, gain, grad_res, out):
    grad = dotg(ranked[...], pad_twice(qa[...]), 1, 0)
    for part, w in ((grad_a, w_a), (grad_b, w_b)):
        for c in range(3):
            grad = grad + dotg(part[c], w[c], 1, 1)
    unit, scale = norm_stats(tok[...].astype(F32))
    out[...] = (grad_res[...] + norm_grad(unit, scale, grad * gain[...])).astype(BF)


def qkv_rows(*args):
    rows, width = args[6].shape
    return pl.pallas_call(
        qkv_rows_kernel,
        in_specs=[whole()] * 9,
        out_specs=whole(),
        out_shape=jax.ShapeDtypeStruct((rows, width), BF),
        compiler_params=params(),
        cost_estimate=cost(7e-6 * 1e15, 16e6),
        name="qkv_rows",
    )(*args)


def swap(rows):
    return lax.ppermute(rows, ("core", "tensor"), SWAP)


def flip(axis):
    return lambda array: lax.ppermute(array, axis, FLIP)


def other_half(local, axis, part_at):
    size = local.shape[axis] // PARTS
    mine = lax.dynamic_slice_in_dim(local, part_at * size, size, axis)
    near = {0: flip("tensor")(mine)}
    near[2] = flip("x")(near[0])
    near[4] = flip("zb")(near[0])
    near[6] = flip("zb")(near[2])
    for k in (0, 2, 4, 6):
        near[k + 1] = flip("core")(near[k])
    return [near[k] for k in range(PARTS)]


def side(array, axis, index, count):
    size = array.shape[axis] // count
    return lax.dynamic_slice_in_dim(array, index * size, size, axis)


class Sum:
    def __init__(self, near, far, shared, core, tensor):
        self.core, self.tensor = core, tensor
        self.rank = near.shape[0]
        self.near, self.far, self.shared = near, far, shared

    def over_cores(self):
        c = self.core
        rank, width = self.shared.shape
        quarters = self.shared.reshape(rank, 4, width // 4)

        def share(index):
            near = side(self.near, 1, index, 2)
            far = side(self.far, 1, index, 2)
            ours = lax.dynamic_index_in_dim(quarters, self.tensor * 2 + index, 1, False)
            theirs = lax.dynamic_index_in_dim(quarters, (1 - self.tensor) * 2 + index, 1, False)
            return jnp.concatenate([near, ours, far, theirs], axis=1)

        got = flip("core")(share(1 - c).astype(BF))
        total = (share(c) + got.astype(F32)).astype(BF)
        self.columns = total.shape[1] // 2
        self.mine = total[:, : self.columns]
        self.send = total[:, self.columns :]
        return self

    def over_pair(self):
        self.pair = jnp.stack([self.mine, flip("tensor")(self.send)])
        return self

    def over_images(self, weights, groups):
        got = [self.pair]
        names, sizes = ("hi", "zb", "x"), groups
        total = sizes[0] * sizes[1] * sizes[2]
        for k in range(1, total):
            got.append(lax.ppermute(self.pair, names, [(i, i ^ k) for i in range(total)]))
        images = jnp.concatenate(got, axis=0)
        self.dense = jnp.einsum("in,irf->nrf", weights, images, preferred_element_type=F32).astype(BF)
        return self

    def spread(self):
        half = self.near.shape[1] // 2
        ours = self.dense[:, :, half:]
        theirs = flip("tensor")(ours)
        first = self.tensor == 0
        pair = jnp.concatenate(
            [self.dense[:, :, :half], jnp.where(first, ours, theirs), jnp.where(first, theirs, ours)], axis=2
        )
        other = flip("core")(pair)
        low = jnp.where(self.core == 0, pair, other).astype(F32)
        high = jnp.where(self.core == 0, other, pair).astype(F32)
        quarter = ours.shape[2]
        near = jnp.concatenate([low[:, :, :half], high[:, :, :half]], axis=2)
        cut = lambda array, index: array[:, :, half + index * quarter : half + (index + 1) * quarter]
        shared = jnp.concatenate([cut(low, 0), cut(high, 0), cut(low, 1), cut(high, 1)], axis=2)
        return near, shared


def quad_body(
    tokens, cotangent, lengths, adapter_ids, gain_one, gain_two, scale_one, scale_two, w_qkv, w_out, w_up, w_down,
    qkv_a, qkv_b, out_a, out_b, up_a, up_b, down_a, down_b,
):
    core, tensor = lax.axis_index("core"), lax.axis_index("tensor")
    groups = tuple(lax.axis_size(name) for name in ("hi", "zb", "x"))
    part_at = lax.axis_index("zb") * 4 + lax.axis_index("x") * 2 + core
    rank, width = qkv_a.shape[1:]
    heads_width = w_qkv.shape[2]
    units = w_up.shape[1]

    tok = swap(tokens[0])
    facts = jnp.stack([lengths[0], adapter_ids[0]])
    facts_other = flip("core")(facts)
    mine = jnp.where(core == tensor, facts, facts_other)
    theirs = jnp.where(core == tensor, facts_other, facts)
    length, adapter, adapter_other = mine[0], mine[1], theirs[1]
    scal = jnp.stack([length, core, part_at, adapter]).astype(jnp.int32)

    qkv_b, out_b, up_b, down_b = (jnp.swapaxes(table, -1, -2) for table in (qkv_b, out_b, up_b, down_b))
    pick = lambda table, index: lax.dynamic_index_in_dim(table, index, 0, False)

    def packed(index):
        qb = jnp.swapaxes(pick(qkv_b, index), 0, 1).reshape(rank, 3 * heads_width)
        return jnp.concatenate([qb, pick(out_a, index), pick(up_b, index), pick(down_a, index)], axis=1)

    pack = flip("tensor")(packed(adapter_other))
    cuts = (3 * heads_width, 4 * heads_width, 4 * heads_width + units)
    qb_other, oa_other, ub_other, da_other = jnp.split(pack, cuts, axis=1)
    qa, oa, ob, ua, ub, da, db = (
        pick(table, adapter) for table in (qkv_a, out_a, out_b, up_a, up_b, down_a, down_b)
    )
    qb = pick(qkv_b, adapter)
    gain_one, gain_two, scale_one, scale_two = (v.reshape(1, width) for v in (gain_one, gain_two, scale_one, scale_two))

    pair_ids = jnp.stack([adapter, adapter_other])
    total = groups[0] * groups[1] * groups[2]
    all_ids = [pair_ids] + [
        lax.ppermute(pair_ids, ("hi", "zb", "x"), [(i, i ^ k) for i in range(total)]) for k in range(1, total)
    ]
    weights = (jnp.concatenate(all_ids)[:, None] == jnp.arange(qkv_a.shape[0])[None, :]).astype(BF)

    w3 = jnp.swapaxes(w_qkv, 0, 1)
    n1, rank_qkv, own_a = qkv_local(tok, gain_one, w3, qa, qb)
    kv_a = flip("core")(own_a[1:])
    w3_parts = other_half(w3, 1, part_at)
    out_parts = other_half(w_out, 0, part_at)
    cot = swap(cotangent[0])
    up_parts = other_half(w_up, 1, part_at)
    down_parts = other_half(w_down, 0, part_at)

    mix_a, logs_a = attend(scal, own_a, kv_a)
    own_b, w3_other = qkv_other(scal, n1, rank_qkv, qb_other, w3_parts)
    kv_b = flip("core")(own_b[1:])
    mix_b, logs_b = attend(scal, own_b, kv_b)
    residual, n2, rank_out, rank_up, grad_mlp, grad_rank, out_other = branch(
        scal, mix_a, mix_b, tok, w_out, out_parts, oa, oa_other, ob, scale_one, gain_two, scale_two, ua, db, cot
    )
    m, g, rd, gru, gub_a, gda_a = mlp(scal, n2, rank_up, grad_mlp, grad_rank, ub, da, [w_up], [w_down])
    m, g, rd, gru, gub_b, gda_b = mlp(
        scal, n2, rank_up, grad_mlp, grad_rank, ub_other, da_other, up_parts, down_parts, (m, g, rd, gru)
    )
    layer, grad_res, grad_a, grad_b, goa_a, goa_b, gob, gua, gdb = middle(
        scal, residual, m, g, rd, gru, db, ua, scale_two, gain_two, scale_one, cot, w_out, out_other,
        oa, oa_other, ob, mix_a, mix_b, rank_out, n2, grad_mlp,
    )
    layer_out = swap(layer)
    early = Sum(
        jnp.concatenate([goa_a, gub_a, gda_a], axis=1),
        jnp.concatenate([goa_b, gub_b, gda_b], axis=1),
        jnp.concatenate([gob, gua, gdb], axis=1),
        core,
        tensor,
    )
    early.over_cores()
    early.over_pair()
    back_a, sent_a = attend_back(scal, own_a, kv_a, mix_a, grad_a, logs_a)
    got_a = flip("core")(sent_a)
    early.over_images(weights, groups)
    back_b, sent_b = attend_back(scal, own_b, kv_b, mix_b, grad_b, logs_b)
    got_b = flip("core")(sent_b)
    qb_other3 = jnp.swapaxes(qb_other.reshape(rank, 3, heads_width), 0, 1)
    sum_a, sum_b, ranked, gqb_a, gqb_b, gqa = qkv_tables(
        back_a, got_a, back_b, got_b, qb, qb_other3, n1, rank_qkv
    )
    flat = lambda table: jnp.swapaxes(table, 0, 1).reshape(rank, 3 * heads_width)
    late = Sum(flat(gqb_a), flat(gqb_b), gqa, core, tensor)
    late.over_cores()
    late.over_pair()
    grad_tokens = qkv_rows(sum_a, sum_b, w3, w3_other, ranked, qa, tok, gain_one, grad_res)
    grad_tokens = swap(grad_tokens).astype(F32)
    late.over_images(weights, groups)
    near, shared = early.spread()
    sum_oa, sum_ub, sum_da = jnp.split(near, (heads_width, heads_width + units), axis=2)
    sum_ob, sum_ua, sum_db = jnp.split(shared, 3, axis=2)
    near, sum_qa = late.spread()
    sum_qb = jnp.swapaxes(near.reshape(-1, rank, 3, heads_width), 1, 2)
    turn = lambda table: jnp.swapaxes(table, -1, -2)
    return (
        layer_out[None],
        grad_tokens[None],
        sum_qa,
        turn(sum_qb),
        sum_oa,
        turn(sum_ob),
        sum_ua,
        turn(sum_ub),
        sum_da,
        turn(sum_db),
    )


def solution(mesh):
    groups, split = mesh.shape["dp"], mesh.shape["tensor"]
    if split == 2 and groups % 8 == 0:
        mesh = Mesh(mesh.devices.reshape(groups // 8, 2, 2, 2, 2), ("hi", "zb", "x", "core", "tensor"))
        dp, body = ("hi", "zb", "x", "core"), quad_body
    else:
        dp, body = "dp", plain_body
    slots = P(dp, "tensor", None)
    in_specs = (
        slots, slots, P(dp), P(dp), P(), P(), P(), P(),
        P(None, None, "tensor"), P("tensor", None), P(None, "tensor"), P("tensor", None),
        P(), P(None, None, "tensor", None), P(None, None, "tensor"), P(),
        P(), P(None, "tensor", None), P(None, None, "tensor"), P(),
    )
    out_specs = (
        slots, slots, P(), P(None, None, "tensor", None), P(None, None, "tensor"), P(),
        P(), P(None, "tensor", None), P(None, None, "tensor"), P(),
    )
    return jax.shard_map(body, mesh=mesh, in_specs=in_specs, out_specs=out_specs, check_vma=False)
```

```python
import functools

import jax
import jax.numpy as jnp
from jax import lax
from jax.experimental import pallas as pl
from jax.experimental.pallas import tpu as pltpu
from jax.sharding import Mesh
from jax.sharding import PartitionSpec as P

HD = 64
ADAPTERS = 8


epsilon = 1e-06
masked_score = -1e30
HIGHEST = lax.Precision.HIGHEST


def product(form, left, right):
    return jnp.einsum(form, left, right, preferred_element_type=jnp.float32)


def precise(form, left, right):
    return jnp.einsum(form, left.astype(jnp.float32), right.astype(jnp.float32), precision=HIGHEST)


def select_rows(onehot, table):
    return product("sn,n...->s...", onehot, table).astype(table.dtype)


def norm_rows(values, gain_vec):
    average = jnp.mean(values, axis=-1, keepdims=True)
    centred = values - average
    variance = jnp.mean(centred * centred, axis=-1, keepdims=True)
    return centred * lax.rsqrt(variance + epsilon) * gain_vec


def norm_back(values, gain_vec, grad_normed):
    normed, pullback = jax.vjp(lambda rows: norm_rows(rows, gain_vec), values)
    return pullback(grad_normed)[0]


def gelu_slope(values):
    return (
        0.5 * (1.0 + lax.erf(values * 0.7071067811865476))
        + values * jnp.exp(-0.5 * values * values) * 0.3989422804014327
    )


def ffn_forward(rows_low, up_mat, down_mat, up_a_sel, up_b_sel, down_a_sel, down_b_sel):
    rank_up = product("std,srd->str", rows_low, up_a_sel).astype(jnp.bfloat16)
    preact = product("std,dh->sth", rows_low, up_mat) + product("str,shr->sth", rank_up, up_b_sel)
    hidden = jax.nn.gelu(preact, approximate=False).astype(jnp.bfloat16)
    rank_down = product("sth,srh->str", hidden, down_a_sel)
    terms = product("sth,hd->std", hidden, down_mat) + precise(
        "str,sdr->std", rank_down, down_b_sel
    )
    return (rank_up, preact, hidden, rank_down, terms)


def ffn_backward(
    rows_low,
    grad_rows,
    up_mat,
    down_mat,
    up_a_sel,
    up_b_sel,
    down_a_sel,
    down_b_sel,
    rank_up,
    preact,
    hidden,
    rank_down,
):
    grad_rank_down = product("std,sdr->str", grad_rows, down_b_sel).astype(jnp.bfloat16)
    grad_hidden = product("std,hd->sth", grad_rows, down_mat) + product(
        "str,srh->sth", grad_rank_down, down_a_sel
    )
    grad_preact = (grad_hidden * gelu_slope(preact)).astype(jnp.bfloat16)
    grad_up_b = product("sth,str->shr", grad_preact, rank_up)
    grad_rank_up = product("sth,shr->str", grad_preact, up_b_sel)
    grad_rows_in = product("sth,dh->std", grad_preact, up_mat) + precise(
        "str,srd->std", grad_rank_up, up_a_sel
    )
    grad_up_a = precise("str,std->srd", grad_rank_up, rows_low)
    grad_down_a = product("str,sth->srh", grad_rank_down, hidden)
    grad_down_b = precise("std,str->sdr", grad_rows, rank_down)
    return (grad_rows_in, (grad_up_a, grad_up_b, grad_down_a, grad_down_b))


def plain_body(
    tokens,
    cotangent,
    lengths,
    adapter_ids,
    gain_one,
    gain_two,
    scale_one,
    scale_two,
    w_qkv,
    w_out,
    w_up,
    w_down,
    qkv_a,
    qkv_b,
    out_a,
    out_b,
    up_a,
    up_b,
    down_a,
    down_b,
):
    shard_rows = tokens.shape[1]
    seq_len = shard_rows * lax.axis_size("tensor")
    heads_local = w_qkv.shape[2] // HD
    scale_attn = HD ** (-0.5)
    first_row = lax.axis_index("tensor") * shard_rows
    positions = jnp.arange(seq_len, dtype=jnp.int32)
    key_valid = positions[None, :] < jnp.maximum(lengths, 1)[:, None]
    local_rows = first_row + jnp.arange(shard_rows, dtype=jnp.int32)
    row_valid = (local_rows[None, :] < lengths[:, None]).astype(jnp.float32)[:, :, None]
    adapters = jnp.arange(ADAPTERS, dtype=jnp.int32)
    onehot = (adapter_ids[:, None] == adapters[None, :]).astype(jnp.bfloat16)
    qkv_a_sel = select_rows(onehot, qkv_a)
    qkv_b_sel = select_rows(onehot, qkv_b)
    out_a_sel = select_rows(onehot, out_a)
    out_b_sel = select_rows(onehot, out_b)
    up_a_sel = select_rows(onehot, up_a)
    down_b_sel = select_rows(onehot, down_b)
    inputs = tokens.astype(jnp.float32)
    normed_one = norm_rows(inputs, gain_one).astype(jnp.bfloat16)
    full_one = lax.all_gather(normed_one, "tensor", axis=1, tiled=True)
    rank_qkv = product("std,srd->str", full_one, qkv_a_sel).astype(jnp.bfloat16)
    projected = (
        product("std,dcf->sctf", full_one, w_qkv) + product("str,scfr->sctf", rank_qkv, qkv_b_sel)
    ).astype(jnp.bfloat16)

    def split_heads(rows):
        return rows.reshape(seq_len, heads_local, HD)

    def masked_scores(queries, keyrows, valid_keys):
        scores = product("qhe,khe->hqk", queries, keyrows) * scale_attn
        return jnp.where(valid_keys[None, None, :], scores, masked_score)

    def attend(slot_items):
        slot_block, valid_keys = slot_items
        queries = split_heads(slot_block[0])
        keyrows = split_heads(slot_block[1])
        values = split_heads(slot_block[2])
        scores = masked_scores(queries, keyrows, valid_keys)
        row_max = jnp.max(scores, axis=-1, keepdims=True)
        exponent = jnp.exp(scores - row_max)
        row_total = jnp.sum(exponent, axis=-1, keepdims=True)
        soft_low = (exponent / row_total).astype(jnp.bfloat16)
        mixed_rows = (
            product("hqk,khe->qhe", soft_low, values).astype(jnp.bfloat16).reshape(seq_len, -1)
        )
        return (mixed_rows, (row_max + jnp.log(row_total))[:, :, 0])

    mixed, log_total = lax.map(attend, (projected, key_valid))
    rank_out = product("stf,srf->str", mixed, out_a_sel)
    attn_terms = product("stf,fd->std", mixed, w_out) + precise("str,sdr->std", rank_out, out_b_sel)
    attn_branch = lax.psum_scatter(attn_terms, "tensor", scatter_dimension=1, tiled=True)
    residual = inputs + scale_one * attn_branch
    normed_two = norm_rows(residual, gain_two).astype(jnp.bfloat16)
    up_mat, down_mat, up_b_all, down_a_all = (
        lax.all_gather(w_up, "tensor", axis=1, tiled=True),
        lax.all_gather(w_down, "tensor", axis=0, tiled=True),
        lax.all_gather(up_b, "tensor", axis=1, tiled=True),
        lax.all_gather(down_a, "tensor", axis=2, tiled=True),
    )
    up_b_sel = select_rows(onehot, up_b_all)
    down_a_sel = select_rows(onehot, down_a_all)
    rank_up, preact, hidden, rank_down, ffn_terms = ffn_forward(
        normed_two, up_mat, down_mat, up_a_sel, up_b_sel, down_a_sel, down_b_sel
    )
    layer_out = ((residual + scale_two * ffn_terms) * row_valid).astype(jnp.bfloat16)
    grad_out = cotangent.astype(jnp.float32) * row_valid
    grad_mlp = (scale_two * grad_out).astype(jnp.bfloat16)
    ffn_grad_in, ffn_grads = ffn_backward(
        normed_two,
        grad_mlp,
        up_mat,
        down_mat,
        up_a_sel,
        up_b_sel,
        down_a_sel,
        down_b_sel,
        rank_up,
        preact,
        hidden,
        rank_down,
    )
    grad_residual = grad_out + norm_back(residual, gain_two, ffn_grad_in)
    grad_attn = (scale_one * grad_residual).astype(jnp.bfloat16)
    full_grad_attn = lax.all_gather(grad_attn, "tensor", axis=1, tiled=True)
    grad_rank_out = product("std,sdr->str", full_grad_attn, out_b_sel).astype(jnp.bfloat16)
    grad_mixed = (
        product("std,fd->stf", full_grad_attn, w_out)
        + product("str,srf->stf", grad_rank_out, out_a_sel)
    ).astype(jnp.bfloat16)
    grad_out_a = product("str,stf->srf", grad_rank_out, mixed)
    grad_out_b = precise("std,str->sdr", full_grad_attn, rank_out)

    def attend_back(slot_items):
        slot_block, valid_keys, log_rows, grad_rows = slot_items
        queries = split_heads(slot_block[0])
        keyrows = split_heads(slot_block[1])
        values = split_heads(slot_block[2])
        scores = masked_scores(queries, keyrows, valid_keys)
        soft = jnp.exp(scores - log_rows[:, :, None])
        soft_low = soft.astype(jnp.bfloat16)
        grad_heads = split_heads(grad_rows)
        grad_soft = product("qhe,khe->hqk", grad_heads, values)
        grad_values = product("hqk,qhe->khe", soft_low, grad_heads)
        grad_scores = (
            soft * (grad_soft - jnp.sum(soft * grad_soft, axis=-1, keepdims=True))
        ).astype(jnp.bfloat16)
        grad_queries = product("hqk,khe->qhe", grad_scores, keyrows) * scale_attn
        grad_keys = product("hqk,qhe->khe", grad_scores, queries) * scale_attn
        return (
            jnp.stack([grad_queries, grad_keys, grad_values])
            .reshape(3, seq_len, -1)
            .astype(jnp.bfloat16)
        )

    grad_projected = lax.map(attend_back, (projected, key_valid, log_total, grad_mixed))
    grad_qkv_b = product("sctf,str->scfr", grad_projected, rank_qkv)
    grad_rank_qkv = product("sctf,scfr->str", grad_projected, qkv_b_sel)
    grad_one_terms = product("sctf,dcf->std", grad_projected, w_qkv) + precise(
        "str,srd->std", grad_rank_qkv, qkv_a_sel
    )
    grad_qkv_a = precise("str,std->srd", grad_rank_qkv, full_one)
    grad_normed_one = lax.psum_scatter(grad_one_terms, "tensor", scatter_dimension=1, tiled=True)
    grad_tokens = grad_residual + norm_back(inputs, gain_one, grad_normed_one)
    onehot_wide = onehot.astype(jnp.float32)

    def stack_slots(slot_grads):
        return jnp.einsum("sn,s...->n...", onehot_wide, slot_grads, precision=HIGHEST)

    grad_up_a, grad_up_b, grad_down_a, grad_down_b = ffn_grads
    sum_qkv_b, sum_out_a = lax.psum((stack_slots(grad_qkv_b), stack_slots(grad_out_a)), "dp")
    joint_sums = lax.psum(
        (
            stack_slots(grad_qkv_a),
            stack_slots(grad_out_b),
            stack_slots(grad_up_a),
            stack_slots(grad_up_b),
            stack_slots(grad_down_a),
            stack_slots(grad_down_b),
        ),
        ("dp", "tensor"),
    )
    sum_qkv_a, sum_out_b, sum_up_a, up_b_whole, down_a_whole, sum_down_b = joint_sums
    width_local = w_up.shape[1]
    first_col = lax.axis_index("tensor") * width_local
    sum_up_b = lax.dynamic_slice_in_dim(up_b_whole, first_col, width_local, 1)
    sum_down_a = lax.dynamic_slice_in_dim(down_a_whole, first_col, width_local, 2)
    return (
        layer_out,
        grad_tokens,
        sum_qkv_a,
        sum_qkv_b,
        sum_out_a,
        sum_out_b,
        sum_up_a,
        sum_up_b,
        sum_down_a,
        sum_down_b,
    )


F32 = jnp.float32
BF = jnp.bfloat16
LOG2E = 1.4426950408889634
PARTS = 8
PAD = 128
FLIP = [(0, 1), (1, 0)]
SWAP = [(1, 2), (2, 1)]


def dotg(a, b, ca, cb):
    return lax.dot_general(a, b, (((ca,), (cb,)), ((), ())), preferred_element_type=F32)


def pad_rows(table):
    rank, width = table.shape
    return jnp.concatenate([table, jnp.zeros((PAD - rank, width), table.dtype)], axis=0)


def pad_twice(table):
    rank, width = table.shape
    return jnp.concatenate([table, table, jnp.zeros((PAD - 2 * rank, width), table.dtype)], axis=0)


def two_terms(wide, rank):
    high = wide.astype(BF).astype(F32)
    return (high + pltpu.roll(wide - high, rank, 1)).astype(BF)


def three_terms(wide):
    high = wide.astype(BF)
    rest = wide - high.astype(F32)
    middle = rest.astype(BF)
    return high, middle, (rest - middle.astype(F32)).astype(BF)


def whole():
    return pl.BlockSpec(memory_space=pltpu.VMEM)


def in_place():
    return pl.BlockSpec(memory_space=pl.ANY)


def scalars():
    return pl.BlockSpec(memory_space=pltpu.SMEM)


def params(mib=58, **more):
    return pltpu.CompilerParams(vmem_limit_bytes=mib * 2**20, **more)


def cost(flops, nbytes):
    return pl.CostEstimate(flops=int(flops * 0.5), bytes_accessed=int(nbytes), transcendentals=0)


def norm_stats(values):
    average = jnp.mean(values, axis=-1, keepdims=True)
    centred = values - average
    scale = lax.rsqrt(jnp.mean(centred * centred, axis=-1, keepdims=True) + epsilon)
    return centred * scale, scale


def norm_grad(unit, scale, grad):
    return scale * (
        grad
        - jnp.mean(grad, axis=-1, keepdims=True)
        - unit * jnp.mean(grad * unit, axis=-1, keepdims=True)
    )


def row_mask(scal, rows):
    at = lax.broadcasted_iota(jnp.int32, (rows, 1), 0) + scal[1] * rows
    return (at < scal[0]).astype(F32)


def choose(scal, here, swapped, target, sem):
    @pl.when(scal[3] != 0)
    def _():
        pltpu.make_async_copy(here, target, sem).start()

    @pl.when(scal[3] == 0)
    def _():
        pltpu.make_async_copy(swapped, target, sem).start()

    return pltpu.make_async_copy(here, target, sem)


def fetch(arrays, nears, target, sem, part_at, axis, size):
    copies = []
    parts = len(nears)
    for number, near in enumerate(nears):
        first = pl.multiple_of(((part_at % parts) ^ near) * size, size)
        place = target.at[:, pl.ds(first, size)] if axis == 1 else target.at[pl.ds(first, size)]
        copies.append(pltpu.make_async_copy(arrays[number // 2].at[number % 2], place, sem.at[near]))
    for copy in copies:
        copy.start()
    return copies


def qkv_local_kernel(scal, here, swapped, gain, w, qa, qb, tok, n1, rank, queries, rest, low, sem):
    step = pl.program_id(0)

    @pl.when(step == 0)
    def _():
        choose(scal, here, swapped, tok, sem.at[0]).wait()
        unit, _ = norm_stats(tok[...].astype(F32))
        normed = (unit * gain[...]).astype(BF)
        n1[...] = normed
        ranked = dotg(normed, pad_rows(qa[...]), 1, 1).astype(BF)
        rank[...] = ranked
        low[...] = ranked

    out = (dotg(n1[...], w[0], 1, 0) + dotg(low[...], pad_rows(qb[...]), 1, 0)).astype(BF)

    @pl.when(step < 2)
    def _():
        rest[0] = out

    @pl.when(step == 2)
    def _():
        queries[...] = out


def qkv_local(scal, tok, swapped, gain, w, qa, qb):
    rows, width = tok.shape
    third = w.shape[2]
    rank = qa.shape[0]
    fixed = lambda c: (0, 0)
    return pl.pallas_call(
        qkv_local_kernel,
        grid=(3,),
        in_specs=[
            scalars(),
            in_place(),
            in_place(),
            pl.BlockSpec((1, width), fixed),
            pl.BlockSpec((1, width, third), lambda c: ((c + 1) % 3, 0, 0)),
            pl.BlockSpec((rank, width), fixed),
            pl.BlockSpec((rank, third), lambda c: (0, (c + 1) % 3)),
        ],
        out_specs=[
            pl.BlockSpec((rows, width), fixed),
            pl.BlockSpec((rows, width), fixed),
            pl.BlockSpec((rows, PAD), fixed),
            pl.BlockSpec((rows, third), fixed),
            pl.BlockSpec((1, rows, third), lambda c: (jnp.minimum(c, 1), 0, 0)),
        ],
        out_shape=[
            jax.ShapeDtypeStruct((rows, width), BF),
            jax.ShapeDtypeStruct((rows, width), BF),
            jax.ShapeDtypeStruct((rows, PAD), BF),
            jax.ShapeDtypeStruct((rows, third), BF),
            jax.ShapeDtypeStruct((2, rows, third), BF),
        ],
        scratch_shapes=[pltpu.VMEM((rows, PAD), BF), pltpu.SemaphoreType.DMA((1,))],
        compiler_params=params(dimension_semantics=("arbitrary",)),
        cost_estimate=cost(7e-6 * 1e15, 8e6),
        name="qkv_local",
    )(scal, tok, swapped, gain, w, qa, qb)


def qkv_other_kernel(nears, scal, n1, rank, qb, *rest):
    arrays, (queries, out, w, sem) = rest[: len(nears) // 2], rest[len(nears) // 2 :]
    third = w.shape[2]
    copies = fetch(arrays, nears, w, sem, scal[2], 1, arrays[0].shape[2])
    for copy in copies:
        copy.wait()
    for c in (1, 2, 0):
        at = slice(c * third, (c + 1) * third)
        terms = (dotg(n1[...], w[c], 1, 0) + dotg(rank[...], pad_rows(qb[:, at]), 1, 0)).astype(BF)
        if c == 0:
            queries[...] = terms
        else:
            out[c - 1] = terms


def qkv_other(scal, n1, rank, qb, half):
    rows, width = n1.shape
    arrays, nears = half.pairs, half.names
    third = arrays[0].shape[3]
    return pl.pallas_call(
        functools.partial(qkv_other_kernel, nears),
        in_specs=[scalars(), whole(), whole(), whole()] + [in_place()] * len(arrays),
        out_specs=[whole()] * 3,
        out_shape=[
            jax.ShapeDtypeStruct((rows, third), BF),
            jax.ShapeDtypeStruct((2, rows, third), BF),
            jax.ShapeDtypeStruct((3, width, third), BF),
        ],
        scratch_shapes=[pltpu.SemaphoreType.DMA((PARTS,))],
        compiler_params=params(),
        cost_estimate=cost(7e-6 * 1e15, 10e6),
        name="qkv_other",
    )(scal, n1, rank, qb, *arrays)


def head_lanes(rows, head):
    lanes = lax.broadcasted_iota(jnp.int32, (rows, 2 * HD), 1)
    return lanes, (lanes < HD) if head == 0 else (lanes >= HD), HD if head == 0 else 0


def key_bias(scal, rows, other):
    side = 1 - scal[1] if other else scal[1]
    at = lax.broadcasted_iota(jnp.int32, (rows, 2 * HD), 0) + side * rows
    return jnp.where(at < jnp.maximum(scal[0], 1), 0.0, masked_score).astype(BF)


def scaled_queries(queries):
    wide = queries.astype(F32) * (HD**-0.5 * LOG2E)
    high = wide.astype(BF)
    return high, (wide - high.astype(F32)).astype(BF)


def attend_kernel(scal, q_ref, k_ref, v_ref, ko_ref, vo_ref, out, log_out, qx, kx, vt):
    rows = q_ref.shape[0]
    queries = q_ref[...]
    zero = jnp.zeros_like(queries)
    one = jnp.ones_like(queries)
    high, low = scaled_queries(queries)
    for head in range(2):
        lanes, own, spare = head_lanes(rows, head)
        qx[head, :, 0:128] = jnp.where(own, high, jnp.where(lanes == spare, one, zero))
        qx[head, :, 128:256] = low
        for side, ref in enumerate((k_ref, ko_ref)):
            at = slice(side * rows, (side + 1) * rows)
            bias = key_bias(scal, rows, side == 1)
            kx[head, at, 0:128] = jnp.where(own, ref[0], jnp.where(lanes == spare, bias, zero))
            kx[head, at, 128:256] = jnp.where(own, ref[0], zero)
    for side, ref in enumerate((v_ref, vo_ref)):
        at = slice(side * rows, (side + 1) * rows)
        turned = ref[0].T
        for head in range(2):
            vt[head, 0:HD, at] = turned[head * HD : (head + 1) * HD]
            vt[head, HD : HD + 16, at] = jnp.ones((16, rows), BF)

    def scores(head):
        return dotg(kx[head], qx[head], 1, 1)

    ahead = scores(0)
    mixed = []
    for head in range(2):
        now = ahead
        if head == 0:
            ahead = scores(1)
        top = jnp.max(now, axis=0, keepdims=True)
        soft = jnp.exp2(now - top).astype(BF)
        terms = dotg(vt[head], soft, 1, 0)
        total = terms[HD : HD + 1]
        mixed.append(terms[0:HD] / total)
        log_out[0, head : head + 1, :] = top + jnp.log2(total)
    out[...] = jnp.concatenate(mixed, axis=0).T.astype(BF)


def attend(scal, queries, own, other):
    _, rows, width = own.shape
    pairs = width // (2 * HD)
    take = lambda c: pl.BlockSpec((1, rows, 2 * HD), lambda p: (c, 0, p))
    return pl.pallas_call(
        attend_kernel,
        grid=(pairs,),
        in_specs=[scalars(), pl.BlockSpec((rows, 2 * HD), lambda p: (0, p)), take(0), take(1), take(0), take(1)],
        out_specs=[
            pl.BlockSpec((rows, 2 * HD), lambda p: (0, p)),
            pl.BlockSpec((1, 8, rows), lambda p: (p, 0, 0)),
        ],
        out_shape=[
            jax.ShapeDtypeStruct((rows, width), BF),
            jax.ShapeDtypeStruct((pairs, 8, rows), F32),
        ],
        scratch_shapes=[
            pltpu.VMEM((2, rows, 256), BF),
            pltpu.VMEM((2, 2 * rows, 256), BF),
            pltpu.VMEM((2, HD + 16, 2 * rows), BF),
        ],
        compiler_params=params(dimension_semantics=("arbitrary",)),
        cost_estimate=cost(16e-6 * 1e15, 6e6),
        name="attend",
    )(scal, queries, own, own, other, other)


def attend_back_kernel(
    scal, q_ref, k_ref, v_ref, ko_ref, vo_ref, mixed_ref, grad_ref, log_ref, queries_out, own_out, other_out,
    qx, gx, qm, gm, kx, vx, kt,
):
    rows = q_ref.shape[0]
    queries, grad = q_ref[...], grad_ref[...]
    zero = jnp.zeros_like(queries)
    one = jnp.ones_like(queries)
    high, low = scaled_queries(queries)
    weighed = grad.astype(F32) * mixed_ref[...].astype(F32)
    logs = log_ref[0].T
    for head in range(2):
        lanes, own, spare = head_lanes(rows, head)

        def spread(columns):
            filled = zero
            for step, column in enumerate(columns):
                filled = jnp.where(lanes == spare + step, column, filled)
            return filled

        row_sum = jnp.sum(jnp.where(own, weighed, 0.0), axis=1, keepdims=True)
        log_terms = three_terms(-logs[:, head : head + 1])
        qx[head, :, 0:128] = jnp.where(
            own, high, spread(log_terms + (jnp.ones_like(log_terms[0]),))
        )
        qx[head, :, 128:256] = jnp.where(own, low, zero)
        gx[head] = jnp.where(own, grad, spread(three_terms(-row_sum)))
        qm[head] = jnp.where(own, queries, zero)
        gm[head] = jnp.where(own, grad, zero)
        extra = (lanes >= spare) & (lanes < spare + 3)
        for side, (key_ref, value_ref) in enumerate(((k_ref, v_ref), (ko_ref, vo_ref))):
            at = slice(side * rows, (side + 1) * rows)
            bias = key_bias(scal, rows, side == 1)
            fill = jnp.where(extra, one, jnp.where(lanes == spare + 3, bias, zero))
            kx[head, at, 0:128] = jnp.where(own, key_ref[0], fill)
            kx[head, at, 128:256] = jnp.where(own, key_ref[0], zero)
            vx[head, at, :] = jnp.where(own, value_ref[0], jnp.where(extra, one, zero))
    for side, ref in enumerate((k_ref, ko_ref)):
        kt[:, side * rows : (side + 1) * rows] = ref[0].T
    steps = [(side, head) for side in range(2) for head in range(2)]

    def first(side, head):
        at = slice(side * rows, (side + 1) * rows)
        return dotg(kx[head, at], qx[head], 1, 1), dotg(vx[head, at], gx[head], 1, 1)

    ahead = first(*steps[0])
    grad_queries = [0.0, 0.0]
    kept = None
    for number, (side, head) in enumerate(steps):
        scores, grad_soft = ahead
        if number + 1 < len(steps):
            ahead = first(*steps[number + 1])
        soft = jnp.exp2(scores)
        grad_scores = (soft * grad_soft).astype(BF)
        values = dotg(soft.astype(BF), gm[head], 1, 0)
        keys = dotg(grad_scores, qm[head], 1, 0)
        at = slice(side * rows, (side + 1) * rows)
        grad_queries[head] += dotg(kt[head * HD : (head + 1) * HD, at], grad_scores, 1, 0)
        if head == 0:
            kept = (keys, values)
        else:
            keys = ((kept[0] + keys) * HD**-0.5).astype(BF)
            values = (kept[1] + values).astype(BF)
            out = own_out if side == 0 else other_out
            out[0], out[1] = keys, values
    queries_out[...] = (jnp.concatenate(grad_queries, axis=0).T * HD**-0.5).astype(BF)


def attend_back(scal, queries, own, other, mixed, grad, logs, piece, pieces):
    _, rows, width = own.shape
    width = width // pieces
    pairs = width // (2 * HD)
    skip = piece * pairs
    take = lambda c: pl.BlockSpec((1, rows, 2 * HD), lambda p: (c, 0, p + skip))
    flat = pl.BlockSpec((rows, 2 * HD), lambda p: (0, p + skip))
    return pl.pallas_call(
        attend_back_kernel,
        grid=(pairs,),
        in_specs=[scalars(), flat, take(0), take(1), take(0), take(1), flat, flat]
        + [pl.BlockSpec((1, 8, rows), lambda p: (p + skip, 0, 0))],
        out_specs=[
            pl.BlockSpec((rows, 2 * HD), lambda p: (0, p)),
            pl.BlockSpec((2, rows, 2 * HD), lambda p: (0, 0, p)),
            pl.BlockSpec((2, rows, 2 * HD), lambda p: (0, 0, p)),
        ],
        out_shape=[
            jax.ShapeDtypeStruct((rows, width), BF),
            jax.ShapeDtypeStruct((2, rows, width), BF),
            jax.ShapeDtypeStruct((2, rows, width), BF),
        ],
        scratch_shapes=[
            pltpu.VMEM((2, rows, 256), BF),
            pltpu.VMEM((2, rows, 128), BF),
            pltpu.VMEM((2, rows, 128), BF),
            pltpu.VMEM((2, rows, 128), BF),
            pltpu.VMEM((2, 2 * rows, 256), BF),
            pltpu.VMEM((2, 2 * rows, 128), BF),
            pltpu.VMEM((2 * HD, 2 * rows), BF),
        ],
        compiler_params=params(dimension_semantics=("arbitrary",)),
        cost_estimate=cost(26e-6 / pieces * 1e15, 9e6),
        name="attend_back",
    )(scal, queries, own, own, other, other, mixed, grad, logs)


def branch_kernel(nears, scal, mix_a, mix_b, tok, w_a, oa_a, oa_b, ob, scale_one, gain_two, ua, *rest):
    arrays = rest[: len(nears) // 2]
    residual, n2, rank_out, rank_up, w_b, sem = rest[len(nears) // 2 :]
    rank = oa_a.shape[0]

    @pl.when(pl.program_id(0) == 0)
    def _():
        for copy in fetch(arrays, nears, w_b, sem, scal[2], 0, arrays[0].shape[1]):
            copy.wait()

    ranked = dotg(mix_a[...], pad_rows(oa_a[...]), 1, 1) + dotg(mix_b[...], pad_rows(oa_b[...]), 1, 1)
    ranked = two_terms(ranked, rank)
    rank_out[...] = ranked
    terms = dotg(mix_a[...], w_a[...], 1, 0) + dotg(mix_b[...], w_b[...], 1, 0)
    terms = terms + dotg(ranked, pad_twice(ob[...]), 1, 0)
    total = tok[...].astype(F32) + scale_one[...] * terms
    residual[...] = total
    unit, _ = norm_stats(total)
    normed = (unit * gain_two[...]).astype(BF)
    n2[...] = normed
    rank_up[...] = dotg(normed, pad_rows(ua[...]), 1, 1).astype(BF)


def blocked(rows, width):
    return pl.BlockSpec((rows, width), lambda step: (step, 0))


def fixed_block(*shape):
    return pl.BlockSpec(shape, lambda step: (0,) * len(shape))


def branch(scal, mix_a, mix_b, tok, w_a, half, oa_a, oa_b, ob, scale_one, gain_two, ua):
    rows, width = tok.shape
    heads = mix_a.shape[1]
    block = rows // 2
    arrays, nears = half.pairs, half.names
    return pl.pallas_call(
        functools.partial(branch_kernel, nears),
        grid=(2,),
        in_specs=[scalars(), blocked(block, heads), blocked(block, heads), blocked(block, width)]
        + [fixed_block(*array.shape) for array in (w_a, oa_a, oa_b, ob, scale_one, gain_two, ua)]
        + [in_place()] * len(arrays),
        out_specs=[blocked(block, width), blocked(block, width), blocked(block, PAD), blocked(block, PAD)]
        + [fixed_block(*w_a.shape)],
        out_shape=[
            jax.ShapeDtypeStruct((rows, width), F32),
            jax.ShapeDtypeStruct((rows, width), BF),
            jax.ShapeDtypeStruct((rows, PAD), BF),
            jax.ShapeDtypeStruct((rows, PAD), BF),
            jax.ShapeDtypeStruct(w_a.shape, BF),
        ],
        scratch_shapes=[pltpu.SemaphoreType.DMA((PARTS,))],
        compiler_params=params(dimension_semantics=("arbitrary",)),
        cost_estimate=cost(8e-6 * 1e15, 16e6),
        name="branch",
    )(scal, mix_a, mix_b, tok, w_a, oa_a, oa_b, ob, scale_one, gain_two, ua, *arrays)


def mlp_kernel(nears, step, more, *refs):
    scal, n2, rank_up, ub, da = refs[:5]
    count = 1 if nears is None else len(nears)
    ups, downs = refs[5 : 5 + count], refs[5 + count : 5 + 2 * count]
    rest = refs[5 + 2 * count :]
    if nears is None:
        here, swapped, scale_two, db, cot, grad_mlp, grad_rank = rest[:7]
        earlier, rest = (), rest[7:]
        chosen = choose(scal, here, swapped, cot, rest[-1].at[0])
    else:
        grad_mlp, grad_rank = rest[:2]
        earlier, rest = rest[2 : 2 + more], rest[2 + more :]
    m_out, g_out, rd_out, gru_out, gub_out, gda_out = rest[:6]
    wu, wd, ubs, das, hidden, grad_pre, sem, early_sem = rest[6:]
    width = wu.shape[1]
    rank = ub.shape[0]
    size = ub.shape[1] // PARTS
    pieces = width // size
    chunks = width // step
    waits = [[] for _ in range(chunks)]
    for piece in range(pieces):
        at = pl.ds(piece * size, size)
        if nears is None:
            sources = ups[0].at[:, at], downs[0].at[at]
        else:
            sources = ups[piece], downs[piece]
        for which, (source, target) in enumerate(zip(sources, (wu.at[:, at], wd.at[at]))):
            copy = pltpu.make_async_copy(source, target, sem.at[which, piece])
            copy.start()
            waits[piece * size // step].append(copy)
    if more:
        early = [
            pltpu.make_async_copy(earlier[0], m_out, early_sem.at[0]),
            pltpu.make_async_copy(earlier[1], g_out, early_sem.at[1]),
        ]
        for copy in early:
            copy.start()

    def place(piece):
        if nears is None:
            return pl.ds(piece * size, size)
        return pl.ds(pl.multiple_of((scal[2] ^ nears[piece]) * size, size), size)

    if nears is None:
        chosen.wait()
        grad_low = (scale_two[...] * (cot[...].astype(F32) * row_mask(scal, cot.shape[0]))).astype(BF)
        grad_mlp[...] = grad_low
        grad_rank[...] = dotg(grad_low, pad_rows(db[...]), 1, 1).astype(BF)
    if more == 6:
        gub_out[...], gda_out[...] = earlier[4][...], earlier[5][...]
    ubs[...] = jnp.zeros_like(ubs)
    das[...] = jnp.zeros_like(das)
    for piece in range(pieces):
        at = slice(piece * size, (piece + 1) * size)
        ubs[0:rank, at] = ub[:, place(piece)]
        das[0:rank, at] = da[:, place(piece)]
    up_turned = rank_up[...].T[0:rank]
    grad_turned = grad_rank[...].T[0:rank]

    def first(k):
        for copy in waits[k]:
            copy.wait()
        at = slice(k * step, (k + 1) * step)
        return (
            dotg(n2[...], wu[:, at], 1, 0) + dotg(rank_up[...], ubs[:, at], 1, 0),
            dotg(grad_mlp[...], wd[at, :], 1, 1) + dotg(grad_rank[...], das[:, at], 1, 0),
        )

    ahead = first(0)
    for k in range(chunks):
        at = slice(k * step, (k + 1) * step)
        preact, grad_hidden = ahead
        if k + 1 < chunks:
            ahead = first(k + 1)
        cdf = 0.5 * (1.0 + lax.erf(preact * 0.7071067811865476))
        hidden[:, at] = (preact * cdf).astype(BF)
        slope = cdf + preact * jnp.exp(-0.5 * preact * preact) * 0.3989422804014327
        grad_pre[:, at] = (grad_hidden * slope).astype(BF)
    ranked = dotg(hidden[...], das[...], 1, 1)
    grad_ranked = dotg(grad_pre[...], ubs[...], 1, 1)
    if more:
        ranked, grad_ranked = ranked + earlier[2][...], grad_ranked + earlier[3][...]
    rd_out[...] = ranked
    gru_out[...] = grad_ranked
    for piece in range(pieces):
        at = slice(piece * size, (piece + 1) * size)
        gub_out[:, place(piece)] = dotg(up_turned, grad_pre[:, at], 1, 0)
        gda_out[:, place(piece)] = dotg(grad_turned, hidden[:, at], 1, 0)
    if more:
        for copy in early:
            copy.wait()
    for at in (slice(k, k + step) for k in range(0, wu.shape[0], step)):
        terms = dotg(hidden[...], wd[:, at], 1, 0)
        grad_terms = dotg(grad_pre[...], wu[at, :], 1, 1)
        if more:
            m_out[:, at] += terms
            g_out[:, at] += grad_terms
        else:
            m_out[:, at] = terms
            g_out[:, at] = grad_terms


def mlp(scal, n2, rank_up, ub, da, ups, downs, grads, nears=None, earlier=()):
    rows, width = n2.shape
    rank, half = ub.shape
    units = half if nears is None else len(nears) * half // PARTS
    step = min(512, units)
    sums = jax.ShapeDtypeStruct((rows, width), F32)
    ranked = jax.ShapeDtypeStruct((rows, PAD), F32)
    table = jax.ShapeDtypeStruct((rank, half), F32)
    low = jax.ShapeDtypeStruct((rows, width), BF)
    first = [low, low, jax.ShapeDtypeStruct((rows, PAD), BF)] if nears is None else []
    return pl.pallas_call(
        functools.partial(mlp_kernel, nears, step, len(earlier)),
        in_specs=[scalars()]
        + [whole()] * 4
        + [in_place()] * (2 * len(ups))
        + ([in_place()] * 2 if nears is None else [])
        + [whole()] * 2
        + ([in_place()] * 2 + [whole()] * (len(earlier) - 2) if earlier else []),
        out_specs=[whole()] * (len(first) + 6),
        out_shape=first + [sums, sums, ranked, ranked, table, table],
        scratch_shapes=[
            pltpu.VMEM((width, units), BF),
            pltpu.VMEM((units, width), BF),
            pltpu.VMEM((PAD, units), BF),
            pltpu.VMEM((PAD, units), BF),
            pltpu.VMEM((rows, units), BF),
            pltpu.VMEM((rows, units), BF),
            pltpu.SemaphoreType.DMA((2, PARTS)),
            pltpu.SemaphoreType.DMA((2,)),
        ],
        compiler_params=params(),
        cost_estimate=cost(25e-6 * units / half * 1e15, 20e6),
        name="mlp",
    )(scal, n2, rank_up, ub, da, *ups, *downs, *grads, *earlier)


def mlp_other(scal, n2, rank_up, ub, da, up, down, grads, earlier):
    for odd in range(2):
        ups, nears = up.held(odd)
        downs, same = down.held(odd)
        assert nears == same
        earlier = mlp(scal, n2, rank_up, ub, da, ups, downs, grads, nears, tuple(earlier))
    return earlier


def middle_kernel(
    scal, residual, m_in, g_in, rd, gru, cot, mix_a, mix_b, rank_out, n2, grad_mlp,
    db, ua, scale_two, gain_two, scale_one, w_a, w_b, oa_a, oa_b, ob,
    layer, grad_res, grad_a, grad_b, goa_a, goa_b, gob, gua, gdb,
):
    step = pl.program_id(0)
    rows = residual.shape[0]
    rank = db.shape[0]
    at = lax.broadcasted_iota(jnp.int32, (rows, 1), 0) + (scal[1] * 2 + step) * rows
    valid = (at < scal[0]).astype(F32)
    down = two_terms(rd[...], rank)
    up = two_terms(gru[...], rank)

    def add(out, terms):
        @pl.when(step == 0)
        def _():
            out[...] = terms

        @pl.when(step > 0)
        def _():
            out[...] += terms

    def turned(terms, right):
        both = dotg(terms.T[0 : 2 * rank], right, 1, 0)
        return both[0:rank] + both[rank : 2 * rank]

    branch_out = m_in[...] + dotg(down, pad_twice(db[...]), 1, 0)
    layer[...] = ((residual[...] + scale_two[...] * branch_out) * valid).astype(BF)
    add(gua, turned(up, n2[...]))
    add(gdb, turned(down, grad_mlp[...]))
    unit, scale = norm_stats(residual[...])
    grad_normed = (g_in[...] + dotg(up, pad_twice(ua[...]), 1, 0)) * gain_two[...]
    grad_total = cot[...].astype(F32) * valid + norm_grad(unit, scale, grad_normed)
    grad_res[...] = grad_total
    grad_attn = (scale_one[...] * grad_total).astype(BF)
    grad_rank = dotg(grad_attn, pad_rows(ob[...]), 1, 1).astype(BF)
    grad_a[...] = (
        dotg(grad_attn, w_a[...], 1, 1) + dotg(grad_rank, pad_rows(oa_a[...]), 1, 0)
    ).astype(BF)
    grad_b[...] = (
        dotg(grad_attn, w_b[...], 1, 1) + dotg(grad_rank, pad_rows(oa_b[...]), 1, 0)
    ).astype(BF)
    rank_turned = grad_rank.T[0:rank]
    add(goa_a, dotg(rank_turned, mix_a[...], 1, 0))
    add(goa_b, dotg(rank_turned, mix_b[...], 1, 0))
    add(gob, turned(rank_out[...], grad_attn))


def middle(scal, by_rows, others):
    rows, width = by_rows[0].shape
    block = rows // 2
    heads = by_rows[6].shape[1]
    rank = others[0].shape[0]
    part = jax.ShapeDtypeStruct((rows, heads), BF)
    table = jax.ShapeDtypeStruct((rank, width), F32)
    half_table = jax.ShapeDtypeStruct((rank, heads), F32)
    return pl.pallas_call(
        middle_kernel,
        grid=(2,),
        in_specs=[scalars()]
        + [blocked(block, array.shape[1]) for array in by_rows]
        + [fixed_block(*array.shape) for array in others],
        out_specs=[blocked(block, width), blocked(block, width), blocked(block, heads), blocked(block, heads)]
        + [fixed_block(*shape) for shape in ((rank, heads),) * 2 + ((rank, width),) * 3],
        out_shape=[jax.ShapeDtypeStruct((rows, width), BF), jax.ShapeDtypeStruct((rows, width), F32)]
        + [part, part, half_table, half_table, table, table, table],
        compiler_params=params(dimension_semantics=("arbitrary",)),
        cost_estimate=cost(9e-6 * 1e15, 20e6),
        name="middle",
    )(scal, *by_rows, *others)


def columns_of(pieces):
    first = 0
    for piece in pieces:
        yield piece, slice(first, first + piece.shape[-1])
        first += piece.shape[-1]


def qkv_tables_kernel(count, *refs):
    sides, refs = (refs[: 3 * count], refs[3 * count : 6 * count]), refs[6 * count :]
    scal, qb_a, qb_b, n1, rank_in, total_a, total_b, rank_out, kept, sent, gqb_a, gqb_b, gqa = refs
    rank = qb_a.shape[0]
    third = qb_a.shape[1] // 3
    rank_turned = rank_in[...].T[0:rank]
    ranked = None
    for side, qb, total, table in zip(sides, (qb_a, qb_b), (total_a, total_b), (gqb_a, gqb_b)):
        queries, owns, gots = side[:count], side[count : 2 * count], side[2 * count :]
        for (piece, at), own, got in zip(columns_of(queries), owns, gots):
            for c in range(3):
                if c == 0:
                    grad = piece[...]
                else:
                    grad = (own[c - 1].astype(F32) + got[c - 1].astype(F32)).astype(BF)
                    total[c - 1, :, at] = grad
                place = slice(c * third + at.start, c * third + at.stop)
                table[:, place] = dotg(rank_turned, grad, 1, 0)
                terms = dotg(grad, pad_rows(qb[:, place]), 1, 1)
                ranked = terms if ranked is None else ranked + terms
    ranked = two_terms(ranked, rank)
    rank_out[...] = ranked
    both = dotg(ranked.T[0 : 2 * rank], n1[...], 1, 0)
    gqa[...] = both[0:rank] + both[rank : 2 * rank]
    first = 0
    for table in (gqb_a, gqa, gqb_b):
        half = table.shape[1] // 2
        at = slice(first, first + half)
        kept[:, at] = table[:, pl.ds(pl.multiple_of(scal[1] * half, half), half)]
        sent[:, at] = table[:, pl.ds(pl.multiple_of((1 - scal[1]) * half, half), half)].astype(BF)
        first += half


def qkv_tables(scal, side_a, side_b, qb_a, qb_b, n1, rank_in):
    rows, width = n1.shape
    rank, columns = qb_a.shape
    count = len(side_a) // 3
    total = jax.ShapeDtypeStruct((2, rows, columns // 3), BF)
    share = columns + width // 2
    return pl.pallas_call(
        functools.partial(qkv_tables_kernel, count),
        in_specs=[whole()] * (6 * count) + [scalars()] + [whole()] * 4,
        out_specs=[whole()] * 5,
        out_shape=[total, total, jax.ShapeDtypeStruct((rows, PAD), BF)]
        + [jax.ShapeDtypeStruct((rank, share), F32), jax.ShapeDtypeStruct((rank, share), BF)],
        scratch_shapes=[pltpu.VMEM((rank, columns), F32)] * 2 + [pltpu.VMEM((rank, width), F32)],
        compiler_params=params(),
        cost_estimate=cost(7e-6 * 1e15, 14e6),
        name="qkv_tables",
    )(*side_a, *side_b, scal, qb_a, qb_b, n1, rank_in)


def qkv_rows_kernel(count, *refs):
    grads_a, grads_b, refs = refs[: count + 1], refs[count + 1 : 2 * count + 2], refs[2 * count + 2 :]
    w_a, w_b, ranked, qa, tok, gain, grad_res, out = refs
    grad = dotg(ranked[...], pad_twice(qa[...]), 1, 0)
    for grads, w in ((grads_a, w_a), (grads_b, w_b)):
        for piece, at in columns_of(grads[:count]):
            grad = grad + dotg(piece[...], w[0, :, at], 1, 1)
        for c in (1, 2):
            grad = grad + dotg(grads[count][c - 1], w[c], 1, 1)
    unit, scale = norm_stats(tok[...].astype(F32))
    out[...] = (grad_res[...] + norm_grad(unit, scale, grad * gain[...])).astype(BF)


def qkv_rows(block_at, blocks, grads_a, grads_b, w_a, w_b, ranked, qa, tok, gain, grad_res):
    rows, width = tok.shape
    block = rows // blocks
    flat = lambda array: pl.BlockSpec((block, array.shape[1]), lambda step: (block_at, 0))
    deep = lambda array: pl.BlockSpec((2, block, array.shape[2]), lambda step: (0, block_at, 0))
    specs = [flat(array) if array.ndim == 2 else deep(array) for array in grads_a + grads_b]
    return pl.pallas_call(
        functools.partial(qkv_rows_kernel, len(grads_a) - 1),
        grid=(1,),
        in_specs=specs
        + [whole(), whole(), flat(ranked), whole(), flat(tok), whole(), flat(grad_res)],
        out_specs=whole(),
        out_shape=jax.ShapeDtypeStruct((block, width), BF),
        compiler_params=params(),
        cost_estimate=cost(12e-6 / blocks * 1e15, 16e6 / blocks),
        name="qkv_rows",
    )(*grads_a, *grads_b, w_a, w_b, ranked, qa, tok, gain, grad_res)


def gather_kernel(ids, images, out, total):
    columns = out.shape[2]
    total[...] = jnp.zeros_like(total)
    for image in range(images.shape[0]):
        adapter = ids[image]
        total[adapter] += images[image, :, 0:columns].astype(F32)
    out[...] = total[...].astype(BF)


def gather_images(ids, images, adapters, columns):
    rank = images.shape[1]
    return pl.pallas_call(
        gather_kernel,
        in_specs=[scalars(), whole()],
        out_specs=whole(),
        out_shape=jax.ShapeDtypeStruct((adapters, rank, columns), BF),
        scratch_shapes=[pltpu.VMEM((adapters, rank, columns), F32)],
        compiler_params=params(),
        cost_estimate=cost(2e-6 * 1e15, 1e6),
        name="gather_images",
    )(ids, images)


def finish_kernel(cut, spans, places, core, own, other, *outs):
    def write(low, high):
        for (shared, start, stop), (number, index) in zip(spans, places):
            first = cut if shared else 0
            half = own.shape[2] - cut if shared else cut
            out = outs[number] if index is None else outs[number].at[:, index]
            middle = min(max(half - start, 0), stop - start)
            if middle > 0:
                out[:, :, 0:middle] = low[:, :, first + start : first + start + middle].astype(F32)
            if middle < stop - start:
                begin = first + start + middle - half
                out[:, :, middle : stop - start] = high[:, :, begin : first + stop - half].astype(F32)

    @pl.when(core[0] == 0)
    def _():
        write(own, other)

    @pl.when(core[0] != 0)
    def _():
        write(other, own)


def finish(core, cut, spans, places, own, other, shapes):
    return pl.pallas_call(
        functools.partial(finish_kernel, cut, spans, places),
        in_specs=[scalars(), whole(), whole()],
        out_specs=[whole()] * len(shapes),
        out_shape=[jax.ShapeDtypeStruct(shape, F32) for shape in shapes],
        compiler_params=params(),
        cost_estimate=cost(2e-6 * 1e15, 4e6),
        name="finish",
    )(core, own, other)


def swap(rows):
    return lax.ppermute(rows, ("core", "tensor"), SWAP)


def flip(axis):
    return lambda array: lax.ppermute(array, axis, FLIP)


def after(value, *others):
    return lax.optimization_barrier((value, others))[0]


class OtherHalf:
    BITS = {"core": 1, "x": 2, "zb": 4}

    def __init__(self, local, axis, part_at, count):
        size = local.shape[axis] // count
        self.mine = lax.dynamic_slice_in_dim(local, (part_at % count) * size, size, axis)
        self.parts = {}
        self.nears = tuple(range(0, count, 2))

    def over_tensor(self, *others):
        self.parts[0] = flip("tensor")(after(self.mine, *others) if others else self.mine)

    def hop(self, near, axis, *others):
        part = after(self.parts[near], *others) if others else self.parts[near]
        self.parts[near ^ self.BITS[axis]] = flip(axis)(part)

    def last_hop(self):
        over_zb, over_x = jnp.split(self.parts[2], 2, axis=1)[0], jnp.split(self.parts[4], 2, axis=1)[1]
        self.parts[6] = jnp.concatenate([flip("zb")(over_zb), flip("x")(over_x)], axis=1)

    def pairs_over_cores(self, *others):
        parts = after(self.parts, *others) if others else self.parts
        even = [jnp.stack([parts[a], parts[b]]) for a, b in zip(self.nears[::2], self.nears[1::2])]
        self.pairs = even + [flip("core")(array) for array in even]
        self.names = self.nears + tuple(near + 1 for near in self.nears)

    def held(self, odd):
        names = tuple(near + odd for near in self.nears)
        return [self.parts[near] for near in names], names


def half_columns(array, index):
    size = array.shape[1] // 2
    return lax.dynamic_slice_in_dim(array, index * size, size, 1)


def by_index(index, own, other, axis):
    return jnp.where(
        index == 0, jnp.concatenate([own, other], axis=axis), jnp.concatenate([other, own], axis=axis)
    )


class Sum:
    def __init__(self, kept, sent, cut, adapter, core, tensor):
        self.core, self.tensor, self.adapter = core, tensor, adapter
        self.kept, self.sent, self.cut = kept, sent, cut

    @staticmethod
    def shares(near, shared, far, core):
        def share(index):
            return jnp.concatenate([half_columns(array, index) for array in (near, shared, far)], axis=1)

        return share(core), share(1 - core).astype(BF)

    def over_cores(self):
        total = (self.kept + flip("core")(self.sent).astype(F32)).astype(BF)
        cut, columns = self.cut, total.shape[1] - self.cut
        note = []
        if self.adapter is not None:
            note = [jnp.broadcast_to(self.adapter.astype(BF), (total.shape[0], PAD))]
        self.mine = jnp.concatenate([total[:, :columns]] + note, axis=1)
        self.send = jnp.concatenate([total[:, columns:], total[:, cut:columns]] + note, axis=1)
        self.columns = columns

    def over_pair(self, *others):
        other = flip("tensor")(self.send)
        other = after(other, *others) if others else other
        self.images = by_index(self.tensor, self.mine[None], other[None], 0)

    def over(self, name, *others):
        if lax.axis_size(name) == 2:
            got = flip(name)(self.images)
            self.images = by_index(lax.axis_index(name), self.images, after(got, *others) if others else got, 0)
        elif lax.axis_size(name) > 2:
            self.images = lax.all_gather(self.images, name, axis=0, tiled=True)

    def adapters_of_images(self):
        return self.images[:, 0, -1].astype(jnp.int32)

    def over_adapters(self, ids, adapters):
        self.dense = gather_images(ids, self.images, adapters, self.columns)
        self.other = flip("core")(self.dense)

    def finish(self, spans, places, shapes):
        core = self.core.astype(jnp.int32)[None]
        return finish(core, self.cut, spans, places, self.dense, self.other, shapes)


def quad_body(
    tokens, cotangent, lengths, adapter_ids, gain_one, gain_two, scale_one, scale_two, w_qkv, w_out, w_up, w_down,
    qkv_a, qkv_b, out_a, out_b, up_a, up_b, down_a, down_b,
):
    core, tensor = lax.axis_index("core"), lax.axis_index("tensor")
    part_at = lax.axis_index("zb") * 4 + lax.axis_index("x") * 2 + core
    adapters, rank, width = qkv_a.shape
    third = w_qkv.shape[2]
    units = w_up.shape[1]

    w3 = jnp.swapaxes(w_qkv, 0, 1)
    half_qkv = OtherHalf(w3, 1, part_at, PARTS)
    half_out = OtherHalf(w_out, 0, part_at, 4)
    half_up = OtherHalf(w_up, 1, part_at, PARTS)
    half_down = OtherHalf(w_down, 0, part_at, PARTS)
    half_qkv.over_tensor()
    tok_here = tokens[0]
    tok_swapped = swap(tok_here)
    facts = jnp.stack([lengths[0], adapter_ids[0]])
    facts_other = flip("core")(facts)
    mine = jnp.where(core == tensor, facts, facts_other)
    theirs = jnp.where(core == tensor, facts_other, facts)
    length, adapter, adapter_other = mine[0], mine[1], theirs[1]
    scal = jnp.stack([length, core, part_at, core == tensor]).astype(jnp.int32)

    qkv_b, out_b, up_b, down_b = (jnp.swapaxes(table, -1, -2) for table in (qkv_b, out_b, up_b, down_b))
    pick = lambda table, index: lax.dynamic_index_in_dim(table, index, 0, False)
    flat = lambda table: jnp.swapaxes(table, 0, 1).reshape(rank, 3 * third)
    packed_first = jnp.concatenate([flat(pick(qkv_b, adapter_other)), pick(out_a, adapter_other)], axis=1)
    packed = jnp.concatenate([pick(table, adapter_other) for table in (up_b, down_a)], axis=1)
    qa, oa, ob, ua, ub, da, db = (
        pick(table, adapter) for table in (qkv_a, out_a, out_b, up_a, up_b, down_a, down_b)
    )
    qb = flat(pick(qkv_b, adapter))
    gain_one, gain_two, scale_one, scale_two = (v.reshape(1, width) for v in (gain_one, gain_two, scale_one, scale_two))

    half_qkv.hop(0, "x")
    half_qkv.hop(0, "zb")
    slices = (scal, packed, packed_first, qa, oa, ob, ua, ub, da, db, qb, half_out.mine, half_up.mine, half_down.mine)
    qb_other, oa_other = jnp.split(flip("tensor")(after(packed_first, half_qkv.parts[0])), (3 * third,), axis=1)
    half_up.over_tensor(half_qkv.parts[4])
    half_qkv.parts[2] = after(half_qkv.parts[2], *slices)
    half_qkv.last_hop()
    tok_swapped = after(tok_swapped, half_qkv.parts[2], half_qkv.parts[4], qb_other, scal)
    tok, n1, rank_qkv, q_a, own_a = qkv_local(scal, tok_here, tok_swapped, gain_one, w3, qa, qb)
    half_qkv.pairs_over_cores()
    kv_a = flip("core")(own_a)
    q_b, own_b, w3_other = qkv_other(scal, after(n1, half_up.parts[0]), rank_qkv, qb_other, half_qkv)
    kv_b = flip("core")(own_b)
    half_out.over_tensor(own_b)
    half_up.hop(0, "x", own_b)
    half_up.hop(0, "zb", own_b)
    cot_swapped = swap(after(cotangent[0], own_b))
    mix_a, logs_a = attend(scal, after(q_a, own_b), own_a, kv_a)
    half_out.hop(0, "x", mix_a)
    half_up.hop(4, "x", mix_a)
    half_down.over_tensor(mix_a)
    mix_b, logs_b = attend(scal, after(q_b, mix_a, half_up.parts[2], half_up.parts[4]), own_b, kv_b)
    half_out.pairs_over_cores(mix_b)
    half_down.hop(0, "x", mix_b)
    half_down.hop(0, "zb", mix_b)
    residual, n2, rank_out, rank_up, out_other = branch(
        scal, mix_a, mix_b, tok, w_out, half_out, oa, oa_other, ob, scale_one, gain_two, ua
    )
    half_down.hop(2, "zb", n2)
    ub_other, da_other = jnp.split(flip("tensor")(after(packed, n2)), 2, axis=1)
    for near in (0, 2, 4):
        half_up.hop(near, "core", n2)
    cot, grad_mlp, grad_rank, m, g, rd, gru, gub_a, gda_a = mlp(
        scal, n2, rank_up, ub, da, [w_up], [w_down], [cotangent[0], cot_swapped, scale_two, db]
    )
    half_up.hop(6, "core", m)
    for near in (0, 2, 4, 6):
        half_down.hop(near, "core", m)
    m, g, rd, gru, gub_b, gda_b = mlp_other(
        scal, n2, rank_up, ub_other, da_other, half_up, half_down, [grad_mlp, grad_rank], (m, g, rd, gru)
    )
    layer, grad_res, grad_a, grad_b, goa_a, goa_b, gob, gua, gdb = middle(
        scal,
        (residual, m, g, rd, gru, cot, mix_a, mix_b, rank_out, n2, grad_mlp),
        (db, ua, scale_two, gain_two, scale_one, w_out, out_other, oa, oa_other, ob),
    )
    shares = Sum.shares(
        jnp.concatenate([goa_a, gub_a, gda_a], axis=1),
        jnp.concatenate([gob, gua, gdb], axis=1),
        jnp.concatenate([goa_b, gub_b, gda_b], axis=1),
        core,
    )
    early = Sum(*shares, third // 2 + units, adapter, core, tensor)
    early.over_cores()

    def back(queries, own, kv, mixed, grad, logs, piece, *others):
        queries = after(queries, *others) if others else queries
        grad_queries, kept, sent = attend_back(scal, queries, own, kv, mixed, grad, logs, piece, 2)
        return grad_queries, kept, flip("core")(sent)

    side_a, side_b = (q_a, own_a, kv_a, mix_a, grad_a, logs_a), (q_b, own_b, kv_b, mix_b, grad_b, logs_b)
    back_1 = back(*side_a, 0)
    layer_swapped = swap(after(layer, back_1[0]))
    early.send = after(early.send, back_1[0])
    back_2 = back(*side_a, 1, early.send)
    early.over_pair(back_2[0])
    back_3 = back(*side_b, 0, early.images)
    early.over("hi", back_3[0])
    back_4 = back(*side_b, 1, early.images, layer_swapped)
    early.over("zb", back_4[0])
    kv_sum_a, kv_sum_b, ranked, kept, sent = qkv_tables(
        after(scal, early.images),
        [part for pair in zip(back_1, back_2) for part in pair],
        [part for pair in zip(back_3, back_4) for part in pair],
        qb, qb_other, n1, rank_qkv,
    )
    late = Sum(kept, sent, 3 * third // 2, None, core, tensor)
    late.over_cores()
    early.over("x", kept)
    grads = (
        [back_1[0], back_2[0], kv_sum_a], [back_3[0], back_4[0], kv_sum_b],
        w3, w3_other, ranked, qa, tok, gain_one, grad_res,
    )
    upper = qkv_rows(0, 2, grads[0], grads[1], after(w3, late.send), *grads[3:])
    late.over_pair(upper)
    lower = qkv_rows(1, 2, grads[0], grads[1], after(w3, late.images), *grads[3:])
    late.over("hi", lower)
    late.over("zb")
    ids = early.adapters_of_images()
    early.over_adapters(ids, adapters)
    late.over("x")
    in_place_already = core == tensor
    grad_tokens = jnp.concatenate(
        [jnp.where(in_place_already, rows, swap(rows)) for rows in (upper, lower)], axis=0
    ).astype(F32)
    layer_out = jnp.where(in_place_already, layer, layer_swapped)
    late.over_adapters(ids, adapters)
    ends = (0, third, third + units, third + 2 * units)
    spans = [(False, ends[k], ends[k + 1]) for k in range(3)] + [(True, k * width, (k + 1) * width) for k in range(3)]
    widths = (third, units, units, width, width, width)
    sum_oa, sum_ub, sum_da, sum_ob, sum_ua, sum_db = early.finish(
        spans, [(k, None) for k in range(6)], [(adapters, rank, size) for size in widths]
    )
    sum_qb, sum_qa = late.finish(
        [(False, c * third, (c + 1) * third) for c in range(3)] + [(True, 0, width)],
        [(0, c) for c in range(3)] + [(1, None)],
        [(adapters, 3, rank, third), (adapters, rank, width)],
    )
    turn = lambda table: jnp.swapaxes(table, -1, -2)
    return (
        layer_out[None],
        grad_tokens[None],
        sum_qa,
        turn(sum_qb),
        sum_oa,
        turn(sum_ob),
        sum_ua,
        turn(sum_ub),
        sum_da,
        turn(sum_db),
    )


def solution(mesh):
    groups, split = mesh.shape["dp"], mesh.shape["tensor"]
    if split == 2 and groups % 8 == 0:
        mesh = Mesh(mesh.devices.reshape(groups // 8, 2, 2, 2, 2), ("hi", "zb", "x", "core", "tensor"))
        dp, body = ("hi", "zb", "x", "core"), quad_body
    else:
        dp, body = "dp", plain_body
    slots = P(dp, "tensor", None)
    in_specs = (
        slots, slots, P(dp), P(dp), P(), P(), P(), P(),
        P(None, None, "tensor"), P("tensor", None), P(None, "tensor"), P("tensor", None),
        P(), P(None, None, "tensor", None), P(None, None, "tensor"), P(),
        P(), P(None, "tensor", None), P(None, None, "tensor"), P(),
    )
    out_specs = (
        slots, slots, P(), P(None, None, "tensor", None), P(None, None, "tensor"), P(),
        P(), P(None, "tensor", None), P(None, None, "tensor"), P(),
    )
    return jax.shard_map(body, mesh=mesh, in_specs=in_specs, out_specs=out_specs, check_vma=False)
```

```python
import functools

import jax
import jax.numpy as jnp
from jax import lax
from jax.experimental import pallas as pl
from jax.experimental.pallas import tpu as pltpu
from jax.sharding import Mesh
from jax.sharding import PartitionSpec as P

HD = 64
ADAPTERS = 8


epsilon = 1e-06
masked_score = -1e30
HIGHEST = lax.Precision.HIGHEST


def product(form, left, right):
    return jnp.einsum(form, left, right, preferred_element_type=jnp.float32)


def precise(form, left, right):
    return jnp.einsum(form, left.astype(jnp.float32), right.astype(jnp.float32), precision=HIGHEST)


def select_rows(onehot, table):
    return product("sn,n...->s...", onehot, table).astype(table.dtype)


def norm_rows(values, gain_vec):
    average = jnp.mean(values, axis=-1, keepdims=True)
    centred = values - average
    variance = jnp.mean(centred * centred, axis=-1, keepdims=True)
    return centred * lax.rsqrt(variance + epsilon) * gain_vec


def norm_back(values, gain_vec, grad_normed):
    normed, pullback = jax.vjp(lambda rows: norm_rows(rows, gain_vec), values)
    return pullback(grad_normed)[0]


def gelu_slope(values):
    return (
        0.5 * (1.0 + lax.erf(values * 0.7071067811865476))
        + values * jnp.exp(-0.5 * values * values) * 0.3989422804014327
    )


def ffn_forward(rows_low, up_mat, down_mat, up_a_sel, up_b_sel, down_a_sel, down_b_sel):
    rank_up = product("std,srd->str", rows_low, up_a_sel).astype(jnp.bfloat16)
    preact = product("std,dh->sth", rows_low, up_mat) + product("str,shr->sth", rank_up, up_b_sel)
    hidden = jax.nn.gelu(preact, approximate=False).astype(jnp.bfloat16)
    rank_down = product("sth,srh->str", hidden, down_a_sel)
    terms = product("sth,hd->std", hidden, down_mat) + precise(
        "str,sdr->std", rank_down, down_b_sel
    )
    return (rank_up, preact, hidden, rank_down, terms)


def ffn_backward(
    rows_low,
    grad_rows,
    up_mat,
    down_mat,
    up_a_sel,
    up_b_sel,
    down_a_sel,
    down_b_sel,
    rank_up,
    preact,
    hidden,
    rank_down,
):
    grad_rank_down = product("std,sdr->str", grad_rows, down_b_sel).astype(jnp.bfloat16)
    grad_hidden = product("std,hd->sth", grad_rows, down_mat) + product(
        "str,srh->sth", grad_rank_down, down_a_sel
    )
    grad_preact = (grad_hidden * gelu_slope(preact)).astype(jnp.bfloat16)
    grad_up_b = product("sth,str->shr", grad_preact, rank_up)
    grad_rank_up = product("sth,shr->str", grad_preact, up_b_sel)
    grad_rows_in = product("sth,dh->std", grad_preact, up_mat) + precise(
        "str,srd->std", grad_rank_up, up_a_sel
    )
    grad_up_a = precise("str,std->srd", grad_rank_up, rows_low)
    grad_down_a = product("str,sth->srh", grad_rank_down, hidden)
    grad_down_b = precise("std,str->sdr", grad_rows, rank_down)
    return (grad_rows_in, (grad_up_a, grad_up_b, grad_down_a, grad_down_b))


def plain_body(
    tokens,
    cotangent,
    lengths,
    adapter_ids,
    gain_one,
    gain_two,
    scale_one,
    scale_two,
    w_qkv,
    w_out,
    w_up,
    w_down,
    qkv_a,
    qkv_b,
    out_a,
    out_b,
    up_a,
    up_b,
    down_a,
    down_b,
):
    shard_rows = tokens.shape[1]
    seq_len = shard_rows * lax.axis_size("tensor")
    heads_local = w_qkv.shape[2] // HD
    scale_attn = HD ** (-0.5)
    first_row = lax.axis_index("tensor") * shard_rows
    positions = jnp.arange(seq_len, dtype=jnp.int32)
    key_valid = positions[None, :] < jnp.maximum(lengths, 1)[:, None]
    local_rows = first_row + jnp.arange(shard_rows, dtype=jnp.int32)
    row_valid = (local_rows[None, :] < lengths[:, None]).astype(jnp.float32)[:, :, None]
    adapters = jnp.arange(ADAPTERS, dtype=jnp.int32)
    onehot = (adapter_ids[:, None] == adapters[None, :]).astype(jnp.bfloat16)
    qkv_a_sel = select_rows(onehot, qkv_a)
    qkv_b_sel = select_rows(onehot, qkv_b)
    out_a_sel = select_rows(onehot, out_a)
    out_b_sel = select_rows(onehot, out_b)
    up_a_sel = select_rows(onehot, up_a)
    down_b_sel = select_rows(onehot, down_b)
    inputs = tokens.astype(jnp.float32)
    normed_one = norm_rows(inputs, gain_one).astype(jnp.bfloat16)
    full_one = lax.all_gather(normed_one, "tensor", axis=1, tiled=True)
    rank_qkv = product("std,srd->str", full_one, qkv_a_sel).astype(jnp.bfloat16)
    projected = (
        product("std,dcf->sctf", full_one, w_qkv) + product("str,scfr->sctf", rank_qkv, qkv_b_sel)
    ).astype(jnp.bfloat16)

    def split_heads(rows):
        return rows.reshape(seq_len, heads_local, HD)

    def masked_scores(queries, keyrows, valid_keys):
        scores = product("qhe,khe->hqk", queries, keyrows) * scale_attn
        return jnp.where(valid_keys[None, None, :], scores, masked_score)

    def attend(slot_items):
        slot_block, valid_keys = slot_items
        queries = split_heads(slot_block[0])
        keyrows = split_heads(slot_block[1])
        values = split_heads(slot_block[2])
        scores = masked_scores(queries, keyrows, valid_keys)
        row_max = jnp.max(scores, axis=-1, keepdims=True)
        exponent = jnp.exp(scores - row_max)
        row_total = jnp.sum(exponent, axis=-1, keepdims=True)
        soft_low = (exponent / row_total).astype(jnp.bfloat16)
        mixed_rows = (
            product("hqk,khe->qhe", soft_low, values).astype(jnp.bfloat16).reshape(seq_len, -1)
        )
        return (mixed_rows, (row_max + jnp.log(row_total))[:, :, 0])

    mixed, log_total = lax.map(attend, (projected, key_valid))
    rank_out = product("stf,srf->str", mixed, out_a_sel)
    attn_terms = product("stf,fd->std", mixed, w_out) + precise("str,sdr->std", rank_out, out_b_sel)
    attn_branch = lax.psum_scatter(attn_terms, "tensor", scatter_dimension=1, tiled=True)
    residual = inputs + scale_one * attn_branch
    normed_two = norm_rows(residual, gain_two).astype(jnp.bfloat16)
    up_mat, down_mat, up_b_all, down_a_all = (
        lax.all_gather(w_up, "tensor", axis=1, tiled=True),
        lax.all_gather(w_down, "tensor", axis=0, tiled=True),
        lax.all_gather(up_b, "tensor", axis=1, tiled=True),
        lax.all_gather(down_a, "tensor", axis=2, tiled=True),
    )
    up_b_sel = select_rows(onehot, up_b_all)
    down_a_sel = select_rows(onehot, down_a_all)
    rank_up, preact, hidden, rank_down, ffn_terms = ffn_forward(
        normed_two, up_mat, down_mat, up_a_sel, up_b_sel, down_a_sel, down_b_sel
    )
    layer_out = ((residual + scale_two * ffn_terms) * row_valid).astype(jnp.bfloat16)
    grad_out = cotangent.astype(jnp.float32) * row_valid
    grad_mlp = (scale_two * grad_out).astype(jnp.bfloat16)
    ffn_grad_in, ffn_grads = ffn_backward(
        normed_two,
        grad_mlp,
        up_mat,
        down_mat,
        up_a_sel,
        up_b_sel,
        down_a_sel,
        down_b_sel,
        rank_up,
        preact,
        hidden,
        rank_down,
    )
    grad_residual = grad_out + norm_back(residual, gain_two, ffn_grad_in)
    grad_attn = (scale_one * grad_residual).astype(jnp.bfloat16)
    full_grad_attn = lax.all_gather(grad_attn, "tensor", axis=1, tiled=True)
    grad_rank_out = product("std,sdr->str", full_grad_attn, out_b_sel).astype(jnp.bfloat16)
    grad_mixed = (
        product("std,fd->stf", full_grad_attn, w_out)
        + product("str,srf->stf", grad_rank_out, out_a_sel)
    ).astype(jnp.bfloat16)
    grad_out_a = product("str,stf->srf", grad_rank_out, mixed)
    grad_out_b = precise("std,str->sdr", full_grad_attn, rank_out)

    def attend_back(slot_items):
        slot_block, valid_keys, log_rows, grad_rows = slot_items
        queries = split_heads(slot_block[0])
        keyrows = split_heads(slot_block[1])
        values = split_heads(slot_block[2])
        scores = masked_scores(queries, keyrows, valid_keys)
        soft = jnp.exp(scores - log_rows[:, :, None])
        soft_low = soft.astype(jnp.bfloat16)
        grad_heads = split_heads(grad_rows)
        grad_soft = product("qhe,khe->hqk", grad_heads, values)
        grad_values = product("hqk,qhe->khe", soft_low, grad_heads)
        grad_scores = (
            soft * (grad_soft - jnp.sum(soft * grad_soft, axis=-1, keepdims=True))
        ).astype(jnp.bfloat16)
        grad_queries = product("hqk,khe->qhe", grad_scores, keyrows) * scale_attn
        grad_keys = product("hqk,qhe->khe", grad_scores, queries) * scale_attn
        return (
            jnp.stack([grad_queries, grad_keys, grad_values])
            .reshape(3, seq_len, -1)
            .astype(jnp.bfloat16)
        )

    grad_projected = lax.map(attend_back, (projected, key_valid, log_total, grad_mixed))
    grad_qkv_b = product("sctf,str->scfr", grad_projected, rank_qkv)
    grad_rank_qkv = product("sctf,scfr->str", grad_projected, qkv_b_sel)
    grad_one_terms = product("sctf,dcf->std", grad_projected, w_qkv) + precise(
        "str,srd->std", grad_rank_qkv, qkv_a_sel
    )
    grad_qkv_a = precise("str,std->srd", grad_rank_qkv, full_one)
    grad_normed_one = lax.psum_scatter(grad_one_terms, "tensor", scatter_dimension=1, tiled=True)
    grad_tokens = grad_residual + norm_back(inputs, gain_one, grad_normed_one)
    onehot_wide = onehot.astype(jnp.float32)

    def stack_slots(slot_grads):
        return jnp.einsum("sn,s...->n...", onehot_wide, slot_grads, precision=HIGHEST)

    grad_up_a, grad_up_b, grad_down_a, grad_down_b = ffn_grads
    sum_qkv_b, sum_out_a = lax.psum((stack_slots(grad_qkv_b), stack_slots(grad_out_a)), "dp")
    joint_sums = lax.psum(
        (
            stack_slots(grad_qkv_a),
            stack_slots(grad_out_b),
            stack_slots(grad_up_a),
            stack_slots(grad_up_b),
            stack_slots(grad_down_a),
            stack_slots(grad_down_b),
        ),
        ("dp", "tensor"),
    )
    sum_qkv_a, sum_out_b, sum_up_a, up_b_whole, down_a_whole, sum_down_b = joint_sums
    width_local = w_up.shape[1]
    first_col = lax.axis_index("tensor") * width_local
    sum_up_b = lax.dynamic_slice_in_dim(up_b_whole, first_col, width_local, 1)
    sum_down_a = lax.dynamic_slice_in_dim(down_a_whole, first_col, width_local, 2)
    return (
        layer_out,
        grad_tokens,
        sum_qkv_a,
        sum_qkv_b,
        sum_out_a,
        sum_out_b,
        sum_up_a,
        sum_up_b,
        sum_down_a,
        sum_down_b,
    )


F32 = jnp.float32
BF = jnp.bfloat16
LOG2E = 1.4426950408889634
PARTS = 8
PAD = 128
FLIP = [(0, 1), (1, 0)]
SWAP = [(1, 2), (2, 1)]


def dotg(a, b, ca, cb):
    return lax.dot_general(a, b, (((ca,), (cb,)), ((), ())), preferred_element_type=F32)


def pad_rows(table):
    rank, width = table.shape
    return jnp.concatenate([table, jnp.zeros((PAD - rank, width), table.dtype)], axis=0)


def pad_twice(table):
    rank, width = table.shape
    return jnp.concatenate([table, table, jnp.zeros((PAD - 2 * rank, width), table.dtype)], axis=0)


def two_terms(wide, rank):
    high = wide.astype(BF).astype(F32)
    return (high + pltpu.roll(wide - high, rank, 1)).astype(BF)


def three_terms(wide):
    high = wide.astype(BF)
    rest = wide - high.astype(F32)
    middle = rest.astype(BF)
    return high, middle, (rest - middle.astype(F32)).astype(BF)


def whole():
    return pl.BlockSpec(memory_space=pltpu.VMEM)


def in_place():
    return pl.BlockSpec(memory_space=pl.ANY)


def scalars():
    return pl.BlockSpec(memory_space=pltpu.SMEM)


def params(mib=58, **more):
    return pltpu.CompilerParams(vmem_limit_bytes=mib * 2**20, **more)


def cost(flops, nbytes):
    return pl.CostEstimate(flops=int(flops * 0.25), bytes_accessed=int(nbytes * 0.025), transcendentals=0)


def norm_stats(values):
    average = jnp.mean(values, axis=-1, keepdims=True)
    centred = values - average
    scale = lax.rsqrt(jnp.mean(centred * centred, axis=-1, keepdims=True) + epsilon)
    return centred * scale, scale


def norm_grad(unit, scale, grad):
    return scale * (
        grad
        - jnp.mean(grad, axis=-1, keepdims=True)
        - unit * jnp.mean(grad * unit, axis=-1, keepdims=True)
    )


def row_mask(scal, rows):
    at = lax.broadcasted_iota(jnp.int32, (rows, 1), 0) + scal[1] * rows
    return (at < scal[0]).astype(F32)


def choose(scal, here, swapped, target, sem):
    @pl.when(scal[3] != 0)
    def _():
        pltpu.make_async_copy(here, target, sem).start()

    @pl.when(scal[3] == 0)
    def _():
        pltpu.make_async_copy(swapped, target, sem).start()

    return pltpu.make_async_copy(here, target, sem)


def fetch(arrays, nears, target, sem, part_at, axis, size):
    copies = []
    parts = len(nears)
    for number, near in enumerate(nears):
        first = pl.multiple_of(((part_at % parts) ^ near) * size, size)
        place = target.at[:, pl.ds(first, size)] if axis == 1 else target.at[pl.ds(first, size)]
        copies.append(pltpu.make_async_copy(arrays[number // 2].at[number % 2], place, sem.at[near]))
    for copy in copies:
        copy.start()
    return copies


def qkv_local_kernel(scal, here, swapped, gain, w, qa, qb, tok, n1, rank, queries, rest, low, sem):
    step = pl.program_id(0)

    @pl.when(step == 0)
    def _():
        choose(scal, here, swapped, tok, sem.at[0]).wait()
        unit, _ = norm_stats(tok[...].astype(F32))
        normed = (unit * gain[...]).astype(BF)
        n1[...] = normed
        ranked = dotg(normed, pad_rows(qa[...]), 1, 1).astype(BF)
        rank[...] = ranked
        low[...] = ranked

    out = (dotg(n1[...], w[0], 1, 0) + dotg(low[...], pad_rows(qb[...]), 1, 0)).astype(BF)

    @pl.when(step < 2)
    def _():
        rest[0] = out

    @pl.when(step == 2)
    def _():
        queries[...] = out


def qkv_local(scal, tok, swapped, gain, w, qa, qb):
    rows, width = tok.shape
    third = w.shape[2]
    rank = qa.shape[0]
    fixed = lambda c: (0, 0)
    return pl.pallas_call(
        qkv_local_kernel,
        grid=(3,),
        in_specs=[
            scalars(),
            in_place(),
            in_place(),
            pl.BlockSpec((1, width), fixed),
            pl.BlockSpec((1, width, third), lambda c: ((c + 1) % 3, 0, 0)),
            pl.BlockSpec((rank, width), fixed),
            pl.BlockSpec((rank, third), lambda c: (0, (c + 1) % 3)),
        ],
        out_specs=[
            pl.BlockSpec((rows, width), fixed),
            pl.BlockSpec((rows, width), fixed),
            pl.BlockSpec((rows, PAD), fixed),
            pl.BlockSpec((rows, third), fixed),
            pl.BlockSpec((1, rows, third), lambda c: (jnp.minimum(c, 1), 0, 0)),
        ],
        out_shape=[
            jax.ShapeDtypeStruct((rows, width), BF),
            jax.ShapeDtypeStruct((rows, width), BF),
            jax.ShapeDtypeStruct((rows, PAD), BF),
            jax.ShapeDtypeStruct((rows, third), BF),
            jax.ShapeDtypeStruct((2, rows, third), BF),
        ],
        scratch_shapes=[pltpu.VMEM((rows, PAD), BF), pltpu.SemaphoreType.DMA((1,))],
        compiler_params=params(dimension_semantics=("arbitrary",)),
        cost_estimate=cost(7e-6 * 1e15, 8e6),
        name="qkv_local",
    )(scal, tok, swapped, gain, w, qa, qb)


def qkv_other_kernel(nears, scal, n1, rank, qb, *rest):
    arrays, (queries, out, w, sem) = rest[: len(nears) // 2], rest[len(nears) // 2 :]
    third = w.shape[2]
    copies = fetch(arrays, nears, w, sem, scal[2], 1, arrays[0].shape[2])
    for copy in copies:
        copy.wait()
    for c in (1, 2, 0):
        at = slice(c * third, (c + 1) * third)
        terms = (dotg(n1[...], w[c], 1, 0) + dotg(rank[...], pad_rows(qb[:, at]), 1, 0)).astype(BF)
        if c == 0:
            queries[...] = terms
        else:
            out[c - 1] = terms


def qkv_other(scal, n1, rank, qb, half):
    rows, width = n1.shape
    arrays, nears = half.pairs, half.names
    third = arrays[0].shape[3]
    return pl.pallas_call(
        functools.partial(qkv_other_kernel, nears),
        in_specs=[scalars(), whole(), whole(), whole()] + [in_place()] * len(arrays),
        out_specs=[whole()] * 3,
        out_shape=[
            jax.ShapeDtypeStruct((rows, third), BF),
            jax.ShapeDtypeStruct((2, rows, third), BF),
            jax.ShapeDtypeStruct((3, width, third), BF),
        ],
        scratch_shapes=[pltpu.SemaphoreType.DMA((PARTS,))],
        compiler_params=params(),
        cost_estimate=cost(7e-6 * 1e15, 10e6),
        name="qkv_other",
    )(scal, n1, rank, qb, *arrays)


def lane_numbers(rows):
    return lax.broadcasted_iota(jnp.int32, (rows, 2 * HD), 1)


def key_fill(scal, rows, other, ones):
    side = 1 - scal[1] if other else scal[1]
    lanes = lane_numbers(rows) % HD
    at = lax.broadcasted_iota(jnp.int32, (rows, 2 * HD), 0) + side * rows
    bias = jnp.where(at < jnp.maximum(scal[0], 1), 0.0, masked_score)
    return jnp.where(lanes < ones, 1.0, jnp.where(lanes == ones, bias, 0.0)).astype(BF)


def lane_terms(wide, rows, with_one):
    lanes = lane_numbers(rows) % HD
    first, second, third = three_terms(wide)
    filled = jnp.where(lanes == 2, third, jnp.full_like(third, 0.0))
    if with_one:
        filled = jnp.where(lanes == 3, jnp.full_like(third, 1.0), filled)
    return jnp.where(lanes == 0, first, jnp.where(lanes == 1, second, filled))


def attend_kernel(scal, q_ref, k_ref, v_ref, ko_ref, vo_ref, out, log_out, qx, kx, vt):
    rows = q_ref.shape[0]
    queries = (q_ref[...].astype(F32) * HD**-0.5).astype(BF)
    lanes = lane_numbers(rows)
    low_half = lanes < HD
    ones = (lanes % HD == 0).astype(BF)
    fills = [key_fill(scal, rows, side == 1, 0) for side in range(2)]
    for head in range(2):
        own = low_half if head == 0 else ~low_half
        qx[head] = jnp.where(own, queries, ones)
        for side, ref in enumerate((k_ref, ko_ref)):
            kx[head, side * rows : (side + 1) * rows] = jnp.where(own, ref[0], fills[side])
    for side, ref in enumerate((v_ref, vo_ref)):
        at = slice(side * rows, (side + 1) * rows)
        turned = ref[0].T
        for head in range(2):
            vt[head, 0:HD, at] = turned[head * HD : (head + 1) * HD]
            vt[head, HD : HD + 16, at] = jnp.ones((16, rows), BF)

    def scores(head):
        return dotg(kx[head], qx[head], 1, 1)

    ahead = scores(0)
    mixed, logs = [], []
    for head in range(2):
        now = ahead
        if head == 0:
            ahead = scores(1)
        top = jnp.max(now, axis=0, keepdims=True)
        soft = jnp.exp(now - top).astype(BF)
        terms = dotg(vt[head], soft, 1, 0)
        total = terms[HD : HD + 1]
        mixed.append(terms[0:HD] / total)
        logs.append(jnp.broadcast_to(top + jnp.log(total), (HD, total.shape[1])))
    out[...] = jnp.concatenate(mixed, axis=0).T.astype(BF)
    log_out[...] = jnp.concatenate([logs[1], logs[0]], axis=0).T


def attend(scal, queries, own, other):
    _, rows, width = own.shape
    pairs = width // (2 * HD)
    take = lambda c: pl.BlockSpec((1, rows, 2 * HD), lambda p: (c, 0, p))
    flat = pl.BlockSpec((rows, 2 * HD), lambda p: (0, p))
    return pl.pallas_call(
        attend_kernel,
        grid=(pairs,),
        in_specs=[scalars(), flat, take(0), take(1), take(0), take(1)],
        out_specs=[flat, flat],
        out_shape=[jax.ShapeDtypeStruct((rows, width), BF), jax.ShapeDtypeStruct((rows, width), F32)],
        scratch_shapes=[
            pltpu.VMEM((2, rows, 2 * HD), BF),
            pltpu.VMEM((2, 2 * rows, 2 * HD), BF),
            pltpu.VMEM((2, HD + 16, 2 * rows), BF),
        ],
        compiler_params=params(dimension_semantics=("arbitrary",)),
        cost_estimate=cost(16e-6 * 1e15, 6e6),
        name="attend",
    )(scal, queries, own, own, other, other)


def attend_back_kernel(
    scal, q_ref, k_ref, v_ref, ko_ref, vo_ref, mixed_ref, grad_ref, log_ref, queries_out, own_out, other_out,
    qx, gx, qm, gm, kx, vx, kt,
):
    rows = q_ref.shape[0]
    queries, grad = q_ref[...], grad_ref[...]
    zero = jnp.zeros_like(queries)
    low_half = lane_numbers(rows) < HD
    scaled = (queries.astype(F32) * HD**-0.5).astype(BF)
    weighed = grad.astype(F32) * mixed_ref[...].astype(F32)
    high = weighed.astype(BF)
    pair = jnp.concatenate([high, (weighed - high.astype(F32)).astype(BF)], axis=1)
    down = lax.broadcasted_iota(jnp.int32, (4 * HD, 2 * HD), 0) // HD % 2
    across = lax.broadcasted_iota(jnp.int32, (4 * HD, 2 * HD), 1) // HD
    sums = dotg(pair, (down != across).astype(BF), 1, 0)
    query_fill = lane_terms(-log_ref[...], rows, True)
    grad_fill = lane_terms(-sums, rows, False)
    fills = [key_fill(scal, rows, side == 1, 3) for side in range(2)]
    value_fill = (lane_numbers(rows) % HD < 3).astype(BF)
    for head in range(2):
        own = low_half if head == 0 else ~low_half
        qx[head] = jnp.where(own, scaled, query_fill)
        gx[head] = jnp.where(own, grad, grad_fill)
        qm[head] = jnp.where(own, queries, zero)
        gm[head] = jnp.where(own, grad, zero)
        for side, (key_ref, value_ref) in enumerate(((k_ref, v_ref), (ko_ref, vo_ref))):
            at = slice(side * rows, (side + 1) * rows)
            kx[head, at] = jnp.where(own, key_ref[0], fills[side])
            vx[head, at] = jnp.where(own, value_ref[0], value_fill)
    for side, ref in enumerate((k_ref, ko_ref)):
        kt[:, side * rows : (side + 1) * rows] = ref[0].T
    steps = [(side, head) for side in range(2) for head in range(2)]

    def first(side, head):
        at = slice(side * rows, (side + 1) * rows)
        return dotg(kx[head, at], qx[head], 1, 1), dotg(vx[head, at], gx[head], 1, 1)

    ahead = first(*steps[0])
    grad_queries = [0.0, 0.0]
    kept = None
    for number, (side, head) in enumerate(steps):
        scores, grad_soft = ahead
        if number + 1 < len(steps):
            ahead = first(*steps[number + 1])
        soft = jnp.exp(scores)
        grad_scores = (soft * grad_soft).astype(BF)
        values = dotg(soft.astype(BF), gm[head], 1, 0)
        keys = dotg(grad_scores, qm[head], 1, 0)
        at = slice(side * rows, (side + 1) * rows)
        grad_queries[head] += dotg(kt[head * HD : (head + 1) * HD, at], grad_scores, 1, 0)
        if head == 0:
            kept = (keys, values)
        else:
            keys = ((kept[0] + keys) * HD**-0.5).astype(BF)
            values = (kept[1] + values).astype(BF)
            out = own_out if side == 0 else other_out
            out[0], out[1] = keys, values
    queries_out[...] = (jnp.concatenate(grad_queries, axis=0).T * HD**-0.5).astype(BF)


def attend_back(scal, queries, own, other, mixed, grad, logs, piece, pieces):
    _, rows, width = own.shape
    width = width // pieces
    pairs = width // (2 * HD)
    skip = piece * pairs
    take = lambda c: pl.BlockSpec((1, rows, 2 * HD), lambda p: (c, 0, p + skip))
    flat = pl.BlockSpec((rows, 2 * HD), lambda p: (0, p + skip))
    both = jax.ShapeDtypeStruct((2, rows, width), BF)
    return pl.pallas_call(
        attend_back_kernel,
        grid=(pairs,),
        in_specs=[scalars(), flat, take(0), take(1), take(0), take(1), flat, flat, flat],
        out_specs=[
            pl.BlockSpec((rows, 2 * HD), lambda p: (0, p)),
            pl.BlockSpec((2, rows, 2 * HD), lambda p: (0, 0, p)),
            pl.BlockSpec((2, rows, 2 * HD), lambda p: (0, 0, p)),
        ],
        out_shape=[jax.ShapeDtypeStruct((rows, width), BF), both, both],
        scratch_shapes=[pltpu.VMEM((2, rows, 2 * HD), BF)] * 4
        + [pltpu.VMEM((2, 2 * rows, 2 * HD), BF)] * 2
        + [pltpu.VMEM((2 * HD, 2 * rows), BF)],
        compiler_params=params(dimension_semantics=("arbitrary",)),
        cost_estimate=cost(26e-6 / pieces * 1e15, 9e6),
        name="attend_back",
    )(scal, queries, own, own, other, other, mixed, grad, logs)


def branch_kernel(nears, scal, mix_a, mix_b, tok, w_a, oa_a, oa_b, obs, scale_one, gain_two, uas, *rest):
    arrays = rest[: len(nears) // 2]
    residual, n2, rank_out, rank_up, w_b, sem = rest[len(nears) // 2 :]
    rank = oa_a.shape[0]
    ob, ua = obs[scal[4]], uas[scal[4]]

    @pl.when(pl.program_id(0) == 0)
    def _():
        for copy in fetch(arrays, nears, w_b, sem, scal[2], 0, arrays[0].shape[1]):
            copy.wait()

    ranked = dotg(mix_a[...], pad_rows(oa_a[...]), 1, 1) + dotg(mix_b[...], pad_rows(oa_b[...]), 1, 1)
    ranked = two_terms(ranked, rank)
    rank_out[...] = ranked
    terms = dotg(mix_a[...], w_a[...], 1, 0) + dotg(mix_b[...], w_b[...], 1, 0)
    terms = terms + dotg(ranked, pad_twice(ob), 1, 0)
    total = tok[...].astype(F32) + scale_one[...] * terms
    residual[...] = total.astype(BF)
    unit, _ = norm_stats(total)
    normed = (unit * gain_two[...]).astype(BF)
    n2[...] = normed
    rank_up[...] = dotg(normed, pad_rows(ua), 1, 1).astype(BF)


def blocked(rows, width):
    return pl.BlockSpec((rows, width), lambda step: (step, 0))


def fixed_block(*shape):
    return pl.BlockSpec(shape, lambda step: (0,) * len(shape))


def branch(scal, mix_a, mix_b, tok, w_a, half, oa_a, oa_b, ob, scale_one, gain_two, ua):
    rows, width = tok.shape
    heads = mix_a.shape[1]
    block = rows // 2
    arrays, nears = half.pairs, half.names
    return pl.pallas_call(
        functools.partial(branch_kernel, nears),
        grid=(2,),
        in_specs=[scalars(), blocked(block, heads), blocked(block, heads), blocked(block, width)]
        + [fixed_block(*array.shape) for array in (w_a, oa_a, oa_b, ob, scale_one, gain_two, ua)]
        + [in_place()] * len(arrays),
        out_specs=[blocked(block, width), blocked(block, width), blocked(block, PAD), blocked(block, PAD)]
        + [fixed_block(*w_a.shape)],
        out_shape=[
            jax.ShapeDtypeStruct((rows, width), BF),
            jax.ShapeDtypeStruct((rows, width), BF),
            jax.ShapeDtypeStruct((rows, PAD), BF),
            jax.ShapeDtypeStruct((rows, PAD), BF),
            jax.ShapeDtypeStruct(w_a.shape, BF),
        ],
        scratch_shapes=[pltpu.SemaphoreType.DMA((PARTS,))],
        compiler_params=params(dimension_semantics=("arbitrary",)),
        cost_estimate=cost(8e-6 * 1e15, 16e6),
        name="branch",
    )(scal, mix_a, mix_b, tok, w_a, oa_a, oa_b, ob, scale_one, gain_two, ua, *arrays)


def mlp_kernel(nears, step, more, *refs):
    scal, n2, rank_up, ub, da = refs[:5]
    count = 1 if nears is None else len(nears)
    ups, downs = refs[5 : 5 + count], refs[5 + count : 5 + 2 * count]
    rest = refs[5 + 2 * count :]
    if nears is None:
        cot, scale_two, dbs, grad_mlp, grad_rank = rest[:5]
        earlier, rest = (), rest[5:]
        ub, da, db = (table.at[scal[4]] for table in (ub, da, dbs))
    else:
        grad_mlp, grad_rank = rest[:2]
        earlier, rest = rest[2 : 2 + more], rest[2 + more :]
    m_out, g_out, rd_out, gru_out, gub_out, gda_out = rest[:6]
    wu, wd, ubs, das, hidden, grad_pre, sem = rest[6:]
    width = wu.shape[1]
    rank = ub.shape[0]
    size = ub.shape[1] // PARTS
    pieces = width // size
    chunks = width // step
    waits = [[] for _ in range(chunks)]
    for piece in range(pieces):
        at = pl.ds(piece * size, size)
        if nears is None:
            sources = ups[0].at[:, at], downs[0].at[at]
        else:
            sources = ups[piece], downs[piece]
        for which, (source, target) in enumerate(zip(sources, (wu.at[:, at], wd.at[at]))):
            copy = pltpu.make_async_copy(source, target, sem.at[which, piece])
            copy.start()
            waits[piece * size // step].append(copy)
    def place(piece):
        if nears is None:
            return pl.ds(piece * size, size)
        return pl.ds(pl.multiple_of((scal[2] ^ nears[piece]) * size, size), size)

    if nears is None:
        grad_low = (scale_two[...] * (cot[...].astype(F32) * row_mask(scal, cot.shape[0]))).astype(BF)
        grad_mlp[...] = grad_low
        grad_rank[...] = dotg(grad_low, pad_rows(db[...]), 1, 1).astype(BF)
    if more == 6:
        gub_out[...], gda_out[...] = earlier[4][...], earlier[5][...]
    ubs[...] = jnp.zeros_like(ubs)
    das[...] = jnp.zeros_like(das)
    for piece in range(pieces):
        at = slice(piece * size, (piece + 1) * size)
        ubs[0:rank, at] = ub[:, place(piece)]
        das[0:rank, at] = da[:, place(piece)]
    up_turned = rank_up[...].T[0:rank]
    grad_turned = grad_rank[...].T[0:rank]

    def first(k):
        for copy in waits[k]:
            copy.wait()
        at = slice(k * step, (k + 1) * step)
        return (
            dotg(n2[...], wu[:, at], 1, 0) + dotg(rank_up[...], ubs[:, at], 1, 0),
            dotg(grad_mlp[...], wd[at, :], 1, 1) + dotg(grad_rank[...], das[:, at], 1, 0),
        )

    ahead = first(0)
    for k in range(chunks):
        at = slice(k * step, (k + 1) * step)
        preact, grad_hidden = ahead
        if k + 1 < chunks:
            ahead = first(k + 1)
        cdf = 0.5 * (1.0 + lax.erf(preact * 0.7071067811865476))
        hidden[:, at] = (preact * cdf).astype(BF)
        slope = cdf + preact * jnp.exp(-0.5 * preact * preact) * 0.3989422804014327
        grad_pre[:, at] = (grad_hidden * slope).astype(BF)
    ranked = dotg(hidden[...], das[...], 1, 1)
    grad_ranked = dotg(grad_pre[...], ubs[...], 1, 1)
    if more:
        ranked, grad_ranked = ranked + earlier[2][...], grad_ranked + earlier[3][...]
    rd_out[...] = ranked
    gru_out[...] = grad_ranked
    for piece in range(pieces):
        at = slice(piece * size, (piece + 1) * size)
        gub_out[:, place(piece)] = dotg(up_turned, grad_pre[:, at], 1, 0)
        gda_out[:, place(piece)] = dotg(grad_turned, hidden[:, at], 1, 0)
    for at in (slice(k, k + step) for k in range(0, wu.shape[0], step)):
        terms = dotg(hidden[...], wd[:, at], 1, 0)
        grad_terms = dotg(grad_pre[...], wu[at, :], 1, 1)
        if more:
            terms = terms + earlier[0][:, at].astype(F32)
            grad_terms = grad_terms + earlier[1][:, at].astype(F32)
        m_out[:, at] = terms.astype(BF)
        g_out[:, at] = grad_terms.astype(BF)


def mlp(scal, n2, rank_up, ub, da, ups, downs, grads, nears=None, earlier=()):
    rows, width = n2.shape
    rank, half = ub.shape[-2:]
    units = half if nears is None else len(nears) * half // PARTS
    step = min(512, units)
    sums = jax.ShapeDtypeStruct((rows, width), BF)
    ranked = jax.ShapeDtypeStruct((rows, PAD), F32)
    table = jax.ShapeDtypeStruct((rank, half), F32)
    low = jax.ShapeDtypeStruct((rows, width), BF)
    first = [low, jax.ShapeDtypeStruct((rows, PAD), BF)] if nears is None else []
    return pl.pallas_call(
        functools.partial(mlp_kernel, nears, step, len(earlier)),
        in_specs=[scalars()]
        + [whole()] * 4
        + [in_place()] * (2 * len(ups))
        + [whole()] * (len(grads) + len(earlier)),
        out_specs=[whole()] * (len(first) + 6),
        out_shape=first + [sums, sums, ranked, ranked, table, table],
        scratch_shapes=[
            pltpu.VMEM((width, units), BF),
            pltpu.VMEM((units, width), BF),
            pltpu.VMEM((PAD, units), BF),
            pltpu.VMEM((PAD, units), BF),
            pltpu.VMEM((rows, units), BF),
            pltpu.VMEM((rows, units), BF),
            pltpu.SemaphoreType.DMA((2, PARTS)),
        ],
        compiler_params=params(),
        cost_estimate=cost(25e-6 * units / half * 1e15, 20e6),
        name="mlp",
    )(scal, n2, rank_up, ub, da, *ups, *downs, *grads, *earlier)


def mlp_other(scal, n2, rank_up, ub, da, up, down, grads, earlier):
    for odd in range(2):
        ups, nears = up.held(odd)
        downs, same = down.held(odd)
        assert nears == same
        earlier = mlp(scal, n2, rank_up, ub, da, ups, downs, grads, nears, tuple(earlier))
    return earlier


def middle_kernel(
    scal, residual, m_in, g_in, rd, gru, cot, mix_a, mix_b, rank_out, n2, grad_mlp,
    dbs, uas, scale_two, gain_two, scale_one, w_a, w_b, oa_a, oa_b, obs,
    layer, grad_res, grad_a, grad_b, goa_a, goa_b, gob, gua, gdb,
):
    step = pl.program_id(0)
    rows = residual.shape[0]
    db, ua, ob = dbs[scal[4]], uas[scal[4]], obs[scal[4]]
    rank = db.shape[0]
    at = lax.broadcasted_iota(jnp.int32, (rows, 1), 0) + (scal[1] * pl.num_programs(0) + step) * rows
    valid = (at < scal[0]).astype(F32)
    down = two_terms(rd[...], rank)
    up = two_terms(gru[...], rank)

    def add(out, terms):
        @pl.when(step == 0)
        def _():
            out[...] = terms

        @pl.when(step > 0)
        def _():
            out[...] += terms

    def turned(terms, right):
        both = dotg(terms.T[0 : 2 * rank], right, 1, 0)
        return both[0:rank] + both[rank : 2 * rank]

    branch_out = m_in[...].astype(F32) + dotg(down, pad_twice(db), 1, 0)
    total = residual[...].astype(F32)
    layer[...] = ((total + scale_two[...] * branch_out) * valid).astype(BF)
    add(gua, turned(up, n2[...]))
    add(gdb, turned(down, grad_mlp[...]))
    unit, scale = norm_stats(total)
    grad_normed = (g_in[...].astype(F32) + dotg(up, pad_twice(ua), 1, 0)) * gain_two[...]
    grad_total = cot[...].astype(F32) * valid + norm_grad(unit, scale, grad_normed)
    grad_res[...] = grad_total.astype(BF)
    grad_attn = (scale_one[...] * grad_total).astype(BF)
    grad_rank = dotg(grad_attn, pad_rows(ob), 1, 1).astype(BF)
    grad_a[...] = (
        dotg(grad_attn, w_a[...], 1, 1) + dotg(grad_rank, pad_rows(oa_a[...]), 1, 0)
    ).astype(BF)
    grad_b[...] = (
        dotg(grad_attn, w_b[...], 1, 1) + dotg(grad_rank, pad_rows(oa_b[...]), 1, 0)
    ).astype(BF)
    rank_turned = grad_rank.T[0:rank]
    add(goa_a, dotg(rank_turned, mix_a[...], 1, 0))
    add(goa_b, dotg(rank_turned, mix_b[...], 1, 0))
    add(gob, turned(rank_out[...], grad_attn))


def middle(scal, by_rows, others, blocks=1):
    rows, width = by_rows[0].shape
    block = rows // blocks
    heads = by_rows[6].shape[1]
    rank = others[0].shape[1]
    part = jax.ShapeDtypeStruct((rows, heads), BF)
    table = jax.ShapeDtypeStruct((rank, width), F32)
    half_table = jax.ShapeDtypeStruct((rank, heads), F32)
    return pl.pallas_call(
        middle_kernel,
        grid=(blocks,),
        in_specs=[scalars()]
        + [blocked(block, array.shape[1]) for array in by_rows]
        + [fixed_block(*array.shape) for array in others],
        out_specs=[blocked(block, width), blocked(block, width), blocked(block, heads), blocked(block, heads)]
        + [fixed_block(*shape) for shape in ((rank, heads),) * 2 + ((rank, width),) * 3],
        out_shape=[jax.ShapeDtypeStruct((rows, width), BF)] * 2
        + [part, part, half_table, half_table, table, table, table],
        compiler_params=params(dimension_semantics=("arbitrary",)),
        cost_estimate=cost(9e-6 * 1e15, 20e6),
        name="middle",
    )(scal, *by_rows, *others)


def columns_of(pieces):
    first = 0
    for piece in pieces:
        yield piece, slice(first, first + piece.shape[-1])
        first += piece.shape[-1]


def qkv_tables_kernel(count, *refs):
    sides, refs = (refs[: 3 * count], refs[3 * count : 6 * count]), refs[6 * count :]
    scal, qb_a, qb_b, n1, rank_in, total_a, total_b, rank_out, kept, sent, gqb_a, gqb_b, gqa = refs
    rank = qb_a.shape[0]
    third = qb_a.shape[1] // 3
    rank_turned = rank_in[...].T[0:rank]
    ranked = None
    for side, qb, total, table in zip(sides, (qb_a, qb_b), (total_a, total_b), (gqb_a, gqb_b)):
        queries, owns, gots = side[:count], side[count : 2 * count], side[2 * count :]
        for (piece, at), own, got in zip(columns_of(queries), owns, gots):
            for c in range(3):
                if c == 0:
                    grad = piece[...]
                else:
                    grad = (own[c - 1].astype(F32) + got[c - 1].astype(F32)).astype(BF)
                    total[c - 1, :, at] = grad
                place = slice(c * third + at.start, c * third + at.stop)
                table[:, place] = dotg(rank_turned, grad, 1, 0)
                terms = dotg(grad, pad_rows(qb[:, place]), 1, 1)
                ranked = terms if ranked is None else ranked + terms
    ranked = two_terms(ranked, rank)
    rank_out[...] = ranked
    both = dotg(ranked.T[0 : 2 * rank], n1[...], 1, 0)
    gqa[...] = both[0:rank] + both[rank : 2 * rank]
    first = 0
    for table in (gqb_a, gqa, gqb_b):
        half = table.shape[1] // 2
        at = slice(first, first + half)
        kept[:, at] = table[:, pl.ds(pl.multiple_of(scal[1] * half, half), half)]
        sent[:, at] = table[:, pl.ds(pl.multiple_of((1 - scal[1]) * half, half), half)].astype(BF)
        first += half


def qkv_tables(scal, side_a, side_b, qb_a, qb_b, n1, rank_in):
    rows, width = n1.shape
    rank, columns = qb_a.shape
    count = len(side_a) // 3
    total = jax.ShapeDtypeStruct((2, rows, columns // 3), BF)
    share = columns + width // 2
    return pl.pallas_call(
        functools.partial(qkv_tables_kernel, count),
        in_specs=[whole()] * (6 * count) + [scalars()] + [whole()] * 4,
        out_specs=[whole()] * 5,
        out_shape=[total, total, jax.ShapeDtypeStruct((rows, PAD), BF)]
        + [jax.ShapeDtypeStruct((rank, share), F32), jax.ShapeDtypeStruct((rank, share), BF)],
        scratch_shapes=[pltpu.VMEM((rank, columns), F32)] * 2 + [pltpu.VMEM((rank, width), F32)],
        compiler_params=params(),
        cost_estimate=cost(7e-6 * 1e15, 14e6),
        name="qkv_tables",
    )(*side_a, *side_b, scal, qb_a, qb_b, n1, rank_in)


def qkv_rows_kernel(count, *refs):
    grads_a, grads_b, refs = refs[: count + 1], refs[count + 1 : 2 * count + 2], refs[2 * count + 2 :]
    w_a, w_b, ranked, qa, tok, gain, grad_res, out = refs
    grad = dotg(ranked[...], pad_twice(qa[...]), 1, 0)
    for grads, w in ((grads_a, w_a), (grads_b, w_b)):
        for piece, at in columns_of(grads[:count]):
            grad = grad + dotg(piece[...], w[0, :, at], 1, 1)
        for c in (1, 2):
            grad = grad + dotg(grads[count][c - 1], w[c], 1, 1)
    unit, scale = norm_stats(tok[...].astype(F32))
    out[...] = (grad_res[...].astype(F32) + norm_grad(unit, scale, grad * gain[...])).astype(BF)


def qkv_rows(block_at, blocks, grads_a, grads_b, w_a, w_b, ranked, qa, tok, gain, grad_res):
    rows, width = tok.shape
    block = rows // blocks
    flat = lambda array: pl.BlockSpec((block, array.shape[1]), lambda step: (block_at, 0))
    deep = lambda array: pl.BlockSpec((2, block, array.shape[2]), lambda step: (0, block_at, 0))
    specs = [flat(array) if array.ndim == 2 else deep(array) for array in grads_a + grads_b]
    return pl.pallas_call(
        functools.partial(qkv_rows_kernel, len(grads_a) - 1),
        grid=(1,),
        in_specs=specs
        + [whole(), whole(), flat(ranked), whole(), flat(tok), whole(), flat(grad_res)],
        out_specs=whole(),
        out_shape=jax.ShapeDtypeStruct((block, width), BF),
        compiler_params=params(),
        cost_estimate=cost(12e-6 / blocks * 1e15, 16e6 / blocks),
        name="qkv_rows",
    )(*grads_a, *grads_b, w_a, w_b, ranked, qa, tok, gain, grad_res)


def gather_kernel(has_ids, flag, *refs):
    ids, (own, got, out, ids_out, total) = refs[0], refs[has_ids:]
    columns = out.shape[2]
    half = own.shape[0]
    total[...] = jnp.zeros_like(total)

    def add(first, images):
        for image in range(half):
            if has_ids:
                adapter = ids[first + image]
            else:
                note = images[image, 0:8, columns : columns + PAD].astype(F32)
                adapter = jnp.max(note).astype(jnp.int32)
            ids_out[first + image] = adapter
            total[adapter] += images[image, :, 0:columns].astype(F32)

    @pl.when(flag[0] == 0)
    def _():
        add(0, own)
        add(half, got)

    @pl.when(flag[0] != 0)
    def _():
        add(0, got)
        add(half, own)

    out[...] = total[...].astype(BF)


def gather_images(flag, ids, pair, adapters, columns):
    count, rank, _ = pair[0].shape
    given = [] if ids is None else [ids]
    return pl.pallas_call(
        functools.partial(gather_kernel, len(given)),
        in_specs=[scalars()] * (1 + len(given)) + [whole()] * 2,
        out_specs=[whole(), scalars()],
        out_shape=[
            jax.ShapeDtypeStruct((adapters, rank, columns), BF),
            jax.ShapeDtypeStruct((2 * count,), jnp.int32),
        ],
        scratch_shapes=[pltpu.VMEM((adapters, rank, columns), F32)],
        compiler_params=params(),
        cost_estimate=cost(2e-6 * 1e15, 1e6),
        name="gather_images",
    )(flag.astype(jnp.int32)[None], *given, *pair)


def finish_kernel(cut, spans, places, core, own, other, *outs):
    def write(low, high):
        for (shared, start, stop), (number, index) in zip(spans, places):
            first = cut if shared else 0
            half = own.shape[2] - cut if shared else cut
            out = outs[number] if index is None else outs[number].at[:, index]
            middle = min(max(half - start, 0), stop - start)
            if middle > 0:
                out[:, :, 0:middle] = low[:, :, first + start : first + start + middle].astype(F32)
            if middle < stop - start:
                begin = first + start + middle - half
                out[:, :, middle : stop - start] = high[:, :, begin : first + stop - half].astype(F32)

    @pl.when(core[0] == 0)
    def _():
        write(own, other)

    @pl.when(core[0] != 0)
    def _():
        write(other, own)


def finish(core, cut, spans, places, own, other, shapes):
    return pl.pallas_call(
        functools.partial(finish_kernel, cut, spans, places),
        in_specs=[scalars(), whole(), whole()],
        out_specs=[whole()] * len(shapes),
        out_shape=[jax.ShapeDtypeStruct(shape, F32) for shape in shapes],
        compiler_params=params(),
        cost_estimate=cost(2e-6 * 1e15, 4e6),
        name="finish",
    )(core, own, other)


def swap(rows):
    return lax.ppermute(rows, ("core", "tensor"), SWAP)


def flip(axis):
    return lambda array: lax.ppermute(array, axis, FLIP)


def after(value, *others):
    return lax.optimization_barrier((value, others))[0]


class OtherHalf:
    BITS = {"core": 1, "x": 2, "zb": 4}

    def __init__(self, local, axis, part_at, count):
        size = local.shape[axis] // count
        self.mine = lax.dynamic_slice_in_dim(local, (part_at % count) * size, size, axis)
        self.parts = {}
        self.nears = tuple(range(0, count, 2))

    def over_tensor(self, *others):
        self.parts[0] = flip("tensor")(after(self.mine, *others) if others else self.mine)

    def hop(self, near, axis, *others):
        part = after(self.parts[near], *others) if others else self.parts[near]
        self.parts[near ^ self.BITS[axis]] = flip(axis)(part)

    def last_hop(self):
        over_zb, over_x = jnp.split(self.parts[2], 2, axis=1)[0], jnp.split(self.parts[4], 2, axis=1)[1]
        self.parts[6] = jnp.concatenate([flip("zb")(over_zb), flip("x")(over_x)], axis=1)

    def pairs_over_cores(self, *others):
        parts = after(self.parts, *others) if others else self.parts
        even = [jnp.stack([parts[a], parts[b]]) for a, b in zip(self.nears[::2], self.nears[1::2])]
        self.pairs = even + [flip("core")(array) for array in even]
        self.names = self.nears + tuple(near + 1 for near in self.nears)

    def held(self, odd):
        names = tuple(near + odd for near in self.nears)
        return [self.parts[near] for near in names], names


def half_columns(array, index):
    size = array.shape[1] // 2
    return lax.dynamic_slice_in_dim(array, index * size, size, 1)


def by_index(index, own, other, axis):
    return jnp.where(
        index == 0, jnp.concatenate([own, other], axis=axis), jnp.concatenate([other, own], axis=axis)
    )


class Sum:
    def __init__(self, kept, sent, cut, adapter, core, tensor):
        self.core, self.tensor, self.adapter = core, tensor, adapter
        self.kept, self.sent, self.cut = kept, sent, cut

    @staticmethod
    def shares(near, shared, far, core):
        def share(index):
            return jnp.concatenate([half_columns(array, index) for array in (near, shared, far)], axis=1)

        return share(core), share(1 - core).astype(BF)

    def over_cores(self):
        total = (self.kept + flip("core")(self.sent).astype(F32)).astype(BF)
        cut, columns = self.cut, total.shape[1] - self.cut
        note = []
        if self.adapter is not None:
            note = [jnp.broadcast_to(self.adapter.astype(BF), (total.shape[0], PAD))]
        self.mine = jnp.concatenate([total[:, :columns]] + note, axis=1)
        self.send = jnp.concatenate([total[:, columns:], total[:, cut:columns]] + note, axis=1)
        self.columns = columns

    def start_pair(self):
        self.flag, self.pair = self.tensor, (self.mine[None], flip("tensor")(self.send)[None])

    def start(self, name):
        self.images = by_index(self.flag, *self.pair, 0)
        if lax.axis_size(name) == 2:
            self.flag, self.pair = lax.axis_index(name), (self.images, flip(name)(self.images))
        else:
            images = lax.all_gather(self.images, name, axis=0, tiled=True)
            half = images.shape[0] // 2
            self.flag, self.pair = jnp.zeros((), jnp.int32), (images[:half], images[half:])

    def arrive(self, *others):
        self.pair = (self.pair[0], after(self.pair[1], *others))

    def over_adapters(self, ids, adapters):
        self.dense, ids = gather_images(self.flag, ids, self.pair, adapters, self.columns)
        self.other = flip("core")(self.dense)
        return ids

    def finish(self, spans, places, shapes):
        core = self.core.astype(jnp.int32)[None]
        return finish(core, self.cut, spans, places, self.dense, self.other, shapes)


def quad_body(
    tokens, cotangent, lengths, adapter_ids, gain_one, gain_two, scale_one, scale_two, w_qkv, w_out, w_up, w_down,
    qkv_a, qkv_b, out_a, out_b, up_a, up_b, down_a, down_b,
):
    core, tensor = lax.axis_index("core"), lax.axis_index("tensor")
    part_at = lax.axis_index("zb") * 4 + lax.axis_index("x") * 2 + core
    adapters, rank, width = qkv_a.shape
    third = w_qkv.shape[2]
    units = w_up.shape[1]

    w3 = jnp.swapaxes(w_qkv, 0, 1)
    half_qkv = OtherHalf(w3, 1, part_at, PARTS)
    half_out = OtherHalf(w_out, 0, part_at, 4)
    half_up = OtherHalf(w_up, 1, part_at, PARTS)
    half_down = OtherHalf(w_down, 0, part_at, PARTS)
    half_qkv.over_tensor()
    tok_here = tokens[0]
    tok_swapped = swap(tok_here)
    facts = jnp.stack([lengths[0], adapter_ids[0]])
    facts_other = flip("core")(facts)
    mine = jnp.where(core == tensor, facts, facts_other)
    theirs = jnp.where(core == tensor, facts_other, facts)
    length, adapter, adapter_other = mine[0], mine[1], theirs[1]
    scal = jnp.stack([length, core, part_at, core == tensor, adapter]).astype(jnp.int32)

    qkv_b, out_b, up_b, down_b = (jnp.swapaxes(table, -1, -2) for table in (qkv_b, out_b, up_b, down_b))
    pick = lambda table, index: lax.dynamic_index_in_dim(table, index, 0, False)
    flat = lambda table: jnp.swapaxes(table, 0, 1).reshape(rank, 3 * third)
    half_qkv.hop(0, "x")
    half_qkv.hop(0, "zb")
    adapter, adapter_other = after((adapter, adapter_other), half_qkv.parts[2])
    packed_first = jnp.concatenate([flat(pick(qkv_b, adapter_other)), pick(out_a, adapter_other)], axis=1)
    packed = jnp.concatenate([pick(table, adapter_other) for table in (up_b, down_a)], axis=1)
    qa, oa = pick(qkv_a, adapter), pick(out_a, adapter)
    qb = flat(pick(qkv_b, adapter))
    gain_one, gain_two, scale_one, scale_two = (v.reshape(1, width) for v in (gain_one, gain_two, scale_one, scale_two))

    qb_other, oa_other = jnp.split(flip("tensor")(packed_first), (3 * third,), axis=1)
    half_up.over_tensor(half_qkv.parts[4], qb_other)
    half_qkv.last_hop()
    tok_swapped = after(tok_swapped, half_qkv.parts[2], half_qkv.parts[4], qb_other, scal)
    tok, n1, rank_qkv, q_a, own_a = qkv_local(scal, tok_here, tok_swapped, gain_one, w3, qa, qb)
    half_qkv.pairs_over_cores()
    kv_a = flip("core")(own_a)
    q_b, own_b, w3_other = qkv_other(scal, after(n1, half_up.parts[0]), rank_qkv, qb_other, half_qkv)
    kv_b = flip("core")(own_b)
    half_out.over_tensor(own_b)
    half_up.hop(0, "x", own_b)
    half_up.hop(0, "zb", own_b)
    cot_swapped = swap(after(cotangent[0], own_b))
    mix_a, logs_a = attend(scal, after(q_a, own_b), own_a, kv_a)
    half_out.hop(0, "x", mix_a)
    half_up.hop(4, "x", mix_a)
    half_down.over_tensor(mix_a)
    mix_b, logs_b = attend(scal, after(q_b, mix_a, half_up.parts[2], half_up.parts[4]), own_b, kv_b)
    half_out.pairs_over_cores(mix_b)
    half_down.hop(0, "x", mix_b)
    half_down.hop(0, "zb", mix_b)
    residual, n2, rank_out, rank_up, out_other = branch(
        scal, after(mix_a, half_up.parts[6], half_down.parts[0]), mix_b, tok, w_out, half_out, oa, oa_other, out_b, scale_one, gain_two, up_a
    )
    half_down.hop(2, "zb", n2)
    ub_other, da_other = jnp.split(flip("tensor")(after(packed, n2)), 2, axis=1)
    for near in (0, 2, 4):
        half_up.hop(near, "core", n2)
    cot = jnp.where(core == tensor, cotangent[0], cot_swapped)
    grad_mlp, grad_rank, m, g, rd, gru, gub_a, gda_a = mlp(
        scal, after(n2, half_down.parts[2], half_down.parts[4]), rank_up, up_b, down_a, [w_up], [w_down],
        [cot, scale_two, down_b],
    )
    half_up.hop(6, "core", m)
    for near in (0, 2, 4, 6):
        half_down.hop(near, "core", m)
    m, g, rd, gru, gub_b, gda_b = mlp_other(
        scal, n2, rank_up, ub_other, da_other, half_up, half_down, [grad_mlp, grad_rank], (m, g, rd, gru)
    )
    layer, grad_res, grad_a, grad_b, goa_a, goa_b, gob, gua, gdb = middle(
        scal,
        (residual, m, g, rd, gru, cot, mix_a, mix_b, rank_out, n2, grad_mlp),
        (down_b, up_a, scale_two, gain_two, scale_one, w_out, out_other, oa, oa_other, out_b),
    )
    shares = Sum.shares(
        jnp.concatenate([goa_a, gub_a, gda_a], axis=1),
        jnp.concatenate([gob, gua, gdb], axis=1),
        jnp.concatenate([goa_b, gub_b, gda_b], axis=1),
        core,
    )
    early = Sum(*shares, third // 2 + units, adapter, core, tensor)
    early.over_cores()

    def back(queries, own, kv, mixed, grad, logs, piece, *others):
        queries = after(queries, *others) if others else queries
        grad_queries, kept, sent = attend_back(scal, queries, own, kv, mixed, grad, logs, piece, 2)
        return grad_queries, kept, flip("core")(sent)

    side_a = (q_a, own_a, kv_a, mix_a, grad_a, logs_a)
    side_b = (q_b, own_b, kv_b, mix_b, grad_b, logs_b)
    early.start_pair()
    back_1 = back(*side_a, 0, early.send)
    early.arrive(back_1[0])
    early.start("hi")
    back_2 = back(*side_a, 1, early.images)
    layer_swapped = swap(after(layer, back_1[0]))
    early.arrive(back_2[0])
    early.start("zb")
    back_3 = back(*side_b, 0, early.images)
    early.arrive(back_3[0])
    early.start("x")
    back_4 = back(*side_b, 1, early.images, layer_swapped)
    kv_sum_a, kv_sum_b, ranked, kept, sent = qkv_tables(
        scal,
        [part for pair in zip(back_1, back_2) for part in pair],
        [part for pair in zip(back_3, back_4) for part in pair],
        qb, qb_other, n1, rank_qkv,
    )
    late = Sum(kept, sent, 3 * third // 2, None, core, tensor)
    late.over_cores()
    late.start_pair()
    grads = (
        [back_1[0], back_2[0], kv_sum_a], [back_3[0], back_4[0], kv_sum_b],
        w3, w3_other, ranked, qa, tok, gain_one, grad_res,
    )
    upper = qkv_rows(0, 2, grads[0], grads[1], after(w3, late.send), *grads[3:])
    upper_swapped = swap(upper)
    late.arrive(upper)
    late.start("hi")
    lower = qkv_rows(1, 2, grads[0], grads[1], after(w3, late.images), *grads[3:])
    lower_swapped = swap(lower)
    late.arrive(lower, upper_swapped)
    late.start("zb")
    late.start("x")
    early.arrive(lower, late.images)
    ids = early.over_adapters(None, adapters)
    in_place_already = core == tensor
    grad_tokens = jnp.concatenate(
        [jnp.where(in_place_already, *rows) for rows in ((upper, upper_swapped), (lower, lower_swapped))], axis=0
    ).astype(F32)
    layer_out = jnp.where(in_place_already, layer, layer_swapped)
    late.over_adapters(ids, adapters)
    ends = (0, third, third + units, third + 2 * units)
    spans = [(False, ends[k], ends[k + 1]) for k in range(3)] + [(True, k * width, (k + 1) * width) for k in range(3)]
    widths = (third, units, units, width, width, width)
    sum_oa, sum_ub, sum_da, sum_ob, sum_ua, sum_db = early.finish(
        spans, [(k, None) for k in range(6)], [(adapters, rank, size) for size in widths]
    )
    sum_qb, sum_qa = late.finish(
        [(False, c * third, (c + 1) * third) for c in range(3)] + [(True, 0, width)],
        [(0, c) for c in range(3)] + [(1, None)],
        [(adapters, 3, rank, third), (adapters, rank, width)],
    )
    turn = lambda table: jnp.swapaxes(table, -1, -2)
    return (
        layer_out[None],
        grad_tokens[None],
        sum_qa,
        turn(sum_qb),
        sum_oa,
        turn(sum_ob),
        sum_ua,
        turn(sum_ub),
        sum_da,
        turn(sum_db),
    )


def solution(mesh):
    groups, split = mesh.shape["dp"], mesh.shape["tensor"]
    if split == 2 and groups % 8 == 0:
        mesh = Mesh(mesh.devices.reshape(groups // 8, 2, 2, 2, 2), ("hi", "zb", "x", "core", "tensor"))
        dp, body = ("hi", "zb", "x", "core"), quad_body
    else:
        dp, body = "dp", plain_body
    slots = P(dp, "tensor", None)
    in_specs = (
        slots, slots, P(dp), P(dp), P(), P(), P(), P(),
        P(None, None, "tensor"), P("tensor", None), P(None, "tensor"), P("tensor", None),
        P(), P(None, None, "tensor", None), P(None, None, "tensor"), P(),
        P(), P(None, "tensor", None), P(None, None, "tensor"), P(),
    )
    out_specs = (
        slots, slots, P(), P(None, None, "tensor", None), P(None, None, "tensor"), P(),
        P(), P(None, "tensor", None), P(None, None, "tensor"), P(),
    )
    return jax.shard_map(body, mesh=mesh, in_specs=in_specs, out_specs=out_specs, check_vma=False)
```

```python
import functools

import jax
import jax.numpy as jnp
from jax import lax
from jax.experimental import pallas as pl
from jax.experimental.pallas import tpu as pltpu
from jax.sharding import Mesh
from jax.sharding import PartitionSpec as P

HD = 64
ADAPTERS = 8


epsilon = 1e-06
masked_score = -1e30
HIGHEST = lax.Precision.HIGHEST


def product(form, left, right):
    return jnp.einsum(form, left, right, preferred_element_type=jnp.float32)


def precise(form, left, right):
    return jnp.einsum(form, left.astype(jnp.float32), right.astype(jnp.float32), precision=HIGHEST)


def select_rows(onehot, table):
    return product("sn,n...->s...", onehot, table).astype(table.dtype)


def norm_rows(values, gain_vec):
    average = jnp.mean(values, axis=-1, keepdims=True)
    centred = values - average
    variance = jnp.mean(centred * centred, axis=-1, keepdims=True)
    return centred * lax.rsqrt(variance + epsilon) * gain_vec


def norm_back(values, gain_vec, grad_normed):
    normed, pullback = jax.vjp(lambda rows: norm_rows(rows, gain_vec), values)
    return pullback(grad_normed)[0]


def gelu_slope(values):
    return (
        0.5 * (1.0 + lax.erf(values * 0.7071067811865476))
        + values * jnp.exp(-0.5 * values * values) * 0.3989422804014327
    )


def ffn_forward(rows_low, up_mat, down_mat, up_a_sel, up_b_sel, down_a_sel, down_b_sel):
    rank_up = product("std,srd->str", rows_low, up_a_sel).astype(jnp.bfloat16)
    preact = product("std,dh->sth", rows_low, up_mat) + product("str,shr->sth", rank_up, up_b_sel)
    hidden = jax.nn.gelu(preact, approximate=False).astype(jnp.bfloat16)
    rank_down = product("sth,srh->str", hidden, down_a_sel)
    terms = product("sth,hd->std", hidden, down_mat) + precise(
        "str,sdr->std", rank_down, down_b_sel
    )
    return (rank_up, preact, hidden, rank_down, terms)


def ffn_backward(
    rows_low,
    grad_rows,
    up_mat,
    down_mat,
    up_a_sel,
    up_b_sel,
    down_a_sel,
    down_b_sel,
    rank_up,
    preact,
    hidden,
    rank_down,
):
    grad_rank_down = product("std,sdr->str", grad_rows, down_b_sel).astype(jnp.bfloat16)
    grad_hidden = product("std,hd->sth", grad_rows, down_mat) + product(
        "str,srh->sth", grad_rank_down, down_a_sel
    )
    grad_preact = (grad_hidden * gelu_slope(preact)).astype(jnp.bfloat16)
    grad_up_b = product("sth,str->shr", grad_preact, rank_up)
    grad_rank_up = product("sth,shr->str", grad_preact, up_b_sel)
    grad_rows_in = product("sth,dh->std", grad_preact, up_mat) + precise(
        "str,srd->std", grad_rank_up, up_a_sel
    )
    grad_up_a = precise("str,std->srd", grad_rank_up, rows_low)
    grad_down_a = product("str,sth->srh", grad_rank_down, hidden)
    grad_down_b = precise("std,str->sdr", grad_rows, rank_down)
    return (grad_rows_in, (grad_up_a, grad_up_b, grad_down_a, grad_down_b))


def plain_body(
    tokens,
    cotangent,
    lengths,
    adapter_ids,
    gain_one,
    gain_two,
    scale_one,
    scale_two,
    w_qkv,
    w_out,
    w_up,
    w_down,
    qkv_a,
    qkv_b,
    out_a,
    out_b,
    up_a,
    up_b,
    down_a,
    down_b,
):
    shard_rows = tokens.shape[1]
    seq_len = shard_rows * lax.axis_size("tensor")
    heads_local = w_qkv.shape[2] // HD
    scale_attn = HD ** (-0.5)
    first_row = lax.axis_index("tensor") * shard_rows
    positions = jnp.arange(seq_len, dtype=jnp.int32)
    key_valid = positions[None, :] < jnp.maximum(lengths, 1)[:, None]
    local_rows = first_row + jnp.arange(shard_rows, dtype=jnp.int32)
    row_valid = (local_rows[None, :] < lengths[:, None]).astype(jnp.float32)[:, :, None]
    adapters = jnp.arange(ADAPTERS, dtype=jnp.int32)
    onehot = (adapter_ids[:, None] == adapters[None, :]).astype(jnp.bfloat16)
    qkv_a_sel = select_rows(onehot, qkv_a)
    qkv_b_sel = select_rows(onehot, qkv_b)
    out_a_sel = select_rows(onehot, out_a)
    out_b_sel = select_rows(onehot, out_b)
    up_a_sel = select_rows(onehot, up_a)
    down_b_sel = select_rows(onehot, down_b)
    inputs = tokens.astype(jnp.float32)
    normed_one = norm_rows(inputs, gain_one).astype(jnp.bfloat16)
    full_one = lax.all_gather(normed_one, "tensor", axis=1, tiled=True)
    rank_qkv = product("std,srd->str", full_one, qkv_a_sel).astype(jnp.bfloat16)
    projected = (
        product("std,dcf->sctf", full_one, w_qkv) + product("str,scfr->sctf", rank_qkv, qkv_b_sel)
    ).astype(jnp.bfloat16)

    def split_heads(rows):
        return rows.reshape(seq_len, heads_local, HD)

    def masked_scores(queries, keyrows, valid_keys):
        scores = product("qhe,khe->hqk", queries, keyrows) * scale_attn
        return jnp.where(valid_keys[None, None, :], scores, masked_score)

    def attend(slot_items):
        slot_block, valid_keys = slot_items
        queries = split_heads(slot_block[0])
        keyrows = split_heads(slot_block[1])
        values = split_heads(slot_block[2])
        scores = masked_scores(queries, keyrows, valid_keys)
        row_max = jnp.max(scores, axis=-1, keepdims=True)
        exponent = jnp.exp(scores - row_max)
        row_total = jnp.sum(exponent, axis=-1, keepdims=True)
        soft_low = (exponent / row_total).astype(jnp.bfloat16)
        mixed_rows = (
            product("hqk,khe->qhe", soft_low, values).astype(jnp.bfloat16).reshape(seq_len, -1)
        )
        return (mixed_rows, (row_max + jnp.log(row_total))[:, :, 0])

    mixed, log_total = lax.map(attend, (projected, key_valid))
    rank_out = product("stf,srf->str", mixed, out_a_sel)
    attn_terms = product("stf,fd->std", mixed, w_out) + precise("str,sdr->std", rank_out, out_b_sel)
    attn_branch = lax.psum_scatter(attn_terms, "tensor", scatter_dimension=1, tiled=True)
    residual = inputs + scale_one * attn_branch
    normed_two = norm_rows(residual, gain_two).astype(jnp.bfloat16)
    up_mat, down_mat, up_b_all, down_a_all = (
        lax.all_gather(w_up, "tensor", axis=1, tiled=True),
        lax.all_gather(w_down, "tensor", axis=0, tiled=True),
        lax.all_gather(up_b, "tensor", axis=1, tiled=True),
        lax.all_gather(down_a, "tensor", axis=2, tiled=True),
    )
    up_b_sel = select_rows(onehot, up_b_all)
    down_a_sel = select_rows(onehot, down_a_all)
    rank_up, preact, hidden, rank_down, ffn_terms = ffn_forward(
        normed_two, up_mat, down_mat, up_a_sel, up_b_sel, down_a_sel, down_b_sel
    )
    layer_out = ((residual + scale_two * ffn_terms) * row_valid).astype(jnp.bfloat16)
    grad_out = cotangent.astype(jnp.float32) * row_valid
    grad_mlp = (scale_two * grad_out).astype(jnp.bfloat16)
    ffn_grad_in, ffn_grads = ffn_backward(
        normed_two,
        grad_mlp,
        up_mat,
        down_mat,
        up_a_sel,
        up_b_sel,
        down_a_sel,
        down_b_sel,
        rank_up,
        preact,
        hidden,
        rank_down,
    )
    grad_residual = grad_out + norm_back(residual, gain_two, ffn_grad_in)
    grad_attn = (scale_one * grad_residual).astype(jnp.bfloat16)
    full_grad_attn = lax.all_gather(grad_attn, "tensor", axis=1, tiled=True)
    grad_rank_out = product("std,sdr->str", full_grad_attn, out_b_sel).astype(jnp.bfloat16)
    grad_mixed = (
        product("std,fd->stf", full_grad_attn, w_out)
        + product("str,srf->stf", grad_rank_out, out_a_sel)
    ).astype(jnp.bfloat16)
    grad_out_a = product("str,stf->srf", grad_rank_out, mixed)
    grad_out_b = precise("std,str->sdr", full_grad_attn, rank_out)

    def attend_back(slot_items):
        slot_block, valid_keys, log_rows, grad_rows = slot_items
        queries = split_heads(slot_block[0])
        keyrows = split_heads(slot_block[1])
        values = split_heads(slot_block[2])
        scores = masked_scores(queries, keyrows, valid_keys)
        soft = jnp.exp(scores - log_rows[:, :, None])
        soft_low = soft.astype(jnp.bfloat16)
        grad_heads = split_heads(grad_rows)
        grad_soft = product("qhe,khe->hqk", grad_heads, values)
        grad_values = product("hqk,qhe->khe", soft_low, grad_heads)
        grad_scores = (
            soft * (grad_soft - jnp.sum(soft * grad_soft, axis=-1, keepdims=True))
        ).astype(jnp.bfloat16)
        grad_queries = product("hqk,khe->qhe", grad_scores, keyrows) * scale_attn
        grad_keys = product("hqk,qhe->khe", grad_scores, queries) * scale_attn
        return (
            jnp.stack([grad_queries, grad_keys, grad_values])
            .reshape(3, seq_len, -1)
            .astype(jnp.bfloat16)
        )

    grad_projected = lax.map(attend_back, (projected, key_valid, log_total, grad_mixed))
    grad_qkv_b = product("sctf,str->scfr", grad_projected, rank_qkv)
    grad_rank_qkv = product("sctf,scfr->str", grad_projected, qkv_b_sel)
    grad_one_terms = product("sctf,dcf->std", grad_projected, w_qkv) + precise(
        "str,srd->std", grad_rank_qkv, qkv_a_sel
    )
    grad_qkv_a = precise("str,std->srd", grad_rank_qkv, full_one)
    grad_normed_one = lax.psum_scatter(grad_one_terms, "tensor", scatter_dimension=1, tiled=True)
    grad_tokens = grad_residual + norm_back(inputs, gain_one, grad_normed_one)
    onehot_wide = onehot.astype(jnp.float32)

    def stack_slots(slot_grads):
        return jnp.einsum("sn,s...->n...", onehot_wide, slot_grads, precision=HIGHEST)

    grad_up_a, grad_up_b, grad_down_a, grad_down_b = ffn_grads
    sum_qkv_b, sum_out_a = lax.psum((stack_slots(grad_qkv_b), stack_slots(grad_out_a)), "dp")
    joint_sums = lax.psum(
        (
            stack_slots(grad_qkv_a),
            stack_slots(grad_out_b),
            stack_slots(grad_up_a),
            stack_slots(grad_up_b),
            stack_slots(grad_down_a),
            stack_slots(grad_down_b),
        ),
        ("dp", "tensor"),
    )
    sum_qkv_a, sum_out_b, sum_up_a, up_b_whole, down_a_whole, sum_down_b = joint_sums
    width_local = w_up.shape[1]
    first_col = lax.axis_index("tensor") * width_local
    sum_up_b = lax.dynamic_slice_in_dim(up_b_whole, first_col, width_local, 1)
    sum_down_a = lax.dynamic_slice_in_dim(down_a_whole, first_col, width_local, 2)
    return (
        layer_out,
        grad_tokens,
        sum_qkv_a,
        sum_qkv_b,
        sum_out_a,
        sum_out_b,
        sum_up_a,
        sum_up_b,
        sum_down_a,
        sum_down_b,
    )


F32 = jnp.float32
BF = jnp.bfloat16
LOG2E = 1.4426950408889634
PARTS = 8
PAD = 128
FLIP = [(0, 1), (1, 0)]
SWAP = [(1, 2), (2, 1)]


def dotg(a, b, ca, cb):
    return lax.dot_general(a, b, (((ca,), (cb,)), ((), ())), preferred_element_type=F32)


def pad_rows(table):
    rank, width = table.shape
    return jnp.concatenate([table, jnp.zeros((PAD - rank, width), table.dtype)], axis=0)


def pad_twice(table):
    rank, width = table.shape
    return jnp.concatenate([table, table, jnp.zeros((PAD - 2 * rank, width), table.dtype)], axis=0)


def two_terms(wide, rank):
    high = wide.astype(BF).astype(F32)
    return (high + pltpu.roll(wide - high, rank, 1)).astype(BF)


def three_terms(wide):
    high = wide.astype(BF)
    rest = wide - high.astype(F32)
    middle = rest.astype(BF)
    return high, middle, (rest - middle.astype(F32)).astype(BF)


def whole():
    return pl.BlockSpec(memory_space=pltpu.VMEM)


def in_place():
    return pl.BlockSpec(memory_space=pl.ANY)


def scalars():
    return pl.BlockSpec(memory_space=pltpu.SMEM)


def params(mib=58, **more):
    return pltpu.CompilerParams(vmem_limit_bytes=mib * 2**20, **more)


def cost(flops, nbytes):
    return pl.CostEstimate(flops=int(flops * 0.25), bytes_accessed=int(nbytes * 0.025), transcendentals=0)


def norm_stats(values):
    average = jnp.mean(values, axis=-1, keepdims=True)
    centred = values - average
    scale = lax.rsqrt(jnp.mean(centred * centred, axis=-1, keepdims=True) + epsilon)
    return centred * scale, scale


def norm_grad(unit, scale, grad):
    return scale * (
        grad
        - jnp.mean(grad, axis=-1, keepdims=True)
        - unit * jnp.mean(grad * unit, axis=-1, keepdims=True)
    )


def row_mask(scal, rows):
    at = lax.broadcasted_iota(jnp.int32, (rows, 1), 0) + scal[1] * rows
    return (at < scal[0]).astype(F32)


def choose(scal, here, swapped, target, sem):
    @pl.when(scal[3] != 0)
    def _():
        pltpu.make_async_copy(here, target, sem).start()

    @pl.when(scal[3] == 0)
    def _():
        pltpu.make_async_copy(swapped, target, sem).start()

    return pltpu.make_async_copy(here, target, sem)


def fetch(arrays, nears, target, sem, part_at, axis, size):
    copies = []
    parts = len(nears)
    for number, near in enumerate(nears):
        first = pl.multiple_of(((part_at % parts) ^ near) * size, size)
        place = target.at[:, pl.ds(first, size)] if axis == 1 else target.at[pl.ds(first, size)]
        copies.append(pltpu.make_async_copy(arrays[number // 2].at[number % 2], place, sem.at[near]))
    for copy in copies:
        copy.start()
    return copies


def qkv_local_kernel(scal, here, swapped, gain, w, qa, qb, tok, n1, rank, queries, rest, low, sem):
    step = pl.program_id(0)

    @pl.when(step == 0)
    def _():
        choose(scal, here, swapped, tok, sem.at[0]).wait()
        unit, _ = norm_stats(tok[...].astype(F32))
        normed = (unit * gain[...]).astype(BF)
        n1[...] = normed
        ranked = dotg(normed, pad_rows(qa[...]), 1, 1).astype(BF)
        rank[...] = ranked
        low[...] = ranked

    out = (dotg(n1[...], w[0], 1, 0) + dotg(low[...], pad_rows(qb[...]), 1, 0)).astype(BF)

    @pl.when(step < 2)
    def _():
        rest[0] = out

    @pl.when(step == 2)
    def _():
        queries[...] = out


def qkv_local(scal, tok, swapped, gain, w, qa, qb):
    rows, width = tok.shape
    third = w.shape[2]
    rank = qa.shape[0]
    fixed = lambda c: (0, 0)
    return pl.pallas_call(
        qkv_local_kernel,
        grid=(3,),
        in_specs=[
            scalars(),
            in_place(),
            in_place(),
            pl.BlockSpec((1, width), fixed),
            pl.BlockSpec((1, width, third), lambda c: ((c + 1) % 3, 0, 0)),
            pl.BlockSpec((rank, width), fixed),
            pl.BlockSpec((rank, third), lambda c: (0, (c + 1) % 3)),
        ],
        out_specs=[
            pl.BlockSpec((rows, width), fixed),
            pl.BlockSpec((rows, width), fixed),
            pl.BlockSpec((rows, PAD), fixed),
            pl.BlockSpec((rows, third), fixed),
            pl.BlockSpec((1, rows, third), lambda c: (jnp.minimum(c, 1), 0, 0)),
        ],
        out_shape=[
            jax.ShapeDtypeStruct((rows, width), BF),
            jax.ShapeDtypeStruct((rows, width), BF),
            jax.ShapeDtypeStruct((rows, PAD), BF),
            jax.ShapeDtypeStruct((rows, third), BF),
            jax.ShapeDtypeStruct((2, rows, third), BF),
        ],
        scratch_shapes=[pltpu.VMEM((rows, PAD), BF), pltpu.SemaphoreType.DMA((1,))],
        compiler_params=params(dimension_semantics=("arbitrary",)),
        cost_estimate=cost(7e-6 * 1e15, 8e6),
        name="qkv_local",
    )(scal, tok, swapped, gain, w, qa, qb)


def qkv_other_kernel(nears, scal, n1, rank, qb, *rest):
    arrays, (queries, out, w, sem) = rest[: len(nears) // 2], rest[len(nears) // 2 :]
    third = w.shape[2]
    copies = fetch(arrays, nears, w, sem, scal[2], 1, arrays[0].shape[2])
    for copy in copies:
        copy.wait()
    for c in (1, 2, 0):
        at = slice(c * third, (c + 1) * third)
        terms = (dotg(n1[...], w[c], 1, 0) + dotg(rank[...], pad_rows(qb[:, at]), 1, 0)).astype(BF)
        if c == 0:
            queries[...] = terms
        else:
            out[c - 1] = terms


def qkv_other(scal, n1, rank, qb, half):
    rows, width = n1.shape
    arrays, nears = half.pairs, half.names
    third = arrays[0].shape[3]
    return pl.pallas_call(
        functools.partial(qkv_other_kernel, nears),
        in_specs=[scalars(), whole(), whole(), whole()] + [in_place()] * len(arrays),
        out_specs=[whole()] * 3,
        out_shape=[
            jax.ShapeDtypeStruct((rows, third), BF),
            jax.ShapeDtypeStruct((2, rows, third), BF),
            jax.ShapeDtypeStruct((3, width, third), BF),
        ],
        scratch_shapes=[pltpu.SemaphoreType.DMA((PARTS,))],
        compiler_params=params(),
        cost_estimate=cost(7e-6 * 1e15, 10e6),
        name="qkv_other",
    )(scal, n1, rank, qb, *arrays)


def lane_numbers(rows):
    return lax.broadcasted_iota(jnp.int32, (rows, 2 * HD), 1)


def key_fill(scal, rows, other, ones):
    side = 1 - scal[1] if other else scal[1]
    lanes = lane_numbers(rows) % HD
    at = lax.broadcasted_iota(jnp.int32, (rows, 2 * HD), 0) + side * rows
    bias = jnp.where(at < jnp.maximum(scal[0], 1), 0.0, masked_score)
    return jnp.where(lanes < ones, 1.0, jnp.where(lanes == ones, bias, 0.0)).astype(BF)


def lane_terms(wide, rows, with_one):
    lanes = lane_numbers(rows) % HD
    first, second, third = three_terms(wide)
    filled = jnp.where(lanes == 2, third, jnp.full_like(third, 0.0))
    if with_one:
        filled = jnp.where(lanes == 3, jnp.full_like(third, 1.0), filled)
    return jnp.where(lanes == 0, first, jnp.where(lanes == 1, second, filled))


def attend_kernel(scal, q_ref, k_ref, v_ref, ko_ref, vo_ref, out, log_out, qx, kx, vt):
    rows = q_ref.shape[0]
    queries = (q_ref[...].astype(F32) * HD**-0.5).astype(BF)
    lanes = lane_numbers(rows)
    low_half = lanes < HD
    ones = (lanes % HD == 0).astype(BF)
    fills = [key_fill(scal, rows, side == 1, 0) for side in range(2)]
    for head in range(2):
        own = low_half if head == 0 else ~low_half
        qx[head] = jnp.where(own, queries, ones)
        for side, ref in enumerate((k_ref, ko_ref)):
            kx[head, side * rows : (side + 1) * rows] = jnp.where(own, ref[0], fills[side])
    for side, ref in enumerate((v_ref, vo_ref)):
        at = slice(side * rows, (side + 1) * rows)
        turned = ref[0].T
        for head in range(2):
            vt[head, 0:HD, at] = turned[head * HD : (head + 1) * HD]
            vt[head, HD : HD + 16, at] = jnp.ones((16, rows), BF)

    def scores(head):
        return dotg(kx[head], qx[head], 1, 1)

    ahead = scores(0)
    mixed, logs = [], []
    for head in range(2):
        now = ahead
        if head == 0:
            ahead = scores(1)
        top = jnp.max(now, axis=0, keepdims=True)
        soft = jnp.exp(now - top).astype(BF)
        terms = dotg(vt[head], soft, 1, 0)
        total = terms[HD : HD + 1]
        mixed.append(terms[0:HD] / total)
        logs.append(jnp.broadcast_to(top + jnp.log(total), (HD, total.shape[1])))
    out[...] = jnp.concatenate(mixed, axis=0).T.astype(BF)
    log_out[...] = jnp.concatenate([logs[1], logs[0]], axis=0).T


def attend(scal, queries, own, other):
    _, rows, width = own.shape
    pairs = width // (2 * HD)
    take = lambda c: pl.BlockSpec((1, rows, 2 * HD), lambda p: (c, 0, p))
    flat = pl.BlockSpec((rows, 2 * HD), lambda p: (0, p))
    return pl.pallas_call(
        attend_kernel,
        grid=(pairs,),
        in_specs=[scalars(), flat, take(0), take(1), take(0), take(1)],
        out_specs=[flat, flat],
        out_shape=[jax.ShapeDtypeStruct((rows, width), BF), jax.ShapeDtypeStruct((rows, width), F32)],
        scratch_shapes=[
            pltpu.VMEM((2, rows, 2 * HD), BF),
            pltpu.VMEM((2, 2 * rows, 2 * HD), BF),
            pltpu.VMEM((2, HD + 16, 2 * rows), BF),
        ],
        compiler_params=params(dimension_semantics=("arbitrary",)),
        cost_estimate=cost(16e-6 * 1e15, 6e6),
        name="attend",
    )(scal, queries, own, own, other, other)


def attend_back_kernel(
    scal, q_ref, k_ref, v_ref, ko_ref, vo_ref, mixed_ref, grad_ref, log_ref, queries_out, own_out, other_out,
    qx, gx, qm, gm, kx, vx, kt,
):
    rows = q_ref.shape[0]
    queries, grad = q_ref[...], grad_ref[...]
    zero = jnp.zeros_like(queries)
    low_half = lane_numbers(rows) < HD
    scaled = (queries.astype(F32) * HD**-0.5).astype(BF)
    weighed = grad.astype(F32) * mixed_ref[...].astype(F32)
    high = weighed.astype(BF)
    pair = jnp.concatenate([high, (weighed - high.astype(F32)).astype(BF)], axis=1)
    down = lax.broadcasted_iota(jnp.int32, (4 * HD, 2 * HD), 0) // HD % 2
    across = lax.broadcasted_iota(jnp.int32, (4 * HD, 2 * HD), 1) // HD
    sums = dotg(pair, (down != across).astype(BF), 1, 0)
    query_fill = lane_terms(-log_ref[...], rows, True)
    grad_fill = lane_terms(-sums, rows, False)
    fills = [key_fill(scal, rows, side == 1, 3) for side in range(2)]
    value_fill = (lane_numbers(rows) % HD < 3).astype(BF)
    for head in range(2):
        own = low_half if head == 0 else ~low_half
        qx[head] = jnp.where(own, scaled, query_fill)
        gx[head] = jnp.where(own, grad, grad_fill)
        qm[head] = jnp.where(own, queries, zero)
        gm[head] = jnp.where(own, grad, zero)
        for side, (key_ref, value_ref) in enumerate(((k_ref, v_ref), (ko_ref, vo_ref))):
            at = slice(side * rows, (side + 1) * rows)
            kx[head, at] = jnp.where(own, key_ref[0], fills[side])
            vx[head, at] = jnp.where(own, value_ref[0], value_fill)
    for side, ref in enumerate((k_ref, ko_ref)):
        kt[:, side * rows : (side + 1) * rows] = ref[0].T
    steps = [(side, head) for side in range(2) for head in range(2)]

    def first(side, head):
        at = slice(side * rows, (side + 1) * rows)
        return dotg(kx[head, at], qx[head], 1, 1), dotg(vx[head, at], gx[head], 1, 1)

    ahead = first(*steps[0])
    grad_queries = [0.0, 0.0]
    kept = None
    for number, (side, head) in enumerate(steps):
        scores, grad_soft = ahead
        if number + 1 < len(steps):
            ahead = first(*steps[number + 1])
        soft = jnp.exp(scores)
        grad_scores = (soft * grad_soft).astype(BF)
        values = dotg(soft.astype(BF), gm[head], 1, 0)
        keys = dotg(grad_scores, qm[head], 1, 0)
        at = slice(side * rows, (side + 1) * rows)
        grad_queries[head] += dotg(kt[head * HD : (head + 1) * HD, at], grad_scores, 1, 0)
        if head == 0:
            kept = (keys, values)
        else:
            keys = ((kept[0] + keys) * HD**-0.5).astype(BF)
            values = (kept[1] + values).astype(BF)
            out = own_out if side == 0 else other_out
            out[0], out[1] = keys, values
    queries_out[...] = (jnp.concatenate(grad_queries, axis=0).T * HD**-0.5).astype(BF)


def attend_back(scal, queries, own, other, mixed, grad, logs, piece, pieces):
    _, rows, width = own.shape
    width = width // pieces
    pairs = width // (2 * HD)
    skip = piece * pairs
    take = lambda c: pl.BlockSpec((1, rows, 2 * HD), lambda p: (c, 0, p + skip))
    flat = pl.BlockSpec((rows, 2 * HD), lambda p: (0, p + skip))
    both = jax.ShapeDtypeStruct((2, rows, width), BF)
    return pl.pallas_call(
        attend_back_kernel,
        grid=(pairs,),
        in_specs=[scalars(), flat, take(0), take(1), take(0), take(1), flat, flat, flat],
        out_specs=[
            pl.BlockSpec((rows, 2 * HD), lambda p: (0, p)),
            pl.BlockSpec((2, rows, 2 * HD), lambda p: (0, 0, p)),
            pl.BlockSpec((2, rows, 2 * HD), lambda p: (0, 0, p)),
        ],
        out_shape=[jax.ShapeDtypeStruct((rows, width), BF), both, both],
        scratch_shapes=[pltpu.VMEM((2, rows, 2 * HD), BF)] * 4
        + [pltpu.VMEM((2, 2 * rows, 2 * HD), BF)] * 2
        + [pltpu.VMEM((2 * HD, 2 * rows), BF)],
        compiler_params=params(dimension_semantics=("arbitrary",)),
        cost_estimate=cost(26e-6 / pieces * 1e15, 9e6),
        name="attend_back",
    )(scal, queries, own, own, other, other, mixed, grad, logs)


def branch_kernel(nears, scal, mix_a, mix_b, tok, w_a, oa_a, oa_b, obs, scale_one, gain_two, uas, *rest):
    arrays = rest[: len(nears) // 2]
    residual, n2, rank_out, rank_up, w_b, sem = rest[len(nears) // 2 :]
    rank = oa_a.shape[0]
    ob, ua = obs[scal[4]], uas[scal[4]]

    @pl.when(pl.program_id(0) == 0)
    def _():
        for copy in fetch(arrays, nears, w_b, sem, scal[2], 0, arrays[0].shape[1]):
            copy.wait()

    ranked = dotg(mix_a[...], pad_rows(oa_a[...]), 1, 1) + dotg(mix_b[...], pad_rows(oa_b[:, -oa_a.shape[1] :]), 1, 1)
    ranked = two_terms(ranked, rank)
    rank_out[...] = ranked
    terms = dotg(mix_a[...], w_a[...], 1, 0) + dotg(mix_b[...], w_b[...], 1, 0)
    terms = terms + dotg(ranked, pad_twice(ob), 1, 0)
    total = tok[...].astype(F32) + scale_one[...] * terms
    residual[...] = total.astype(BF)
    unit, _ = norm_stats(total)
    normed = (unit * gain_two[...]).astype(BF)
    n2[...] = normed
    rank_up[...] = dotg(normed, pad_rows(ua), 1, 1).astype(BF)


def blocked(rows, width):
    return pl.BlockSpec((rows, width), lambda step: (step, 0))


def fixed_block(*shape):
    return pl.BlockSpec(shape, lambda step: (0,) * len(shape))


def branch(scal, mix_a, mix_b, tok, w_a, half, oa_a, oa_b, ob, scale_one, gain_two, ua):
    rows, width = tok.shape
    heads = mix_a.shape[1]
    block = rows // 2
    arrays, nears = half.pairs, half.names
    return pl.pallas_call(
        functools.partial(branch_kernel, nears),
        grid=(2,),
        in_specs=[scalars(), blocked(block, heads), blocked(block, heads), blocked(block, width)]
        + [fixed_block(*array.shape) for array in (w_a, oa_a, oa_b, ob, scale_one, gain_two, ua)]
        + [in_place()] * len(arrays),
        out_specs=[blocked(block, width), blocked(block, width), blocked(block, PAD), blocked(block, PAD)]
        + [fixed_block(*w_a.shape)],
        out_shape=[
            jax.ShapeDtypeStruct((rows, width), BF),
            jax.ShapeDtypeStruct((rows, width), BF),
            jax.ShapeDtypeStruct((rows, PAD), BF),
            jax.ShapeDtypeStruct((rows, PAD), BF),
            jax.ShapeDtypeStruct(w_a.shape, BF),
        ],
        scratch_shapes=[pltpu.SemaphoreType.DMA((PARTS,))],
        compiler_params=params(dimension_semantics=("arbitrary",)),
        cost_estimate=cost(8e-6 * 1e15, 16e6),
        name="branch",
    )(scal, mix_a, mix_b, tok, w_a, oa_a, oa_b, ob, scale_one, gain_two, ua, *arrays)


def mlp_kernel(nears, step, more, *refs):
    scal, n2, rank_up, ub, da = refs[:5]
    count = 1 if nears is None else len(nears)
    ups, downs = refs[5 : 5 + count], refs[5 + count : 5 + 2 * count]
    rest = refs[5 + 2 * count :]
    if nears is None:
        cot, scale_two, dbs, grad_mlp, grad_rank = rest[:5]
        earlier, rest = (), rest[5:]
        ub, da, db = (table.at[scal[4]] for table in (ub, da, dbs))
    else:
        grad_mlp, grad_rank = rest[:2]
        earlier, rest = rest[2 : 2 + more], rest[2 + more :]
    m_out, g_out, rd_out, gru_out, gub_out, gda_out = rest[:6]
    wu, wd, ubs, das, hidden, grad_pre, sem = rest[6:]
    width = wu.shape[1]
    rank = ub.shape[0]
    size = gub_out.shape[1] // PARTS
    pieces = width // size
    chunks = width // step
    waits = [[] for _ in range(chunks)]
    for piece in range(pieces):
        at = pl.ds(piece * size, size)
        if nears is None:
            sources = ups[0].at[:, at], downs[0].at[at]
        else:
            sources = ups[piece], downs[piece]
        for which, (source, target) in enumerate(zip(sources, (wu.at[:, at], wd.at[at]))):
            copy = pltpu.make_async_copy(source, target, sem.at[which, piece])
            copy.start()
            waits[piece * size // step].append(copy)
    def place(piece, first=0):
        if nears is None:
            return pl.ds(piece * size, size)
        return pl.ds(pl.multiple_of((scal[2] ^ nears[piece]) * size + first, size), size)

    if nears is None:
        grad_low = (scale_two[...] * (cot[...].astype(F32) * row_mask(scal, cot.shape[0]))).astype(BF)
        grad_mlp[...] = grad_low
        grad_rank[...] = dotg(grad_low, pad_rows(db[...]), 1, 1).astype(BF)
    if more == 6:
        gub_out[...], gda_out[...] = earlier[4][...], earlier[5][...]
    ubs[...] = jnp.zeros_like(ubs)
    das[...] = jnp.zeros_like(das)
    for piece in range(pieces):
        at = slice(piece * size, (piece + 1) * size)
        ubs[0:rank, at] = ub[:, place(piece)]
        das[0:rank, at] = da[:, place(piece, da.shape[1] // 2)]
    up_turned = rank_up[...].T[0:rank]
    grad_turned = grad_rank[...].T[0:rank]

    def first(k):
        for copy in waits[k]:
            copy.wait()
        at = slice(k * step, (k + 1) * step)
        return (
            dotg(n2[...], wu[:, at], 1, 0) + dotg(rank_up[...], ubs[:, at], 1, 0),
            dotg(grad_mlp[...], wd[at, :], 1, 1) + dotg(grad_rank[...], das[:, at], 1, 0),
        )

    ahead = first(0)
    for k in range(chunks):
        at = slice(k * step, (k + 1) * step)
        preact, grad_hidden = ahead
        if k + 1 < chunks:
            ahead = first(k + 1)
        cdf = 0.5 * (1.0 + lax.erf(preact * 0.7071067811865476))
        hidden[:, at] = (preact * cdf).astype(BF)
        slope = cdf + preact * jnp.exp(-0.5 * preact * preact) * 0.3989422804014327
        grad_pre[:, at] = (grad_hidden * slope).astype(BF)
    ranked = dotg(hidden[...], das[...], 1, 1)
    grad_ranked = dotg(grad_pre[...], ubs[...], 1, 1)
    if more:
        ranked, grad_ranked = ranked + earlier[2][...], grad_ranked + earlier[3][...]
    rd_out[...] = ranked
    gru_out[...] = grad_ranked
    for piece in range(pieces):
        at = slice(piece * size, (piece + 1) * size)
        gub_out[:, place(piece)] = dotg(up_turned, grad_pre[:, at], 1, 0)
        gda_out[:, place(piece)] = dotg(grad_turned, hidden[:, at], 1, 0)
    for at in (slice(k, k + step) for k in range(0, wu.shape[0], step)):
        terms = dotg(hidden[...], wd[:, at], 1, 0)
        grad_terms = dotg(grad_pre[...], wu[at, :], 1, 1)
        if more:
            terms = terms + earlier[0][:, at].astype(F32)
            grad_terms = grad_terms + earlier[1][:, at].astype(F32)
        m_out[:, at] = terms.astype(BF)
        g_out[:, at] = grad_terms.astype(BF)


def mlp(scal, n2, rank_up, ub, da, ups, downs, grads, nears=None, earlier=()):
    rows, width = n2.shape
    rank, half = ub.shape[-2:]
    half = half if nears is None else half // 2
    units = half if nears is None else len(nears) * half // PARTS
    step = min(512, units)
    sums = jax.ShapeDtypeStruct((rows, width), BF)
    ranked = jax.ShapeDtypeStruct((rows, PAD), F32)
    table = jax.ShapeDtypeStruct((rank, half), F32)
    low = jax.ShapeDtypeStruct((rows, width), BF)
    first = [low, jax.ShapeDtypeStruct((rows, PAD), BF)] if nears is None else []
    return pl.pallas_call(
        functools.partial(mlp_kernel, nears, step, len(earlier)),
        in_specs=[scalars()]
        + [whole()] * 4
        + [in_place()] * (2 * len(ups))
        + [whole()] * (len(grads) + len(earlier)),
        out_specs=[whole()] * (len(first) + 6),
        out_shape=first + [sums, sums, ranked, ranked, table, table],
        scratch_shapes=[
            pltpu.VMEM((width, units), BF),
            pltpu.VMEM((units, width), BF),
            pltpu.VMEM((PAD, units), BF),
            pltpu.VMEM((PAD, units), BF),
            pltpu.VMEM((rows, units), BF),
            pltpu.VMEM((rows, units), BF),
            pltpu.SemaphoreType.DMA((2, PARTS)),
        ],
        compiler_params=params(),
        cost_estimate=cost(25e-6 * units / half * 1e15, 20e6),
        name="mlp",
    )(scal, n2, rank_up, ub, da, *ups, *downs, *grads, *earlier)


def mlp_other(scal, n2, rank_up, tables, up, down, grads, earlier):
    for odd in range(2):
        ups, nears = up.held(odd)
        downs, same = down.held(odd)
        assert nears == same
        earlier = mlp(scal, n2, rank_up, tables, tables, ups, downs, grads, nears, tuple(earlier))
    return earlier


def middle_kernel(
    scal, residual, m_in, g_in, rd, gru, cot, mix_a, mix_b, rank_out, n2, grad_mlp,
    dbs, uas, scale_two, gain_two, scale_one, w_a, w_b, oa_a, oa_b, obs,
    layer, grad_res, grad_a, grad_b, goa_a, goa_b, gob, gua, gdb,
):
    step = pl.program_id(0)
    rows = residual.shape[0]
    db, ua, ob = dbs[scal[4]], uas[scal[4]], obs[scal[4]]
    rank = db.shape[0]
    at = lax.broadcasted_iota(jnp.int32, (rows, 1), 0) + (scal[1] * pl.num_programs(0) + step) * rows
    valid = (at < scal[0]).astype(F32)
    down = two_terms(rd[...], rank)
    up = two_terms(gru[...], rank)

    def add(out, terms):
        @pl.when(step == 0)
        def _():
            out[...] = terms

        @pl.when(step > 0)
        def _():
            out[...] += terms

    def turned(terms, right):
        both = dotg(terms.T[0 : 2 * rank], right, 1, 0)
        return both[0:rank] + both[rank : 2 * rank]

    branch_out = m_in[...].astype(F32) + dotg(down, pad_twice(db), 1, 0)
    total = residual[...].astype(F32)
    layer[...] = ((total + scale_two[...] * branch_out) * valid).astype(BF)
    add(gua, turned(up, n2[...]))
    add(gdb, turned(down, grad_mlp[...]))
    unit, scale = norm_stats(total)
    grad_normed = (g_in[...].astype(F32) + dotg(up, pad_twice(ua), 1, 0)) * gain_two[...]
    grad_total = cot[...].astype(F32) * valid + norm_grad(unit, scale, grad_normed)
    grad_res[...] = grad_total.astype(BF)
    grad_attn = (scale_one[...] * grad_total).astype(BF)
    grad_rank = dotg(grad_attn, pad_rows(ob), 1, 1).astype(BF)
    grad_a[...] = (
        dotg(grad_attn, w_a[...], 1, 1) + dotg(grad_rank, pad_rows(oa_a[...]), 1, 0)
    ).astype(BF)
    grad_b[...] = (
        dotg(grad_attn, w_b[...], 1, 1) + dotg(grad_rank, pad_rows(oa_b[:, -oa_a.shape[1] :]), 1, 0)
    ).astype(BF)
    rank_turned = grad_rank.T[0:rank]
    add(goa_a, dotg(rank_turned, mix_a[...], 1, 0))
    add(goa_b, dotg(rank_turned, mix_b[...], 1, 0))
    add(gob, turned(rank_out[...], grad_attn))


def middle(scal, by_rows, others, blocks=1):
    rows, width = by_rows[0].shape
    block = rows // blocks
    heads = by_rows[6].shape[1]
    rank = others[0].shape[1]
    part = jax.ShapeDtypeStruct((rows, heads), BF)
    table = jax.ShapeDtypeStruct((rank, width), F32)
    half_table = jax.ShapeDtypeStruct((rank, heads), F32)
    return pl.pallas_call(
        middle_kernel,
        grid=(blocks,),
        in_specs=[scalars()]
        + [blocked(block, array.shape[1]) for array in by_rows]
        + [fixed_block(*array.shape) for array in others],
        out_specs=[blocked(block, width), blocked(block, width), blocked(block, heads), blocked(block, heads)]
        + [fixed_block(*shape) for shape in ((rank, heads),) * 2 + ((rank, width),) * 3],
        out_shape=[jax.ShapeDtypeStruct((rows, width), BF)] * 2
        + [part, part, half_table, half_table, table, table, table],
        compiler_params=params(dimension_semantics=("arbitrary",)),
        cost_estimate=cost(9e-6 * 1e15, 20e6),
        name="middle",
    )(scal, *by_rows, *others)


def columns_of(pieces):
    first = 0
    for piece in pieces:
        yield piece, slice(first, first + piece.shape[-1])
        first += piece.shape[-1]


def qkv_tables_kernel(counts, *refs):
    sides = []
    for count in counts:
        sides.append((refs[:count], refs[count : 2 * count], refs[2 * count : 3 * count]))
        refs = refs[3 * count :]
    scal, qb_a, qb_b, n1, rank_in, total_a, total_b, rank_out, kept, sent, gqb_a, gqb_b, gqa = refs
    rank = qb_a.shape[0]
    third = qb_a.shape[1] // 3
    rank_turned = rank_in[...].T[0:rank]
    ranked = None
    for side, qb, total, table in zip(sides, (qb_a, qb_b), (total_a, total_b), (gqb_a, gqb_b)):
        queries, owns, gots = side
        for (piece, at), own, got in zip(columns_of(queries), owns, gots):
            for c in range(3):
                if c == 0:
                    grad = piece[...]
                else:
                    grad = (own[c - 1].astype(F32) + got[c - 1].astype(F32)).astype(BF)
                    total[c - 1, :, at] = grad
                place = slice(c * third + at.start, c * third + at.stop)
                table[:, place] = dotg(rank_turned, grad, 1, 0)
                terms = dotg(grad, pad_rows(qb[:, place]), 1, 1)
                ranked = terms if ranked is None else ranked + terms
    ranked = two_terms(ranked, rank)
    rank_out[...] = ranked
    both = dotg(ranked.T[0 : 2 * rank], n1[...], 1, 0)
    gqa[...] = both[0:rank] + both[rank : 2 * rank]
    first = 0
    for table in (gqb_a, gqa, gqb_b):
        half = table.shape[1] // 2
        at = slice(first, first + half)
        kept[:, at] = table[:, pl.ds(pl.multiple_of(scal[1] * half, half), half)]
        sent[:, at] = table[:, pl.ds(pl.multiple_of((1 - scal[1]) * half, half), half)].astype(BF)
        first += half


def qkv_tables(scal, side_a, side_b, qb_a, qb_b, n1, rank_in):
    rows, width = n1.shape
    rank, columns = qb_a.shape
    pieces = [piece for side in (side_a, side_b) for group in side for piece in group]
    total = jax.ShapeDtypeStruct((2, rows, columns // 3), BF)
    share = columns + width // 2
    return pl.pallas_call(
        functools.partial(qkv_tables_kernel, (len(side_a[0]), len(side_b[0]))),
        in_specs=[whole()] * len(pieces) + [scalars()] + [whole()] * 4,
        out_specs=[whole()] * 5,
        out_shape=[total, total, jax.ShapeDtypeStruct((rows, PAD), BF)]
        + [jax.ShapeDtypeStruct((rank, share), F32), jax.ShapeDtypeStruct((rank, share), BF)],
        scratch_shapes=[pltpu.VMEM((rank, columns), F32)] * 2 + [pltpu.VMEM((rank, width), F32)],
        compiler_params=params(),
        cost_estimate=cost(7e-6 * 1e15, 14e6),
        name="qkv_tables",
    )(*pieces, scal, qb_a, qb_b, n1, rank_in)


def qkv_rows_kernel(count_a, count_b, *refs):
    grads_a, grads_b, refs = refs[:count_a], refs[count_a : count_a + count_b], refs[count_a + count_b :]
    w_a, w_b, ranked, qa, tok, gain, grad_res, out = refs
    grad = dotg(ranked[...], pad_twice(qa[...]), 1, 0)
    for grads, w in ((grads_a, w_a), (grads_b, w_b)):
        for piece, at in columns_of(grads[:-1]):
            grad = grad + dotg(piece[...], w[0, :, at], 1, 1)
        for c in (1, 2):
            grad = grad + dotg(grads[-1][c - 1], w[c], 1, 1)
    unit, scale = norm_stats(tok[...].astype(F32))
    out[...] = (grad_res[...].astype(F32) + norm_grad(unit, scale, grad * gain[...])).astype(BF)


def qkv_rows(block_at, blocks, grads_a, grads_b, w_a, w_b, ranked, qa, tok, gain, grad_res):
    rows, width = tok.shape
    block = rows // blocks
    flat = lambda array: pl.BlockSpec((block, array.shape[1]), lambda step: (block_at, 0))
    deep = lambda array: pl.BlockSpec((2, block, array.shape[2]), lambda step: (0, block_at, 0))
    specs = [flat(array) if array.ndim == 2 else deep(array) for array in grads_a + grads_b]
    return pl.pallas_call(
        functools.partial(qkv_rows_kernel, len(grads_a), len(grads_b)),
        grid=(1,),
        in_specs=specs
        + [whole(), whole(), flat(ranked), whole(), flat(tok), whole(), flat(grad_res)],
        out_specs=whole(),
        out_shape=jax.ShapeDtypeStruct((block, width), BF),
        compiler_params=params(),
        cost_estimate=cost(12e-6 / blocks * 1e15, 16e6 / blocks),
        name="qkv_rows",
    )(*grads_a, *grads_b, w_a, w_b, ranked, qa, tok, gain, grad_res)


def gather_kernel(has_ids, flag, *refs):
    ids, (own, got, out, ids_out, total) = refs[0], refs[has_ids:]
    columns = out.shape[2]
    half = own.shape[0]
    total[...] = jnp.zeros_like(total)

    def add(first, images):
        for image in range(half):
            if has_ids:
                adapter = ids[first + image]
            else:
                note = images[image, 0:8, columns : columns + PAD].astype(F32)
                adapter = jnp.max(note).astype(jnp.int32)
            ids_out[first + image] = adapter
            total[adapter] += images[image, :, 0:columns].astype(F32)

    @pl.when(flag[0] == 0)
    def _():
        add(0, own)
        add(half, got)

    @pl.when(flag[0] != 0)
    def _():
        add(0, got)
        add(half, own)

    out[...] = total[...].astype(BF)


def gather_images(flag, ids, pair, adapters, columns):
    count, rank, _ = pair[0].shape
    given = [] if ids is None else [ids]
    return pl.pallas_call(
        functools.partial(gather_kernel, len(given)),
        in_specs=[scalars()] * (1 + len(given)) + [whole()] * 2,
        out_specs=[whole(), scalars()],
        out_shape=[
            jax.ShapeDtypeStruct((adapters, rank, columns), BF),
            jax.ShapeDtypeStruct((2 * count,), jnp.int32),
        ],
        scratch_shapes=[pltpu.VMEM((adapters, rank, columns), F32)],
        compiler_params=params(),
        cost_estimate=cost((20e-6 if ids is None else 1e-6) * 1e15, 1e6),
        name="gather_images",
    )(flag.astype(jnp.int32)[None], *given, *pair)


def finish_kernel(cut, spans, places, core, own, other, *outs):
    def write(low, high):
        for (shared, start, stop), (number, index) in zip(spans, places):
            first = cut if shared else 0
            half = own.shape[2] - cut if shared else cut
            out = outs[number] if index is None else outs[number].at[:, index]
            middle = min(max(half - start, 0), stop - start)
            if middle > 0:
                out[:, :, 0:middle] = low[:, :, first + start : first + start + middle].astype(F32)
            if middle < stop - start:
                begin = first + start + middle - half
                out[:, :, middle : stop - start] = high[:, :, begin : first + stop - half].astype(F32)

    @pl.when(core[0] == 0)
    def _():
        write(own, other)

    @pl.when(core[0] != 0)
    def _():
        write(other, own)


def finish(core, cut, spans, places, own, other, shapes, seconds=1e-6):
    return pl.pallas_call(
        functools.partial(finish_kernel, cut, spans, places),
        in_specs=[scalars(), whole(), whole()],
        out_specs=[whole()] * len(shapes),
        out_shape=[jax.ShapeDtypeStruct(shape, F32) for shape in shapes],
        compiler_params=params(),
        cost_estimate=cost(seconds * 1e15, 1e6),
        name="finish",
    )(core, own, other)


def swap(rows):
    return lax.ppermute(rows, ("core", "tensor"), SWAP)


def flip(axis):
    return lambda array: lax.ppermute(array, axis, FLIP)


def after(value, *others):
    return lax.optimization_barrier((value, others))[0]


class OtherHalf:
    BITS = {"core": 1, "x": 2, "zb": 4}

    def __init__(self, local, axis, part_at, count):
        size = local.shape[axis] // count
        self.mine = lax.dynamic_slice_in_dim(local, (part_at % count) * size, size, axis)
        self.parts = {}
        self.nears = tuple(range(0, count, 2))

    def over_tensor(self, *others):
        self.parts[0] = flip("tensor")(after(self.mine, *others) if others else self.mine)

    def hop(self, near, axis, *others):
        part = after(self.parts[near], *others) if others else self.parts[near]
        self.parts[near ^ self.BITS[axis]] = flip(axis)(part)

    def last_hop(self):
        over_zb, over_x = jnp.split(self.parts[2], 2, axis=1)[0], jnp.split(self.parts[4], 2, axis=1)[1]
        self.parts[6] = jnp.concatenate([flip("zb")(over_zb), flip("x")(over_x)], axis=1)

    def pairs_over_cores(self, *others):
        parts = after(self.parts, *others) if others else self.parts
        even = [jnp.stack([parts[a], parts[b]]) for a, b in zip(self.nears[::2], self.nears[1::2])]
        self.pairs = even + [flip("core")(array) for array in even]
        self.names = self.nears + tuple(near + 1 for near in self.nears)

    def held(self, odd):
        names = tuple(near + odd for near in self.nears)
        return [self.parts[near] for near in names], names


def half_columns(array, index):
    size = array.shape[1] // 2
    return lax.dynamic_slice_in_dim(array, index * size, size, 1)


def by_index(index, own, other, axis):
    return jnp.where(
        index == 0, jnp.concatenate([own, other], axis=axis), jnp.concatenate([other, own], axis=axis)
    )


class Sum:
    def __init__(self, kept, sent, cut, adapter, core, tensor):
        self.core, self.tensor, self.adapter = core, tensor, adapter
        self.kept, self.sent, self.cut = kept, sent, cut

    @staticmethod
    def shares(near, shared, far, core):
        def share(index):
            return jnp.concatenate([half_columns(array, index) for array in (near, shared, far)], axis=1)

        return share(core), share(1 - core).astype(BF)

    def over_cores(self):
        total = (self.kept + flip("core")(self.sent).astype(F32)).astype(BF)
        cut, columns = self.cut, total.shape[1] - self.cut
        note = []
        if self.adapter is not None:
            note = [jnp.broadcast_to(self.adapter.astype(BF), (total.shape[0], PAD))]
        self.mine = jnp.concatenate([total[:, :columns]] + note, axis=1)
        self.send = jnp.concatenate([total[:, columns:], total[:, cut:columns]] + note, axis=1)
        self.columns = columns

    def start_pair(self):
        self.flag, self.pair = self.tensor, (self.mine[None], flip("tensor")(self.send)[None])

    def start(self, name):
        self.images = by_index(self.flag, *self.pair, 0)
        if lax.axis_size(name) == 2:
            self.flag, self.pair = lax.axis_index(name), (self.images, flip(name)(self.images))
        else:
            images = lax.all_gather(self.images, name, axis=0, tiled=True)
            half = images.shape[0] // 2
            self.flag, self.pair = jnp.zeros((), jnp.int32), (images[:half], images[half:])

    def arrive(self, *others):
        self.pair = (self.pair[0], after(self.pair[1], *others))

    def over_adapters(self, ids, adapters):
        self.dense, ids = gather_images(self.flag, ids, self.pair, adapters, self.columns)
        self.other = flip("core")(self.dense)
        return ids

    def finish(self, spans, places, shapes, *seconds):
        core = self.core.astype(jnp.int32)[None]
        return finish(core, self.cut, spans, places, self.dense, self.other, shapes, *seconds)


def quad_body(
    tokens, cotangent, lengths, adapter_ids, gain_one, gain_two, scale_one, scale_two, w_qkv, w_out, w_up, w_down,
    qkv_a, qkv_b, out_a, out_b, up_a, up_b, down_a, down_b,
):
    core, tensor = lax.axis_index("core"), lax.axis_index("tensor")
    part_at = lax.axis_index("zb") * 4 + lax.axis_index("x") * 2 + core
    adapters, rank, width = qkv_a.shape
    third = w_qkv.shape[2]
    units = w_up.shape[1]

    w3 = jnp.swapaxes(w_qkv, 0, 1)
    half_qkv = OtherHalf(w3, 1, part_at, PARTS)
    half_out = OtherHalf(w_out, 0, part_at, 4)
    half_up = OtherHalf(w_up, 1, part_at, PARTS)
    half_down = OtherHalf(w_down, 0, part_at, PARTS)
    half_qkv.over_tensor()
    tok_here = tokens[0]
    tok_swapped = swap(tok_here)
    facts = jnp.stack([lengths[0], adapter_ids[0]])
    facts_other = flip("core")(facts)
    mine = jnp.where(core == tensor, facts, facts_other)
    theirs = jnp.where(core == tensor, facts_other, facts)
    length, adapter, adapter_other = mine[0], mine[1], theirs[1]
    scal = jnp.stack([length, core, part_at, core == tensor, adapter]).astype(jnp.int32)

    qkv_b, out_b, up_b, down_b = (jnp.swapaxes(table, -1, -2) for table in (qkv_b, out_b, up_b, down_b))
    pick = lambda table, index: lax.dynamic_index_in_dim(table, index, 0, False)
    flat = lambda table: jnp.swapaxes(table, 0, 1).reshape(rank, 3 * third)
    half_qkv.hop(0, "x")
    half_qkv.hop(0, "zb")
    packed_first = jnp.concatenate([flat(pick(qkv_b, adapter_other)), pick(out_a, adapter_other)], axis=1)
    packed = jnp.concatenate([pick(table, adapter_other) for table in (up_b, down_a)], axis=1)
    qa, oa = pick(qkv_a, adapter), pick(out_a, adapter)
    qb = flat(pick(qkv_b, adapter))
    gain_one, gain_two, scale_one, scale_two = (v.reshape(1, width) for v in (gain_one, gain_two, scale_one, scale_two))

    other_tables = flip("tensor")(packed_first)
    half_up.over_tensor(half_qkv.parts[4], other_tables)
    half_qkv.last_hop()
    half_qkv.parts[6] = after(half_qkv.parts[6], scal, qa, qb, other_tables, half_up.mine)
    tok_swapped = after(tok_swapped, half_qkv.parts[2], half_qkv.parts[4], other_tables, scal, half_out.mine, half_down.mine)
    tok, n1, rank_qkv, q_a, own_a = qkv_local(scal, tok_here, tok_swapped, gain_one, w3, qa, qb)
    half_qkv.pairs_over_cores()
    kv_a = flip("core")(own_a)
    q_b, own_b, w3_other = qkv_other(scal, after(n1, half_up.parts[0]), rank_qkv, other_tables, half_qkv)
    kv_b = flip("core")(own_b)
    half_out.over_tensor(own_b)
    half_up.hop(0, "x", own_b)
    half_up.hop(0, "zb", own_b)
    cot_swapped = swap(after(cotangent[0], own_b))
    mix_a, logs_a = attend(scal, after(q_a, own_b), own_a, kv_a)
    half_out.hop(0, "x", mix_a)
    half_up.hop(4, "x", mix_a)
    half_down.over_tensor(mix_a)
    mix_b, logs_b = attend(scal, after(q_b, mix_a, half_up.parts[2], half_up.parts[4]), own_b, kv_b)
    half_out.pairs_over_cores(mix_b)
    half_down.hop(0, "x", mix_b)
    half_down.hop(0, "zb", mix_b)
    residual, n2, rank_out, rank_up, out_other = branch(
        scal, after(mix_a, half_up.parts[6], half_down.parts[0]), mix_b, tok, w_out, half_out, oa, other_tables, out_b, scale_one, gain_two, up_a
    )
    half_down.hop(2, "zb", n2)
    other_units = flip("tensor")(after(packed, n2))
    for near in (0, 2, 4):
        half_up.hop(near, "core", n2)
    cot = jnp.where(core == tensor, cotangent[0], cot_swapped)
    grad_mlp, grad_rank, m, g, rd, gru, gub_a, gda_a = mlp(
        scal, after(n2, half_down.parts[2], half_down.parts[4]), rank_up, up_b, down_a, [w_up], [w_down],
        [cot, scale_two, down_b],
    )
    half_up.hop(6, "core", m)
    for near in (0, 2, 4, 6):
        half_down.hop(near, "core", m)
    m, g, rd, gru, gub_b, gda_b = mlp_other(
        scal, n2, rank_up, other_units, half_up, half_down, [grad_mlp, grad_rank], (m, g, rd, gru)
    )
    layer, grad_res, grad_a, grad_b, goa_a, goa_b, gob, gua, gdb = middle(
        scal,
        (residual, m, g, rd, gru, cot, mix_a, mix_b, rank_out, n2, grad_mlp),
        (down_b, up_a, scale_two, gain_two, scale_one, w_out, out_other, oa, other_tables, out_b),
    )
    shares = Sum.shares(
        jnp.concatenate([goa_a, gub_a, gda_a], axis=1),
        jnp.concatenate([gob, gua, gdb], axis=1),
        jnp.concatenate([goa_b, gub_b, gda_b], axis=1),
        core,
    )
    early = Sum(*shares, third // 2 + units, adapter, core, tensor)
    early.over_cores()

    def back(queries, own, kv, mixed, grad, logs, piece, pieces, *others):
        return attend_back(scal, after(queries, *others), own, kv, mixed, grad, logs, piece, pieces)

    def exchanged(back, *others):
        return back[0], back[1], flip("core")(after(back[2], *others) if others else back[2])


    side_a = (q_a, own_a, kv_a, mix_a, grad_a, logs_a)
    side_b = (q_b, own_b, kv_b, mix_b, grad_b, logs_b)
    early.start_pair()
    back_1 = back(*side_a, 0, 2, early.send)
    early.arrive(back_1[0])
    early.start("hi")
    back_1 = exchanged(back_1, early.images)
    layer_swapped = swap(after(layer, back_1[0]))
    back_2 = back(*side_a, 1, 2, early.images)
    early.arrive(back_2[0])
    early.start("zb")
    back_2 = exchanged(back_2, early.images)
    back_3 = back(*side_b, 0, 2, early.images)
    early.arrive(back_3[0])
    early.start("x")
    back_3 = exchanged(back_3, early.images)
    back_4 = exchanged(back(*side_b, 1, 2, early.images, layer_swapped))
    kv_sum_a, kv_sum_b, ranked, kept, sent = qkv_tables(
        scal,
        [list(pair) for pair in zip(back_1, back_2)],
        [list(pair) for pair in zip(back_3, back_4)],
        qb, other_tables, n1, rank_qkv,
    )
    early.arrive(kept)
    late = Sum(kept, after(sent, early.pair[1]), 3 * third // 2, None, core, tensor)
    late.over_cores()
    late.start_pair()
    early.arrive(late.send)
    ids = early.over_adapters(None, adapters)
    late.arrive(early.dense)
    late.start("hi")
    grad_rows = qkv_rows(
        0, 1, [back_1[0], back_2[0], kv_sum_a], [back_3[0], back_4[0], kv_sum_b],
        after(w3, late.images), w3_other, ranked, qa, tok, gain_one, grad_res,
    )
    late.arrive(grad_rows)
    grad_rows_swapped = swap(after(grad_rows, late.pair[1]))
    early.other = after(early.other, grad_rows)
    late.start("zb")
    late.start("x")
    late.arrive(grad_rows_swapped)
    in_place_already = core == tensor
    grad_tokens = jnp.where(in_place_already, grad_rows, grad_rows_swapped).astype(F32)
    layer_out = jnp.where(in_place_already, layer, layer_swapped)
    late.over_adapters(ids, adapters)
    ends = (0, third, third + units, third + 2 * units)
    spans = [(False, ends[k], ends[k + 1]) for k in range(3)] + [(True, k * width, (k + 1) * width) for k in range(3)]
    widths = (third, units, units, width, width, width)
    sum_oa, sum_ub, sum_da, sum_ob, sum_ua, sum_db = early.finish(
        spans, [(k, None) for k in range(6)], [(adapters, rank, size) for size in widths], 20e-6
    )
    sum_qb, sum_qa = late.finish(
        [(False, c * third, (c + 1) * third) for c in range(3)] + [(True, 0, width)],
        [(0, c) for c in range(3)] + [(1, None)],
        [(adapters, 3, rank, third), (adapters, rank, width)],
    )
    turn = lambda table: jnp.swapaxes(table, -1, -2)
    return (
        layer_out[None],
        grad_tokens[None],
        sum_qa,
        turn(sum_qb),
        sum_oa,
        turn(sum_ob),
        sum_ua,
        turn(sum_ub),
        sum_da,
        turn(sum_db),
    )


def solution(mesh):
    groups, split = mesh.shape["dp"], mesh.shape["tensor"]
    if split == 2 and groups % 8 == 0:
        mesh = Mesh(mesh.devices.reshape(groups // 8, 2, 2, 2, 2), ("hi", "zb", "x", "core", "tensor"))
        dp, body = ("hi", "zb", "x", "core"), quad_body
    else:
        dp, body = "dp", plain_body
    slots = P(dp, "tensor", None)
    in_specs = (
        slots, slots, P(dp), P(dp), P(), P(), P(), P(),
        P(None, None, "tensor"), P("tensor", None), P(None, "tensor"), P("tensor", None),
        P(), P(None, None, "tensor", None), P(None, None, "tensor"), P(),
        P(), P(None, "tensor", None), P(None, None, "tensor"), P(),
    )
    out_specs = (
        slots, slots, P(), P(None, None, "tensor", None), P(None, None, "tensor"), P(),
        P(), P(None, "tensor", None), P(None, None, "tensor"), P(),
    )
    return jax.shard_map(body, mesh=mesh, in_specs=in_specs, out_specs=out_specs, check_vma=False)
```

```python
import functools

import jax
import jax.numpy as jnp
from jax import lax
from jax.experimental import pallas as pl
from jax.experimental.pallas import tpu as pltpu
from jax.sharding import Mesh
from jax.sharding import PartitionSpec as P

HD = 64
ADAPTERS = 8


epsilon = 1e-06
masked_score = -1e30
HIGHEST = lax.Precision.HIGHEST


def product(form, left, right):
    return jnp.einsum(form, left, right, preferred_element_type=jnp.float32)


def precise(form, left, right):
    return jnp.einsum(form, left.astype(jnp.float32), right.astype(jnp.float32), precision=HIGHEST)


def select_rows(onehot, table):
    return product("sn,n...->s...", onehot, table).astype(table.dtype)


def norm_rows(values, gain_vec):
    average = jnp.mean(values, axis=-1, keepdims=True)
    centred = values - average
    variance = jnp.mean(centred * centred, axis=-1, keepdims=True)
    return centred * lax.rsqrt(variance + epsilon) * gain_vec


def norm_back(values, gain_vec, grad_normed):
    normed, pullback = jax.vjp(lambda rows: norm_rows(rows, gain_vec), values)
    return pullback(grad_normed)[0]


def gelu_slope(values):
    return (
        0.5 * (1.0 + lax.erf(values * 0.7071067811865476))
        + values * jnp.exp(-0.5 * values * values) * 0.3989422804014327
    )


def ffn_forward(rows_low, up_mat, down_mat, up_a_sel, up_b_sel, down_a_sel, down_b_sel):
    rank_up = product("std,srd->str", rows_low, up_a_sel).astype(jnp.bfloat16)
    preact = product("std,dh->sth", rows_low, up_mat) + product("str,shr->sth", rank_up, up_b_sel)
    hidden = jax.nn.gelu(preact, approximate=False).astype(jnp.bfloat16)
    rank_down = product("sth,srh->str", hidden, down_a_sel)
    terms = product("sth,hd->std", hidden, down_mat) + precise(
        "str,sdr->std", rank_down, down_b_sel
    )
    return (rank_up, preact, hidden, rank_down, terms)


def ffn_backward(
    rows_low,
    grad_rows,
    up_mat,
    down_mat,
    up_a_sel,
    up_b_sel,
    down_a_sel,
    down_b_sel,
    rank_up,
    preact,
    hidden,
    rank_down,
):
    grad_rank_down = product("std,sdr->str", grad_rows, down_b_sel).astype(jnp.bfloat16)
    grad_hidden = product("std,hd->sth", grad_rows, down_mat) + product(
        "str,srh->sth", grad_rank_down, down_a_sel
    )
    grad_preact = (grad_hidden * gelu_slope(preact)).astype(jnp.bfloat16)
    grad_up_b = product("sth,str->shr", grad_preact, rank_up)
    grad_rank_up = product("sth,shr->str", grad_preact, up_b_sel)
    grad_rows_in = product("sth,dh->std", grad_preact, up_mat) + precise(
        "str,srd->std", grad_rank_up, up_a_sel
    )
    grad_up_a = precise("str,std->srd", grad_rank_up, rows_low)
    grad_down_a = product("str,sth->srh", grad_rank_down, hidden)
    grad_down_b = precise("std,str->sdr", grad_rows, rank_down)
    return (grad_rows_in, (grad_up_a, grad_up_b, grad_down_a, grad_down_b))


def plain_body(
    tokens,
    cotangent,
    lengths,
    adapter_ids,
    gain_one,
    gain_two,
    scale_one,
    scale_two,
    w_qkv,
    w_out,
    w_up,
    w_down,
    qkv_a,
    qkv_b,
    out_a,
    out_b,
    up_a,
    up_b,
    down_a,
    down_b,
):
    shard_rows = tokens.shape[1]
    seq_len = shard_rows * lax.axis_size("tensor")
    heads_local = w_qkv.shape[2] // HD
    scale_attn = HD ** (-0.5)
    first_row = lax.axis_index("tensor") * shard_rows
    positions = jnp.arange(seq_len, dtype=jnp.int32)
    key_valid = positions[None, :] < jnp.maximum(lengths, 1)[:, None]
    local_rows = first_row + jnp.arange(shard_rows, dtype=jnp.int32)
    row_valid = (local_rows[None, :] < lengths[:, None]).astype(jnp.float32)[:, :, None]
    adapters = jnp.arange(ADAPTERS, dtype=jnp.int32)
    onehot = (adapter_ids[:, None] == adapters[None, :]).astype(jnp.bfloat16)
    qkv_a_sel = select_rows(onehot, qkv_a)
    qkv_b_sel = select_rows(onehot, qkv_b)
    out_a_sel = select_rows(onehot, out_a)
    out_b_sel = select_rows(onehot, out_b)
    up_a_sel = select_rows(onehot, up_a)
    down_b_sel = select_rows(onehot, down_b)
    inputs = tokens.astype(jnp.float32)
    normed_one = norm_rows(inputs, gain_one).astype(jnp.bfloat16)
    full_one = lax.all_gather(normed_one, "tensor", axis=1, tiled=True)
    rank_qkv = product("std,srd->str", full_one, qkv_a_sel).astype(jnp.bfloat16)
    projected = (
        product("std,dcf->sctf", full_one, w_qkv) + product("str,scfr->sctf", rank_qkv, qkv_b_sel)
    ).astype(jnp.bfloat16)

    def split_heads(rows):
        return rows.reshape(seq_len, heads_local, HD)

    def masked_scores(queries, keyrows, valid_keys):
        scores = product("qhe,khe->hqk", queries, keyrows) * scale_attn
        return jnp.where(valid_keys[None, None, :], scores, masked_score)

    def attend(slot_items):
        slot_block, valid_keys = slot_items
        queries = split_heads(slot_block[0])
        keyrows = split_heads(slot_block[1])
        values = split_heads(slot_block[2])
        scores = masked_scores(queries, keyrows, valid_keys)
        row_max = jnp.max(scores, axis=-1, keepdims=True)
        exponent = jnp.exp(scores - row_max)
        row_total = jnp.sum(exponent, axis=-1, keepdims=True)
        soft_low = (exponent / row_total).astype(jnp.bfloat16)
        mixed_rows = (
            product("hqk,khe->qhe", soft_low, values).astype(jnp.bfloat16).reshape(seq_len, -1)
        )
        return (mixed_rows, (row_max + jnp.log(row_total))[:, :, 0])

    mixed, log_total = lax.map(attend, (projected, key_valid))
    rank_out = product("stf,srf->str", mixed, out_a_sel)
    attn_terms = product("stf,fd->std", mixed, w_out) + precise("str,sdr->std", rank_out, out_b_sel)
    attn_branch = lax.psum_scatter(attn_terms, "tensor", scatter_dimension=1, tiled=True)
    residual = inputs + scale_one * attn_branch
    normed_two = norm_rows(residual, gain_two).astype(jnp.bfloat16)
    up_mat, down_mat, up_b_all, down_a_all = (
        lax.all_gather(w_up, "tensor", axis=1, tiled=True),
        lax.all_gather(w_down, "tensor", axis=0, tiled=True),
        lax.all_gather(up_b, "tensor", axis=1, tiled=True),
        lax.all_gather(down_a, "tensor", axis=2, tiled=True),
    )
    up_b_sel = select_rows(onehot, up_b_all)
    down_a_sel = select_rows(onehot, down_a_all)
    rank_up, preact, hidden, rank_down, ffn_terms = ffn_forward(
        normed_two, up_mat, down_mat, up_a_sel, up_b_sel, down_a_sel, down_b_sel
    )
    layer_out = ((residual + scale_two * ffn_terms) * row_valid).astype(jnp.bfloat16)
    grad_out = cotangent.astype(jnp.float32) * row_valid
    grad_mlp = (scale_two * grad_out).astype(jnp.bfloat16)
    ffn_grad_in, ffn_grads = ffn_backward(
        normed_two,
        grad_mlp,
        up_mat,
        down_mat,
        up_a_sel,
        up_b_sel,
        down_a_sel,
        down_b_sel,
        rank_up,
        preact,
        hidden,
        rank_down,
    )
    grad_residual = grad_out + norm_back(residual, gain_two, ffn_grad_in)
    grad_attn = (scale_one * grad_residual).astype(jnp.bfloat16)
    full_grad_attn = lax.all_gather(grad_attn, "tensor", axis=1, tiled=True)
    grad_rank_out = product("std,sdr->str", full_grad_attn, out_b_sel).astype(jnp.bfloat16)
    grad_mixed = (
        product("std,fd->stf", full_grad_attn, w_out)
        + product("str,srf->stf", grad_rank_out, out_a_sel)
    ).astype(jnp.bfloat16)
    grad_out_a = product("str,stf->srf", grad_rank_out, mixed)
    grad_out_b = precise("std,str->sdr", full_grad_attn, rank_out)

    def attend_back(slot_items):
        slot_block, valid_keys, log_rows, grad_rows = slot_items
        queries = split_heads(slot_block[0])
        keyrows = split_heads(slot_block[1])
        values = split_heads(slot_block[2])
        scores = masked_scores(queries, keyrows, valid_keys)
        soft = jnp.exp(scores - log_rows[:, :, None])
        soft_low = soft.astype(jnp.bfloat16)
        grad_heads = split_heads(grad_rows)
        grad_soft = product("qhe,khe->hqk", grad_heads, values)
        grad_values = product("hqk,qhe->khe", soft_low, grad_heads)
        grad_scores = (
            soft * (grad_soft - jnp.sum(soft * grad_soft, axis=-1, keepdims=True))
        ).astype(jnp.bfloat16)
        grad_queries = product("hqk,khe->qhe", grad_scores, keyrows) * scale_attn
        grad_keys = product("hqk,qhe->khe", grad_scores, queries) * scale_attn
        return (
            jnp.stack([grad_queries, grad_keys, grad_values])
            .reshape(3, seq_len, -1)
            .astype(jnp.bfloat16)
        )

    grad_projected = lax.map(attend_back, (projected, key_valid, log_total, grad_mixed))
    grad_qkv_b = product("sctf,str->scfr", grad_projected, rank_qkv)
    grad_rank_qkv = product("sctf,scfr->str", grad_projected, qkv_b_sel)
    grad_one_terms = product("sctf,dcf->std", grad_projected, w_qkv) + precise(
        "str,srd->std", grad_rank_qkv, qkv_a_sel
    )
    grad_qkv_a = precise("str,std->srd", grad_rank_qkv, full_one)
    grad_normed_one = lax.psum_scatter(grad_one_terms, "tensor", scatter_dimension=1, tiled=True)
    grad_tokens = grad_residual + norm_back(inputs, gain_one, grad_normed_one)
    onehot_wide = onehot.astype(jnp.float32)

    def stack_slots(slot_grads):
        return jnp.einsum("sn,s...->n...", onehot_wide, slot_grads, precision=HIGHEST)

    grad_up_a, grad_up_b, grad_down_a, grad_down_b = ffn_grads
    sum_qkv_b, sum_out_a = lax.psum((stack_slots(grad_qkv_b), stack_slots(grad_out_a)), "dp")
    joint_sums = lax.psum(
        (
            stack_slots(grad_qkv_a),
            stack_slots(grad_out_b),
            stack_slots(grad_up_a),
            stack_slots(grad_up_b),
            stack_slots(grad_down_a),
            stack_slots(grad_down_b),
        ),
        ("dp", "tensor"),
    )
    sum_qkv_a, sum_out_b, sum_up_a, up_b_whole, down_a_whole, sum_down_b = joint_sums
    width_local = w_up.shape[1]
    first_col = lax.axis_index("tensor") * width_local
    sum_up_b = lax.dynamic_slice_in_dim(up_b_whole, first_col, width_local, 1)
    sum_down_a = lax.dynamic_slice_in_dim(down_a_whole, first_col, width_local, 2)
    return (
        layer_out,
        grad_tokens,
        sum_qkv_a,
        sum_qkv_b,
        sum_out_a,
        sum_out_b,
        sum_up_a,
        sum_up_b,
        sum_down_a,
        sum_down_b,
    )


F32 = jnp.float32
BF = jnp.bfloat16
LOG2E = 1.4426950408889634
PARTS = 8
PAD = 128
FLIP = [(0, 1), (1, 0)]
SWAP = [(1, 2), (2, 1)]


def dotg(a, b, ca, cb):
    return lax.dot_general(a, b, (((ca,), (cb,)), ((), ())), preferred_element_type=F32)


def pad_rows(table):
    rank, width = table.shape
    return jnp.concatenate([table, jnp.zeros((PAD - rank, width), table.dtype)], axis=0)


def pad_twice(table):
    rank, width = table.shape
    return jnp.concatenate([table, table, jnp.zeros((PAD - 2 * rank, width), table.dtype)], axis=0)


def two_terms(wide, rank):
    high = wide.astype(BF).astype(F32)
    return (high + pltpu.roll(wide - high, rank, 1)).astype(BF)


def three_terms(wide):
    high = wide.astype(BF)
    rest = wide - high.astype(F32)
    middle = rest.astype(BF)
    return high, middle, (rest - middle.astype(F32)).astype(BF)


def whole():
    return pl.BlockSpec(memory_space=pltpu.VMEM)


def in_place():
    return pl.BlockSpec(memory_space=pl.ANY)


def scalars():
    return pl.BlockSpec(memory_space=pltpu.SMEM)


def params(mib=58, **more):
    return pltpu.CompilerParams(vmem_limit_bytes=mib * 2**20, **more)


def cost(flops, nbytes):
    return pl.CostEstimate(flops=int(flops * 0.25), bytes_accessed=int(nbytes * 0.025), transcendentals=0)


def norm_stats(values):
    average = jnp.mean(values, axis=-1, keepdims=True)
    centred = values - average
    scale = lax.rsqrt(jnp.mean(centred * centred, axis=-1, keepdims=True) + epsilon)
    return centred * scale, scale


def norm_grad(unit, scale, grad):
    return scale * (
        grad
        - jnp.mean(grad, axis=-1, keepdims=True)
        - unit * jnp.mean(grad * unit, axis=-1, keepdims=True)
    )


def row_mask(scal, rows):
    at = lax.broadcasted_iota(jnp.int32, (rows, 1), 0) + scal[1] * rows
    return (at < scal[0]).astype(F32)


def choose(scal, here, swapped, target, sem):
    @pl.when(scal[3] != 0)
    def _():
        pltpu.make_async_copy(here, target, sem).start()

    @pl.when(scal[3] == 0)
    def _():
        pltpu.make_async_copy(swapped, target, sem).start()

    return pltpu.make_async_copy(here, target, sem)


def fetch(arrays, nears, target, sem, part_at, axis, size):
    copies = []
    parts = len(nears)
    for number, near in enumerate(nears):
        first = pl.multiple_of(((part_at % parts) ^ near) * size, size)
        place = target.at[:, pl.ds(first, size)] if axis == 1 else target.at[pl.ds(first, size)]
        copies.append(pltpu.make_async_copy(arrays[number // 2].at[number % 2], place, sem.at[near]))
    for copy in copies:
        copy.start()
    return copies


def qkv_local_kernel(scal, here, swapped, gain, w, qa, qb, tok, n1, rank, queries, rest, low, sem):
    step = pl.program_id(0)

    @pl.when(step == 0)
    def _():
        choose(scal, here, swapped, tok, sem.at[0]).wait()
        unit, _ = norm_stats(tok[...].astype(F32))
        normed = (unit * gain[...]).astype(BF)
        n1[...] = normed
        ranked = dotg(normed, pad_rows(qa[...]), 1, 1).astype(BF)
        rank[...] = ranked
        low[...] = ranked

    out = (dotg(n1[...], w[0], 1, 0) + dotg(low[...], pad_rows(qb[...]), 1, 0)).astype(BF)

    @pl.when(step < 2)
    def _():
        rest[0] = out

    @pl.when(step == 2)
    def _():
        queries[...] = out


def qkv_local(scal, tok, swapped, gain, w, qa, qb):
    rows, width = tok.shape
    third = w.shape[2]
    rank = qa.shape[0]
    fixed = lambda c: (0, 0)
    return pl.pallas_call(
        qkv_local_kernel,
        grid=(3,),
        in_specs=[
            scalars(),
            in_place(),
            in_place(),
            pl.BlockSpec((1, width), fixed),
            pl.BlockSpec((1, width, third), lambda c: ((c + 1) % 3, 0, 0)),
            pl.BlockSpec((rank, width), fixed),
            pl.BlockSpec((rank, third), lambda c: (0, (c + 1) % 3)),
        ],
        out_specs=[
            pl.BlockSpec((rows, width), fixed),
            pl.BlockSpec((rows, width), fixed),
            pl.BlockSpec((rows, PAD), fixed),
            pl.BlockSpec((rows, third), fixed),
            pl.BlockSpec((1, rows, third), lambda c: (jnp.minimum(c, 1), 0, 0)),
        ],
        out_shape=[
            jax.ShapeDtypeStruct((rows, width), BF),
            jax.ShapeDtypeStruct((rows, width), BF),
            jax.ShapeDtypeStruct((rows, PAD), BF),
            jax.ShapeDtypeStruct((rows, third), BF),
            jax.ShapeDtypeStruct((2, rows, third), BF),
        ],
        scratch_shapes=[pltpu.VMEM((rows, PAD), BF), pltpu.SemaphoreType.DMA((1,))],
        compiler_params=params(dimension_semantics=("arbitrary",)),
        cost_estimate=cost(1e-7 * 1e15, 1e5),
        name="qkv_local",
    )(scal, tok, swapped, gain, w, qa, qb)


def qkv_other_kernel(nears, scal, n1, rank, qb, *rest):
    arrays, (queries, out, w, sem) = rest[: len(nears) // 2], rest[len(nears) // 2 :]
    third = w.shape[2]
    copies = fetch(arrays, nears, w, sem, scal[2], 1, arrays[0].shape[2])
    for copy in copies:
        copy.wait()
    for c in (1, 2, 0):
        at = slice(c * third, (c + 1) * third)
        terms = (dotg(n1[...], w[c], 1, 0) + dotg(rank[...], pad_rows(qb[:, at]), 1, 0)).astype(BF)
        if c == 0:
            queries[...] = terms
        else:
            out[c - 1] = terms


def qkv_other(scal, n1, rank, qb, half):
    rows, width = n1.shape
    arrays, nears = half.pairs, half.names
    third = arrays[0].shape[3]
    return pl.pallas_call(
        functools.partial(qkv_other_kernel, nears),
        in_specs=[scalars(), whole(), whole(), whole()] + [in_place()] * len(arrays),
        out_specs=[whole()] * 3,
        out_shape=[
            jax.ShapeDtypeStruct((rows, third), BF),
            jax.ShapeDtypeStruct((2, rows, third), BF),
            jax.ShapeDtypeStruct((3, width, third), BF),
        ],
        scratch_shapes=[pltpu.SemaphoreType.DMA((PARTS,))],
        compiler_params=params(),
        cost_estimate=cost(7e-6 * 1e15, 10e6),
        name="qkv_other",
    )(scal, n1, rank, qb, *arrays)


def lane_numbers(rows):
    return lax.broadcasted_iota(jnp.int32, (rows, 2 * HD), 1)


def key_fill(scal, rows, other, ones):
    side = 1 - scal[1] if other else scal[1]
    lanes = lane_numbers(rows) % HD
    at = lax.broadcasted_iota(jnp.int32, (rows, 2 * HD), 0) + side * rows
    bias = jnp.where(at < jnp.maximum(scal[0], 1), 0.0, masked_score)
    return jnp.where(lanes < ones, 1.0, jnp.where(lanes == ones, bias, 0.0)).astype(BF)


def lane_terms(wide, rows, with_one):
    lanes = lane_numbers(rows) % HD
    first, second, third = three_terms(wide)
    filled = jnp.where(lanes == 2, third, jnp.full_like(third, 0.0))
    if with_one:
        filled = jnp.where(lanes == 3, jnp.full_like(third, 1.0), filled)
    return jnp.where(lanes == 0, first, jnp.where(lanes == 1, second, filled))


def attend_kernel(scal, q_ref, k_ref, v_ref, ko_ref, vo_ref, out, log_out, qx, kx, vt):
    rows = q_ref.shape[0]
    queries = (q_ref[...].astype(F32) * HD**-0.5).astype(BF)
    lanes = lane_numbers(rows)
    low_half = lanes < HD
    ones = (lanes % HD == 0).astype(BF)
    fills = [key_fill(scal, rows, side == 1, 0) for side in range(2)]
    for head in range(2):
        own = low_half if head == 0 else ~low_half
        qx[head] = jnp.where(own, queries, ones)
        for side, ref in enumerate((k_ref, ko_ref)):
            kx[head, side * rows : (side + 1) * rows] = jnp.where(own, ref[0], fills[side])
    for side, ref in enumerate((v_ref, vo_ref)):
        at = slice(side * rows, (side + 1) * rows)
        turned = ref[0].T
        for head in range(2):
            vt[head, 0:HD, at] = turned[head * HD : (head + 1) * HD]
            vt[head, HD : HD + 16, at] = jnp.ones((16, rows), BF)

    def scores(head):
        return dotg(kx[head], qx[head], 1, 1)

    ahead = scores(0)
    mixed, logs = [], []
    for head in range(2):
        now = ahead
        if head == 0:
            ahead = scores(1)
        top = jnp.max(now, axis=0, keepdims=True)
        soft = jnp.exp(now - top).astype(BF)
        terms = dotg(vt[head], soft, 1, 0)
        total = terms[HD : HD + 1]
        mixed.append(terms[0:HD] / total)
        logs.append(jnp.broadcast_to(top + jnp.log(total), (HD, total.shape[1])))
    out[...] = jnp.concatenate(mixed, axis=0).T.astype(BF)
    log_out[...] = jnp.concatenate([logs[1], logs[0]], axis=0).T


def attend(scal, queries, own, other):
    _, rows, width = own.shape
    pairs = width // (2 * HD)
    take = lambda c: pl.BlockSpec((1, rows, 2 * HD), lambda p: (c, 0, p))
    flat = pl.BlockSpec((rows, 2 * HD), lambda p: (0, p))
    return pl.pallas_call(
        attend_kernel,
        grid=(pairs,),
        in_specs=[scalars(), flat, take(0), take(1), take(0), take(1)],
        out_specs=[flat, flat],
        out_shape=[jax.ShapeDtypeStruct((rows, width), BF), jax.ShapeDtypeStruct((rows, width), F32)],
        scratch_shapes=[
            pltpu.VMEM((2, rows, 2 * HD), BF),
            pltpu.VMEM((2, 2 * rows, 2 * HD), BF),
            pltpu.VMEM((2, HD + 16, 2 * rows), BF),
        ],
        compiler_params=params(dimension_semantics=("arbitrary",)),
        cost_estimate=cost(16e-6 * 1e15, 6e6),
        name="attend",
    )(scal, queries, own, own, other, other)


def attend_back_kernel(
    scal, q_ref, k_ref, v_ref, ko_ref, vo_ref, mixed_ref, grad_ref, log_ref, queries_out, own_out, other_out,
    qx, gx, qm, gm, kx, vx, kt,
):
    rows = q_ref.shape[0]
    queries, grad = q_ref[...], grad_ref[...]
    zero = jnp.zeros_like(queries)
    low_half = lane_numbers(rows) < HD
    scaled = (queries.astype(F32) * HD**-0.5).astype(BF)
    weighed = grad.astype(F32) * mixed_ref[...].astype(F32)
    high = weighed.astype(BF)
    pair = jnp.concatenate([high, (weighed - high.astype(F32)).astype(BF)], axis=1)
    down = lax.broadcasted_iota(jnp.int32, (4 * HD, 2 * HD), 0) // HD % 2
    across = lax.broadcasted_iota(jnp.int32, (4 * HD, 2 * HD), 1) // HD
    sums = dotg(pair, (down != across).astype(BF), 1, 0)
    query_fill = lane_terms(-log_ref[...], rows, True)
    grad_fill = lane_terms(-sums, rows, False)
    fills = [key_fill(scal, rows, side == 1, 3) for side in range(2)]
    value_fill = (lane_numbers(rows) % HD < 3).astype(BF)
    for head in range(2):
        own = low_half if head == 0 else ~low_half
        qx[head] = jnp.where(own, scaled, query_fill)
        gx[head] = jnp.where(own, grad, grad_fill)
        qm[head] = jnp.where(own, queries, zero)
        gm[head] = jnp.where(own, grad, zero)
        for side, (key_ref, value_ref) in enumerate(((k_ref, v_ref), (ko_ref, vo_ref))):
            at = slice(side * rows, (side + 1) * rows)
            kx[head, at] = jnp.where(own, key_ref[0], fills[side])
            vx[head, at] = jnp.where(own, value_ref[0], value_fill)
    for side, ref in enumerate((k_ref, ko_ref)):
        kt[:, side * rows : (side + 1) * rows] = ref[0].T
    steps = [(side, head) for side in range(2) for head in range(2)]

    def first(side, head):
        at = slice(side * rows, (side + 1) * rows)
        return dotg(kx[head, at], qx[head], 1, 1), dotg(vx[head, at], gx[head], 1, 1)

    ahead = first(*steps[0])
    grad_queries = [0.0, 0.0]
    kept = None
    for number, (side, head) in enumerate(steps):
        scores, grad_soft = ahead
        if number + 1 < len(steps):
            ahead = first(*steps[number + 1])
        soft = jnp.exp(scores)
        grad_scores = (soft * grad_soft).astype(BF)
        values = dotg(soft.astype(BF), gm[head], 1, 0)
        keys = dotg(grad_scores, qm[head], 1, 0)
        at = slice(side * rows, (side + 1) * rows)
        grad_queries[head] += dotg(kt[head * HD : (head + 1) * HD, at], grad_scores, 1, 0)
        if head == 0:
            kept = (keys, values)
        else:
            keys = ((kept[0] + keys) * HD**-0.5).astype(BF)
            values = (kept[1] + values).astype(BF)
            out = own_out if side == 0 else other_out
            out[0], out[1] = keys, values
    queries_out[...] = (jnp.concatenate(grad_queries, axis=0).T * HD**-0.5).astype(BF)


def attend_back(scal, queries, own, other, mixed, grad, logs, piece, pieces):
    _, rows, width = own.shape
    width = width // pieces
    pairs = width // (2 * HD)
    skip = piece * pairs
    take = lambda c: pl.BlockSpec((1, rows, 2 * HD), lambda p: (c, 0, p + skip))
    flat = pl.BlockSpec((rows, 2 * HD), lambda p: (0, p + skip))
    both = jax.ShapeDtypeStruct((2, rows, width), BF)
    return pl.pallas_call(
        attend_back_kernel,
        grid=(pairs,),
        in_specs=[scalars(), flat, take(0), take(1), take(0), take(1), flat, flat, flat],
        out_specs=[
            pl.BlockSpec((rows, 2 * HD), lambda p: (0, p)),
            pl.BlockSpec((2, rows, 2 * HD), lambda p: (0, 0, p)),
            pl.BlockSpec((2, rows, 2 * HD), lambda p: (0, 0, p)),
        ],
        out_shape=[jax.ShapeDtypeStruct((rows, width), BF), both, both],
        scratch_shapes=[pltpu.VMEM((2, rows, 2 * HD), BF)] * 4
        + [pltpu.VMEM((2, 2 * rows, 2 * HD), BF)] * 2
        + [pltpu.VMEM((2 * HD, 2 * rows), BF)],
        compiler_params=params(dimension_semantics=("arbitrary",)),
        cost_estimate=cost(26e-6 / pieces * 1e15, 9e6),
        name="attend_back",
    )(scal, queries, own, own, other, other, mixed, grad, logs)


def branch_kernel(nears, scal, mix_a, mix_b, tok, w_a, oa_a, oa_b, obs, scale_one, gain_two, uas, *rest):
    arrays = rest[: len(nears) // 2]
    residual, n2, rank_out, rank_up, w_b, sem = rest[len(nears) // 2 :]
    rank = oa_a.shape[0]
    ob, ua = obs[scal[4]], uas[scal[4]]

    @pl.when(pl.program_id(0) == 0)
    def _():
        for copy in fetch(arrays, nears, w_b, sem, scal[2], 0, arrays[0].shape[1]):
            copy.wait()

    ranked = dotg(mix_a[...], pad_rows(oa_a[...]), 1, 1) + dotg(mix_b[...], pad_rows(oa_b[:, -oa_a.shape[1] :]), 1, 1)
    ranked = two_terms(ranked, rank)
    rank_out[...] = ranked
    terms = dotg(mix_a[...], w_a[...], 1, 0) + dotg(mix_b[...], w_b[...], 1, 0)
    terms = terms + dotg(ranked, pad_twice(ob), 1, 0)
    total = tok[...].astype(F32) + scale_one[...] * terms
    residual[...] = total.astype(BF)
    unit, _ = norm_stats(total)
    normed = (unit * gain_two[...]).astype(BF)
    n2[...] = normed
    rank_up[...] = dotg(normed, pad_rows(ua), 1, 1).astype(BF)


def blocked(rows, width):
    return pl.BlockSpec((rows, width), lambda step: (step, 0))


def fixed_block(*shape):
    return pl.BlockSpec(shape, lambda step: (0,) * len(shape))


def branch(scal, mix_a, mix_b, tok, w_a, half, oa_a, oa_b, ob, scale_one, gain_two, ua):
    rows, width = tok.shape
    heads = mix_a.shape[1]
    block = rows // 2
    arrays, nears = half.pairs, half.names
    return pl.pallas_call(
        functools.partial(branch_kernel, nears),
        grid=(2,),
        in_specs=[scalars(), blocked(block, heads), blocked(block, heads), blocked(block, width)]
        + [fixed_block(*array.shape) for array in (w_a, oa_a, oa_b, ob, scale_one, gain_two, ua)]
        + [in_place()] * len(arrays),
        out_specs=[blocked(block, width), blocked(block, width), blocked(block, PAD), blocked(block, PAD)]
        + [fixed_block(*w_a.shape)],
        out_shape=[
            jax.ShapeDtypeStruct((rows, width), BF),
            jax.ShapeDtypeStruct((rows, width), BF),
            jax.ShapeDtypeStruct((rows, PAD), BF),
            jax.ShapeDtypeStruct((rows, PAD), BF),
            jax.ShapeDtypeStruct(w_a.shape, BF),
        ],
        scratch_shapes=[pltpu.SemaphoreType.DMA((PARTS,))],
        compiler_params=params(dimension_semantics=("arbitrary",)),
        cost_estimate=cost(8e-6 * 1e15, 16e6),
        name="branch",
    )(scal, mix_a, mix_b, tok, w_a, oa_a, oa_b, ob, scale_one, gain_two, ua, *arrays)


def mlp_kernel(nears, counts, step, more, *refs):
    scal, n2, rank_up, ub, da = refs[:5]
    ups, downs, rest = refs[5 : 5 + counts[0]], refs[5 + counts[0] : 5 + sum(counts)], refs[5 + sum(counts) :]
    if nears is None:
        cot, scale_two, dbs, grad_mlp, grad_rank = rest[:5]
        earlier, rest = (), rest[5:]
        ub, da, db = (table.at[scal[4]] for table in (ub, da, dbs))
    else:
        grad_mlp, grad_rank = rest[:2]
        earlier, rest = rest[2 : 2 + more], rest[2 + more :]
    m_out, g_out, rd_out, gru_out, gub_out, gda_out = rest[:6]
    wu, wd, ubs, das, hidden, grad_pre, sem = rest[6:]
    width = wu.shape[1]
    rank = ub.shape[0]
    size = gub_out.shape[1] // PARTS
    pieces = width // size
    chunks = width // step
    waits = [[] for _ in range(chunks)]
    for piece in range(pieces):
        at = pl.ds(piece * size, size)
        if nears is None:
            sources = ups[0].at[:, at], downs[0].at[at]
        else:
            last = counts[0] - 1
            sources = ups[piece] if piece < last else ups[last].at[piece - last], downs[piece]
        for which, (source, target) in enumerate(zip(sources, (wu.at[:, at], wd.at[at]))):
            copy = pltpu.make_async_copy(source, target, sem.at[which, piece])
            copy.start()
            waits[piece * size // step].append(copy)
    def place(piece, first=0):
        if nears is None:
            return pl.ds(piece * size, size)
        return pl.ds(pl.multiple_of((scal[2] ^ nears[piece]) * size + first, size), size)

    if nears is None:
        grad_low = (scale_two[...] * (cot[...].astype(F32) * row_mask(scal, cot.shape[0]))).astype(BF)
        grad_mlp[...] = grad_low
        grad_rank[...] = dotg(grad_low, pad_rows(db[...]), 1, 1).astype(BF)
    ubs[...] = jnp.zeros_like(ubs)
    das[...] = jnp.zeros_like(das)
    for piece in range(pieces):
        at = slice(piece * size, (piece + 1) * size)
        ubs[0:rank, at] = ub[:, place(piece)]
        das[0:rank, at] = da[:, place(piece, da.shape[1] // 2)]
    up_turned = rank_up[...].T[0:rank]
    grad_turned = grad_rank[...].T[0:rank]

    def first(k):
        for copy in waits[k]:
            copy.wait()
        at = slice(k * step, (k + 1) * step)
        return (
            dotg(n2[...], wu[:, at], 1, 0) + dotg(rank_up[...], ubs[:, at], 1, 0),
            dotg(grad_mlp[...], wd[at, :], 1, 1) + dotg(grad_rank[...], das[:, at], 1, 0),
        )

    ahead = first(0)
    for k in range(chunks):
        at = slice(k * step, (k + 1) * step)
        preact, grad_hidden = ahead
        if k + 1 < chunks:
            ahead = first(k + 1)
        cdf = 0.5 * (1.0 + lax.erf(preact * 0.7071067811865476))
        hidden[:, at] = (preact * cdf).astype(BF)
        slope = cdf + preact * jnp.exp(-0.5 * preact * preact) * 0.3989422804014327
        grad_pre[:, at] = (grad_hidden * slope).astype(BF)
    ranked = dotg(hidden[...], das[...], 1, 1)
    grad_ranked = dotg(grad_pre[...], ubs[...], 1, 1)
    if more:
        ranked, grad_ranked = ranked + earlier[2][...], grad_ranked + earlier[3][...]
    rd_out[...] = ranked
    gru_out[...] = grad_ranked
    for piece in range(pieces):
        at = slice(piece * size, (piece + 1) * size)
        gub_out[:, place(piece)] = dotg(up_turned, grad_pre[:, at], 1, 0)
        gda_out[:, place(piece)] = dotg(grad_turned, hidden[:, at], 1, 0)
    for at in (slice(k, k + step) for k in range(0, wu.shape[0], step)):
        terms = dotg(hidden[...], wd[:, at], 1, 0)
        grad_terms = dotg(grad_pre[...], wu[at, :], 1, 1)
        if more:
            terms = terms + earlier[0][:, at].astype(F32)
            grad_terms = grad_terms + earlier[1][:, at].astype(F32)
        m_out[:, at] = terms.astype(BF)
        g_out[:, at] = grad_terms.astype(BF)


def mlp(scal, n2, rank_up, ub, da, ups, downs, grads, nears=None, earlier=()):
    rows, width = n2.shape
    rank, half = ub.shape[-2:]
    half = half if nears is None else half // 2
    units = half if nears is None else len(nears) * half // PARTS
    step = min(512, units)
    sums = jax.ShapeDtypeStruct((rows, width), BF)
    ranked = jax.ShapeDtypeStruct((rows, PAD), F32)
    table = jax.ShapeDtypeStruct((rank, half), F32)
    low = jax.ShapeDtypeStruct((rows, width), BF)
    first = [low, jax.ShapeDtypeStruct((rows, PAD), BF)] if nears is None else []
    return pl.pallas_call(
        functools.partial(mlp_kernel, nears, (len(ups), len(downs)), step, len(earlier)),
        in_specs=[scalars()]
        + [whole()] * 4
        + [in_place()] * (len(ups) + len(downs))
        + [whole()] * (len(grads) + len(earlier)),
        out_specs=[whole()] * (len(first) + 6),
        out_shape=first + [sums, sums, ranked, ranked, table, table],
        scratch_shapes=[
            pltpu.VMEM((width, units), BF),
            pltpu.VMEM((units, width), BF),
            pltpu.VMEM((PAD, units), BF),
            pltpu.VMEM((PAD, units), BF),
            pltpu.VMEM((rows, units), BF),
            pltpu.VMEM((rows, units), BF),
            pltpu.SemaphoreType.DMA((2, PARTS)),
        ],
        compiler_params=params(),
        cost_estimate=cost(25e-6 * units / half * 1e15, 20e6),
        name="mlp",
    )(scal, n2, rank_up, ub, da, *ups, *downs, *grads, *earlier)


def middle_kernel(
    scal, residual, m_in, g_in, rd, gru, cot, mix_a, mix_b, rank_out, n2, grad_mlp,
    dbs, uas, scale_two, gain_two, scale_one, w_a, w_b, oa_a, oa_b, obs,
    layer, grad_res, grad_a, grad_b, goa_a, goa_b, gob, gua, gdb,
):
    step = pl.program_id(0)
    rows = residual.shape[0]
    db, ua, ob = dbs[scal[4]], uas[scal[4]], obs[scal[4]]
    rank = db.shape[0]
    at = lax.broadcasted_iota(jnp.int32, (rows, 1), 0) + (scal[1] * pl.num_programs(0) + step) * rows
    valid = (at < scal[0]).astype(F32)
    down = two_terms(rd[...], rank)
    up = two_terms(gru[...], rank)

    def add(out, terms):
        @pl.when(step == 0)
        def _():
            out[...] = terms

        @pl.when(step > 0)
        def _():
            out[...] += terms

    def turned(terms, right):
        both = dotg(terms.T[0 : 2 * rank], right, 1, 0)
        return both[0:rank] + both[rank : 2 * rank]

    branch_out = m_in[...].astype(F32) + dotg(down, pad_twice(db), 1, 0)
    total = residual[...].astype(F32)
    layer[...] = ((total + scale_two[...] * branch_out) * valid).astype(BF)
    add(gua, turned(up, n2[...]))
    add(gdb, turned(down, grad_mlp[...]))
    unit, scale = norm_stats(total)
    grad_normed = (g_in[...].astype(F32) + dotg(up, pad_twice(ua), 1, 0)) * gain_two[...]
    grad_total = cot[...].astype(F32) * valid + norm_grad(unit, scale, grad_normed)
    grad_res[...] = grad_total.astype(BF)
    grad_attn = (scale_one[...] * grad_total).astype(BF)
    grad_rank = dotg(grad_attn, pad_rows(ob), 1, 1).astype(BF)
    grad_a[...] = (
        dotg(grad_attn, w_a[...], 1, 1) + dotg(grad_rank, pad_rows(oa_a[...]), 1, 0)
    ).astype(BF)
    grad_b[...] = (
        dotg(grad_attn, w_b[...], 1, 1) + dotg(grad_rank, pad_rows(oa_b[:, -oa_a.shape[1] :]), 1, 0)
    ).astype(BF)
    rank_turned = grad_rank.T[0:rank]
    add(goa_a, dotg(rank_turned, mix_a[...], 1, 0))
    add(goa_b, dotg(rank_turned, mix_b[...], 1, 0))
    add(gob, turned(rank_out[...], grad_attn))


def middle(scal, by_rows, others, blocks=1):
    rows, width = by_rows[0].shape
    block = rows // blocks
    heads = by_rows[6].shape[1]
    rank = others[0].shape[1]
    part = jax.ShapeDtypeStruct((rows, heads), BF)
    table = jax.ShapeDtypeStruct((rank, width), F32)
    half_table = jax.ShapeDtypeStruct((rank, heads), F32)
    return pl.pallas_call(
        middle_kernel,
        grid=(blocks,),
        in_specs=[scalars()]
        + [blocked(block, array.shape[1]) for array in by_rows]
        + [fixed_block(*array.shape) for array in others],
        out_specs=[blocked(block, width), blocked(block, width), blocked(block, heads), blocked(block, heads)]
        + [fixed_block(*shape) for shape in ((rank, heads),) * 2 + ((rank, width),) * 3],
        out_shape=[jax.ShapeDtypeStruct((rows, width), BF)] * 2
        + [part, part, half_table, half_table, table, table, table],
        compiler_params=params(dimension_semantics=("arbitrary",)),
        cost_estimate=cost(9e-6 * 1e15, 20e6),
        name="middle",
    )(scal, *by_rows, *others)


def columns_of(pieces):
    first = 0
    for piece in pieces:
        yield piece, slice(first, first + piece.shape[-1])
        first += piece.shape[-1]


def qkv_tables_kernel(counts, *refs):
    sides = []
    for count in counts:
        sides.append((refs[:count], refs[count : 2 * count], refs[2 * count : 3 * count]))
        refs = refs[3 * count :]
    scal, qb_a, qb_b, n1, rank_in, total_a, total_b, rank_out, kept, sent, gqb_a, gqb_b, gqa = refs
    rank = qb_a.shape[0]
    third = qb_a.shape[1] // 3
    rank_turned = rank_in[...].T[0:rank]
    ranked = None
    for side, qb, total, table in zip(sides, (qb_a, qb_b), (total_a, total_b), (gqb_a, gqb_b)):
        queries, owns, gots = side
        for (piece, at), own, got in zip(columns_of(queries), owns, gots):
            for c in range(3):
                if c == 0:
                    grad = piece[...]
                else:
                    grad = (own[c - 1].astype(F32) + got[c - 1].astype(F32)).astype(BF)
                    total[c - 1, :, at] = grad
                place = slice(c * third + at.start, c * third + at.stop)
                table[:, place] = dotg(rank_turned, grad, 1, 0)
                terms = dotg(grad, pad_rows(qb[:, place]), 1, 1)
                ranked = terms if ranked is None else ranked + terms
    ranked = two_terms(ranked, rank)
    rank_out[...] = ranked
    both = dotg(ranked.T[0 : 2 * rank], n1[...], 1, 0)
    gqa[...] = both[0:rank] + both[rank : 2 * rank]
    first = 0
    for table in (gqb_a, gqa, gqb_b):
        half = table.shape[1] // 2
        at = slice(first, first + half)
        kept[:, at] = table[:, pl.ds(pl.multiple_of(scal[1] * half, half), half)]
        sent[:, at] = table[:, pl.ds(pl.multiple_of((1 - scal[1]) * half, half), half)].astype(BF)
        first += half


def qkv_tables(scal, side_a, side_b, qb_a, qb_b, n1, rank_in):
    rows, width = n1.shape
    rank, columns = qb_a.shape
    pieces = [piece for side in (side_a, side_b) for group in side for piece in group]
    total = jax.ShapeDtypeStruct((2, rows, columns // 3), BF)
    share = columns + width // 2
    return pl.pallas_call(
        functools.partial(qkv_tables_kernel, (len(side_a[0]), len(side_b[0]))),
        in_specs=[whole()] * len(pieces) + [scalars()] + [whole()] * 4,
        out_specs=[whole()] * 5,
        out_shape=[total, total, jax.ShapeDtypeStruct((rows, PAD), BF)]
        + [jax.ShapeDtypeStruct((rank, share), F32), jax.ShapeDtypeStruct((rank, share), BF)],
        scratch_shapes=[pltpu.VMEM((rank, columns), F32)] * 2 + [pltpu.VMEM((rank, width), F32)],
        compiler_params=params(),
        cost_estimate=cost(7e-6 * 1e15, 14e6),
        name="qkv_tables",
    )(*pieces, scal, qb_a, qb_b, n1, rank_in)


def qkv_rows_kernel(count_a, count_b, *refs):
    grads_a, grads_b, refs = refs[:count_a], refs[count_a : count_a + count_b], refs[count_a + count_b :]
    w_a, w_b, ranked, qa, tok, gain, grad_res, out = refs
    grad = dotg(ranked[...], pad_twice(qa[...]), 1, 0)
    for grads, w in ((grads_a, w_a), (grads_b, w_b)):
        for piece, at in columns_of(grads[:-1]):
            grad = grad + dotg(piece[...], w[0, :, at], 1, 1)
        for c in (1, 2):
            grad = grad + dotg(grads[-1][c - 1], w[c], 1, 1)
    unit, scale = norm_stats(tok[...].astype(F32))
    out[...] = (grad_res[...].astype(F32) + norm_grad(unit, scale, grad * gain[...])).astype(BF)


def qkv_rows(block_at, blocks, grads_a, grads_b, w_a, w_b, ranked, qa, tok, gain, grad_res):
    rows, width = tok.shape
    block = rows // blocks
    flat = lambda array: pl.BlockSpec((block, array.shape[1]), lambda step: (block_at, 0))
    deep = lambda array: pl.BlockSpec((2, block, array.shape[2]), lambda step: (0, block_at, 0))
    specs = [flat(array) if array.ndim == 2 else deep(array) for array in grads_a + grads_b]
    return pl.pallas_call(
        functools.partial(qkv_rows_kernel, len(grads_a), len(grads_b)),
        grid=(1,),
        in_specs=specs
        + [whole(), whole(), flat(ranked), whole(), flat(tok), whole(), flat(grad_res)],
        out_specs=whole(),
        out_shape=jax.ShapeDtypeStruct((block, width), BF),
        compiler_params=params(),
        cost_estimate=cost(12e-6 / blocks * 1e15, 16e6 / blocks),
        name="qkv_rows",
    )(*grads_a, *grads_b, w_a, w_b, ranked, qa, tok, gain, grad_res)


def gather_kernel(has_ids, flag, *refs):
    ids, (own, got, out, ids_out, total) = refs[0], refs[has_ids:]
    columns = out.shape[2]
    half = own.shape[0]
    total[...] = jnp.zeros_like(total)

    def add(first, images):
        for image in range(half):
            if has_ids:
                adapter = ids[first + image]
            else:
                note = images[image, 0:8, columns : columns + PAD].astype(F32)
                adapter = jnp.max(note).astype(jnp.int32)
            ids_out[first + image] = adapter
            total[adapter] += images[image, :, 0:columns].astype(F32)

    @pl.when(flag[0] == 0)
    def _():
        add(0, own)
        add(half, got)

    @pl.when(flag[0] != 0)
    def _():
        add(0, got)
        add(half, own)

    out[...] = total[...].astype(BF)


def gather_images(flag, ids, pair, adapters, columns):
    count, rank, _ = pair[0].shape
    given = [] if ids is None else [ids]
    return pl.pallas_call(
        functools.partial(gather_kernel, len(given)),
        in_specs=[scalars()] * (1 + len(given)) + [whole()] * 2,
        out_specs=[whole(), scalars()],
        out_shape=[
            jax.ShapeDtypeStruct((adapters, rank, columns), BF),
            jax.ShapeDtypeStruct((2 * count,), jnp.int32),
        ],
        scratch_shapes=[pltpu.VMEM((adapters, rank, columns), F32)],
        compiler_params=params(),
        cost_estimate=cost((20e-6 if ids is None else 1e-6) * 1e15, 1e6),
        name="gather_images",
    )(flag.astype(jnp.int32)[None], *given, *pair)


def finish_kernel(cut, spans, places, core, own, other, *outs):
    def write(low, high):
        for (shared, start, stop), (number, index) in zip(spans, places):
            first = cut if shared else 0
            half = own.shape[2] - cut if shared else cut
            out = outs[number] if index is None else outs[number].at[:, index]
            middle = min(max(half - start, 0), stop - start)
            if middle > 0:
                out[:, :, 0:middle] = low[:, :, first + start : first + start + middle].astype(F32)
            if middle < stop - start:
                begin = first + start + middle - half
                out[:, :, middle : stop - start] = high[:, :, begin : first + stop - half].astype(F32)

    @pl.when(core[0] == 0)
    def _():
        write(own, other)

    @pl.when(core[0] != 0)
    def _():
        write(other, own)


def finish(core, cut, spans, places, own, other, shapes, seconds=1e-6):
    return pl.pallas_call(
        functools.partial(finish_kernel, cut, spans, places),
        in_specs=[scalars(), whole(), whole()],
        out_specs=[whole()] * len(shapes),
        out_shape=[jax.ShapeDtypeStruct(shape, F32) for shape in shapes],
        compiler_params=params(),
        cost_estimate=cost(seconds * 1e15, 1e6),
        name="finish",
    )(core, own, other)


def swap(rows):
    return lax.ppermute(rows, ("core", "tensor"), SWAP)


def flip(axis):
    return lambda array: lax.ppermute(array, axis, FLIP)


def after(value, *others):
    return lax.optimization_barrier((value, others))[0]


class OtherHalf:
    BITS = {"core": 1, "x": 2, "zb": 4}

    def __init__(self, local, axis, part_at, count):
        size = local.shape[axis] // count
        self.mine = lax.dynamic_slice_in_dim(local, (part_at % count) * size, size, axis)
        self.parts = {}
        self.nears = tuple(range(0, count, 2))

    def over_tensor(self, *others):
        self.parts[0] = flip("tensor")(after(self.mine, *others) if others else self.mine)

    def hop(self, near, axis, *others):
        part = after(self.parts[near], *others) if others else self.parts[near]
        self.parts[near ^ self.BITS[axis]] = flip(axis)(part)

    def last_hop(self):
        over_zb, over_x = jnp.split(self.parts[2], 2, axis=1)[0], jnp.split(self.parts[4], 2, axis=1)[1]
        self.parts[6] = jnp.concatenate([flip("zb")(over_zb), flip("x")(over_x)], axis=1)

    def pairs_over_cores(self, *others):
        parts = after(self.parts, *others) if others else self.parts
        even = [jnp.stack([parts[a], parts[b]]) for a, b in zip(self.nears[::2], self.nears[1::2])]
        self.pairs = even + [flip("core")(array) for array in even]
        self.names = self.nears + tuple(near + 1 for near in self.nears)


def half_columns(array, index):
    size = array.shape[1] // 2
    return lax.dynamic_slice_in_dim(array, index * size, size, 1)


def by_index(index, own, other, axis):
    return jnp.where(
        index == 0, jnp.concatenate([own, other], axis=axis), jnp.concatenate([other, own], axis=axis)
    )


class Sum:
    def __init__(self, kept, sent, cut, adapter, core, tensor):
        self.core, self.tensor, self.adapter = core, tensor, adapter
        self.kept, self.sent, self.cut = kept, sent, cut

    @staticmethod
    def shares(near, shared, far, core):
        def share(index):
            return jnp.concatenate([half_columns(array, index) for array in (near, shared, far)], axis=1)

        return share(core), share(1 - core).astype(BF)

    def over_cores(self):
        total = (self.kept + flip("core")(self.sent).astype(F32)).astype(BF)
        cut, columns = self.cut, total.shape[1] - self.cut
        note = []
        if self.adapter is not None:
            note = [jnp.broadcast_to(self.adapter.astype(BF), (total.shape[0], PAD))]
        self.mine = jnp.concatenate([total[:, :columns]] + note, axis=1)
        self.send = jnp.concatenate([total[:, columns:], total[:, cut:columns]] + note, axis=1)
        self.columns = columns

    def start_pair(self):
        self.flag, self.pair = self.tensor, (self.mine[None], flip("tensor")(self.send)[None])

    def start(self, name):
        self.images = by_index(self.flag, *self.pair, 0)
        if lax.axis_size(name) == 2:
            self.flag, self.pair = lax.axis_index(name), (self.images, flip(name)(self.images))
        else:
            images = lax.all_gather(self.images, name, axis=0, tiled=True)
            half = images.shape[0] // 2
            self.flag, self.pair = jnp.zeros((), jnp.int32), (images[:half], images[half:])

    def arrive(self, *others):
        self.pair = (self.pair[0], after(self.pair[1], *others))

    def over_adapters(self, ids, adapters):
        self.dense, ids = gather_images(self.flag, ids, self.pair, adapters, self.columns)
        self.other = flip("core")(self.dense)
        return ids

    def finish(self, spans, places, shapes, *seconds):
        core = self.core.astype(jnp.int32)[None]
        return finish(core, self.cut, spans, places, self.dense, self.other, shapes, *seconds)


def quad_body(
    tokens, cotangent, lengths, adapter_ids, gain_one, gain_two, scale_one, scale_two, w_qkv, w_out, w_up, w_down,
    qkv_a, qkv_b, out_a, out_b, up_a, up_b, down_a, down_b,
):
    core, tensor = lax.axis_index("core"), lax.axis_index("tensor")
    part_at = lax.axis_index("zb") * 4 + lax.axis_index("x") * 2 + core
    adapters, rank, width = qkv_a.shape
    third = w_qkv.shape[2]
    units = w_up.shape[1]

    w3 = jnp.swapaxes(w_qkv, 0, 1)
    half_qkv = OtherHalf(w3, 1, part_at, PARTS)
    half_out = OtherHalf(w_out, 0, part_at, 4)
    half_up = OtherHalf(w_up, 1, part_at, PARTS)
    half_down = OtherHalf(w_down, 0, part_at, PARTS)
    half_qkv.over_tensor()
    tok_here = tokens[0]
    tok_swapped = swap(tok_here)
    facts = jnp.stack([lengths[0], adapter_ids[0]])
    facts_other = flip("core")(facts)
    mine = jnp.where(core == tensor, facts, facts_other)
    theirs = jnp.where(core == tensor, facts_other, facts)
    length, adapter, adapter_other = mine[0], mine[1], theirs[1]
    scal = jnp.stack([length, core, part_at, core == tensor, adapter]).astype(jnp.int32)

    qkv_b, out_b, up_b, down_b = (jnp.swapaxes(table, -1, -2) for table in (qkv_b, out_b, up_b, down_b))
    pick = lambda table, index: lax.dynamic_index_in_dim(table, index, 0, False)
    flat = lambda table: jnp.swapaxes(table, 0, 1).reshape(rank, 3 * third)
    half_qkv.parts[0] = after(half_qkv.parts[0], half_out.mine, half_up.mine, half_down.mine)
    half_qkv.hop(0, "x")
    half_qkv.hop(0, "zb")
    packed_first = jnp.concatenate([flat(pick(qkv_b, adapter_other)), pick(out_a, adapter_other)], axis=1)
    packed = jnp.concatenate([pick(table, adapter_other) for table in (up_b, down_a)], axis=1)
    qa, oa = pick(qkv_a, adapter), pick(out_a, adapter)
    qb = flat(pick(qkv_b, adapter))
    gain_one, gain_two, scale_one, scale_two = (v.reshape(1, width) for v in (gain_one, gain_two, scale_one, scale_two))

    other_tables = flip("tensor")(packed_first)
    half_up.over_tensor(half_qkv.parts[4])
    half_qkv.last_hop()
    half_qkv.parts[6] = after(half_qkv.parts[6], scal, qa, qb, other_tables, half_up.mine)
    tok_swapped = after(tok_swapped, half_qkv.parts[2], half_qkv.parts[4], other_tables, scal, half_out.mine, half_down.mine)
    tok, n1, rank_qkv, q_a, own_a = qkv_local(scal, tok_here, tok_swapped, gain_one, w3, qa, qb)
    half_qkv.pairs_over_cores()
    kv_a = flip("core")(own_a)
    q_b, own_b, w3_other = qkv_other(scal, after(n1, half_up.parts[0]), rank_qkv, other_tables, half_qkv)
    kv_b = flip("core")(own_b)
    half_out.over_tensor(own_b)
    half_up.hop(0, "x", own_b)
    half_up.hop(0, "zb", own_b)
    cot_swapped = swap(after(cotangent[0], own_b))
    mix_a, logs_a = attend(scal, after(q_a, own_b), own_a, kv_a)
    half_out.hop(0, "x", mix_a)
    half_up.hop(4, "x", mix_a)
    half_down.over_tensor(mix_a)
    mix_b, logs_b = attend(scal, after(q_b, mix_a, half_up.parts[2], half_up.parts[4]), own_b, kv_b)
    half_out.pairs_over_cores(mix_b)
    half_down.hop(0, "x", mix_b)
    half_down.hop(0, "zb", mix_b)
    residual, n2, rank_out, rank_up, out_other = branch(
        scal, after(mix_a, half_up.parts[6], half_down.parts[0]), mix_b, tok, w_out, half_out, oa, other_tables, out_b, scale_one, gain_two, up_a
    )
    half_down.hop(2, "zb", n2)
    other_units = flip("tensor")(after(packed, mix_b))
    evens = (0, 2, 4, 6)
    ups = after([half_up.parts[near] for near in evens], mix_b)
    ups_odd = flip("core")(jnp.stack(ups))
    for near in evens[:3]:
        half_down.hop(near, "core", n2)
    cot = jnp.where(core == tensor, cotangent[0], cot_swapped)
    grad_mlp, grad_rank, m, g, rd, gru, gub_a, gda_a = mlp(
        scal, after(n2, half_down.parts[2], half_down.parts[4], other_units), rank_up, up_b, down_a, [w_up], [w_down],
        [cot, scale_two, down_b],
    )
    half_down.hop(6, "core", m)
    nears = evens + tuple(near + 1 for near in evens)
    m, g, rd, gru, gub_b, gda_b = mlp(
        scal, n2, rank_up, other_units, other_units, [*ups, ups_odd], [half_down.parts[near] for near in nears],
        [grad_mlp, grad_rank], nears, (m, g, rd, gru),
    )
    layer, grad_res, grad_a, grad_b, goa_a, goa_b, gob, gua, gdb = middle(
        scal,
        (residual, m, g, rd, gru, cot, mix_a, mix_b, rank_out, n2, grad_mlp),
        (down_b, up_a, scale_two, gain_two, scale_one, w_out, out_other, oa, other_tables, out_b),
    )
    shares = Sum.shares(
        jnp.concatenate([goa_a, gub_a, gda_a], axis=1),
        jnp.concatenate([gob, gua, gdb], axis=1),
        jnp.concatenate([goa_b, gub_b, gda_b], axis=1),
        core,
    )
    early = Sum(*shares, third // 2 + units, adapter, core, tensor)
    early.over_cores()

    def back(queries, own, kv, mixed, grad, logs, piece, pieces, *others):
        return attend_back(scal, after(queries, *others), own, kv, mixed, grad, logs, piece, pieces)

    def exchanged(back, *others):
        return back[0], back[1], flip("core")(after(back[2], *others) if others else back[2])


    side_a = (q_a, own_a, kv_a, mix_a, grad_a, logs_a)
    side_b = (q_b, own_b, kv_b, mix_b, grad_b, logs_b)
    early.start_pair()
    back_1 = back(*side_a, 0, 2, early.send)
    early.arrive(back_1[0])
    early.start("hi")
    back_1 = exchanged(back_1, early.images)
    layer_swapped = swap(after(layer, back_1[0]))
    back_2 = back(*side_a, 1, 2, early.images)
    early.arrive(back_2[0])
    early.start("zb")
    back_2 = exchanged(back_2, early.images)
    back_3 = back(*side_b, 0, 2, early.images)
    early.arrive(back_3[0])
    early.start("x")
    back_3 = exchanged(back_3, early.images)
    back_4 = exchanged(back(*side_b, 1, 2, early.images, layer_swapped))
    kv_sum_a, kv_sum_b, ranked, kept, sent = qkv_tables(
        scal,
        [list(pair) for pair in zip(back_1, back_2)],
        [list(pair) for pair in zip(back_3, back_4)],
        qb, other_tables, n1, rank_qkv,
    )
    early.arrive(kept)
    late = Sum(kept, after(sent, early.pair[1]), 3 * third // 2, None, core, tensor)
    late.over_cores()
    late.start_pair()
    early.arrive(late.send)
    ids = early.over_adapters(None, adapters)
    late.arrive(early.dense)
    late.start("hi")
    grad_rows = qkv_rows(
        0, 1, [back_1[0], back_2[0], kv_sum_a], [back_3[0], back_4[0], kv_sum_b],
        after(w3, late.images), w3_other, ranked, qa, tok, gain_one, grad_res,
    )
    late.arrive(grad_rows)
    grad_rows_swapped = swap(after(grad_rows, late.pair[1]))
    early.other = after(early.other, grad_rows)
    late.start("zb")
    late.start("x")
    late.arrive(grad_rows_swapped)
    in_place_already = core == tensor
    grad_tokens = jnp.where(in_place_already, grad_rows, grad_rows_swapped).astype(F32)
    layer_out = jnp.where(in_place_already, layer, layer_swapped)
    late.over_adapters(ids, adapters)
    ends = (0, third, third + units, third + 2 * units)
    spans = [(False, ends[k], ends[k + 1]) for k in range(3)] + [(True, k * width, (k + 1) * width) for k in range(3)]
    widths = (third, units, units, width, width, width)
    sum_oa, sum_ub, sum_da, sum_ob, sum_ua, sum_db = early.finish(
        spans, [(k, None) for k in range(6)], [(adapters, rank, size) for size in widths], 20e-6
    )
    sum_qb, sum_qa = late.finish(
        [(False, c * third, (c + 1) * third) for c in range(3)] + [(True, 0, width)],
        [(0, c) for c in range(3)] + [(1, None)],
        [(adapters, 3, rank, third), (adapters, rank, width)],
    )
    turn = lambda table: jnp.swapaxes(table, -1, -2)
    return (
        layer_out[None],
        grad_tokens[None],
        sum_qa,
        turn(sum_qb),
        sum_oa,
        turn(sum_ob),
        sum_ua,
        turn(sum_ub),
        sum_da,
        turn(sum_db),
    )


def solution(mesh):
    groups, split = mesh.shape["dp"], mesh.shape["tensor"]
    if split == 2 and groups % 8 == 0:
        mesh = Mesh(mesh.devices.reshape(groups // 8, 2, 2, 2, 2), ("hi", "zb", "x", "core", "tensor"))
        dp, body = ("hi", "zb", "x", "core"), quad_body
    else:
        dp, body = "dp", plain_body
    slots = P(dp, "tensor", None)
    in_specs = (
        slots, slots, P(dp), P(dp), P(), P(), P(), P(),
        P(None, None, "tensor"), P("tensor", None), P(None, "tensor"), P("tensor", None),
        P(), P(None, None, "tensor", None), P(None, None, "tensor"), P(),
        P(), P(None, "tensor", None), P(None, None, "tensor"), P(),
    )
    out_specs = (
        slots, slots, P(), P(None, None, "tensor", None), P(None, None, "tensor"), P(),
        P(), P(None, "tensor", None), P(None, None, "tensor"), P(),
    )
    return jax.shard_map(body, mesh=mesh, in_specs=in_specs, out_specs=out_specs, check_vma=False)
```

```python
import functools

import jax
import jax.numpy as jnp
from jax import lax
from jax.experimental import pallas as pl
from jax.experimental.pallas import tpu as pltpu
from jax.sharding import Mesh
from jax.sharding import PartitionSpec as P

HD = 64
ADAPTERS = 8


epsilon = 1e-06
masked_score = -1e30
HIGHEST = lax.Precision.HIGHEST


def product(form, left, right):
    return jnp.einsum(form, left, right, preferred_element_type=jnp.float32)


def precise(form, left, right):
    return jnp.einsum(form, left.astype(jnp.float32), right.astype(jnp.float32), precision=HIGHEST)


def select_rows(onehot, table):
    return product("sn,n...->s...", onehot, table).astype(table.dtype)


def norm_rows(values, gain_vec):
    average = jnp.mean(values, axis=-1, keepdims=True)
    centred = values - average
    variance = jnp.mean(centred * centred, axis=-1, keepdims=True)
    return centred * lax.rsqrt(variance + epsilon) * gain_vec


def norm_back(values, gain_vec, grad_normed):
    normed, pullback = jax.vjp(lambda rows: norm_rows(rows, gain_vec), values)
    return pullback(grad_normed)[0]


def gelu_slope(values):
    return (
        0.5 * (1.0 + lax.erf(values * 0.7071067811865476))
        + values * jnp.exp(-0.5 * values * values) * 0.3989422804014327
    )


def ffn_forward(rows_low, up_mat, down_mat, up_a_sel, up_b_sel, down_a_sel, down_b_sel):
    rank_up = product("std,srd->str", rows_low, up_a_sel).astype(jnp.bfloat16)
    preact = product("std,dh->sth", rows_low, up_mat) + product("str,shr->sth", rank_up, up_b_sel)
    hidden = jax.nn.gelu(preact, approximate=False).astype(jnp.bfloat16)
    rank_down = product("sth,srh->str", hidden, down_a_sel)
    terms = product("sth,hd->std", hidden, down_mat) + precise(
        "str,sdr->std", rank_down, down_b_sel
    )
    return (rank_up, preact, hidden, rank_down, terms)


def ffn_backward(
    rows_low,
    grad_rows,
    up_mat,
    down_mat,
    up_a_sel,
    up_b_sel,
    down_a_sel,
    down_b_sel,
    rank_up,
    preact,
    hidden,
    rank_down,
):
    grad_rank_down = product("std,sdr->str", grad_rows, down_b_sel).astype(jnp.bfloat16)
    grad_hidden = product("std,hd->sth", grad_rows, down_mat) + product(
        "str,srh->sth", grad_rank_down, down_a_sel
    )
    grad_preact = (grad_hidden * gelu_slope(preact)).astype(jnp.bfloat16)
    grad_up_b = product("sth,str->shr", grad_preact, rank_up)
    grad_rank_up = product("sth,shr->str", grad_preact, up_b_sel)
    grad_rows_in = product("sth,dh->std", grad_preact, up_mat) + precise(
        "str,srd->std", grad_rank_up, up_a_sel
    )
    grad_up_a = precise("str,std->srd", grad_rank_up, rows_low)
    grad_down_a = product("str,sth->srh", grad_rank_down, hidden)
    grad_down_b = precise("std,str->sdr", grad_rows, rank_down)
    return (grad_rows_in, (grad_up_a, grad_up_b, grad_down_a, grad_down_b))


def plain_body(
    tokens,
    cotangent,
    lengths,
    adapter_ids,
    gain_one,
    gain_two,
    scale_one,
    scale_two,
    w_qkv,
    w_out,
    w_up,
    w_down,
    qkv_a,
    qkv_b,
    out_a,
    out_b,
    up_a,
    up_b,
    down_a,
    down_b,
):
    shard_rows = tokens.shape[1]
    seq_len = shard_rows * lax.axis_size("tensor")
    heads_local = w_qkv.shape[2] // HD
    scale_attn = HD ** (-0.5)
    first_row = lax.axis_index("tensor") * shard_rows
    positions = jnp.arange(seq_len, dtype=jnp.int32)
    key_valid = positions[None, :] < jnp.maximum(lengths, 1)[:, None]
    local_rows = first_row + jnp.arange(shard_rows, dtype=jnp.int32)
    row_valid = (local_rows[None, :] < lengths[:, None]).astype(jnp.float32)[:, :, None]
    adapters = jnp.arange(ADAPTERS, dtype=jnp.int32)
    onehot = (adapter_ids[:, None] == adapters[None, :]).astype(jnp.bfloat16)
    qkv_a_sel = select_rows(onehot, qkv_a)
    qkv_b_sel = select_rows(onehot, qkv_b)
    out_a_sel = select_rows(onehot, out_a)
    out_b_sel = select_rows(onehot, out_b)
    up_a_sel = select_rows(onehot, up_a)
    down_b_sel = select_rows(onehot, down_b)
    inputs = tokens.astype(jnp.float32)
    normed_one = norm_rows(inputs, gain_one).astype(jnp.bfloat16)
    full_one = lax.all_gather(normed_one, "tensor", axis=1, tiled=True)
    rank_qkv = product("std,srd->str", full_one, qkv_a_sel).astype(jnp.bfloat16)
    projected = (
        product("std,dcf->sctf", full_one, w_qkv) + product("str,scfr->sctf", rank_qkv, qkv_b_sel)
    ).astype(jnp.bfloat16)

    def split_heads(rows):
        return rows.reshape(seq_len, heads_local, HD)

    def masked_scores(queries, keyrows, valid_keys):
        scores = product("qhe,khe->hqk", queries, keyrows) * scale_attn
        return jnp.where(valid_keys[None, None, :], scores, masked_score)

    def attend(slot_items):
        slot_block, valid_keys = slot_items
        queries = split_heads(slot_block[0])
        keyrows = split_heads(slot_block[1])
        values = split_heads(slot_block[2])
        scores = masked_scores(queries, keyrows, valid_keys)
        row_max = jnp.max(scores, axis=-1, keepdims=True)
        exponent = jnp.exp(scores - row_max)
        row_total = jnp.sum(exponent, axis=-1, keepdims=True)
        soft_low = (exponent / row_total).astype(jnp.bfloat16)
        mixed_rows = (
            product("hqk,khe->qhe", soft_low, values).astype(jnp.bfloat16).reshape(seq_len, -1)
        )
        return (mixed_rows, (row_max + jnp.log(row_total))[:, :, 0])

    mixed, log_total = lax.map(attend, (projected, key_valid))
    rank_out = product("stf,srf->str", mixed, out_a_sel)
    attn_terms = product("stf,fd->std", mixed, w_out) + precise("str,sdr->std", rank_out, out_b_sel)
    attn_branch = lax.psum_scatter(attn_terms, "tensor", scatter_dimension=1, tiled=True)
    residual = inputs + scale_one * attn_branch
    normed_two = norm_rows(residual, gain_two).astype(jnp.bfloat16)
    up_mat, down_mat, up_b_all, down_a_all = (
        lax.all_gather(w_up, "tensor", axis=1, tiled=True),
        lax.all_gather(w_down, "tensor", axis=0, tiled=True),
        lax.all_gather(up_b, "tensor", axis=1, tiled=True),
        lax.all_gather(down_a, "tensor", axis=2, tiled=True),
    )
    up_b_sel = select_rows(onehot, up_b_all)
    down_a_sel = select_rows(onehot, down_a_all)
    rank_up, preact, hidden, rank_down, ffn_terms = ffn_forward(
        normed_two, up_mat, down_mat, up_a_sel, up_b_sel, down_a_sel, down_b_sel
    )
    layer_out = ((residual + scale_two * ffn_terms) * row_valid).astype(jnp.bfloat16)
    grad_out = cotangent.astype(jnp.float32) * row_valid
    grad_mlp = (scale_two * grad_out).astype(jnp.bfloat16)
    ffn_grad_in, ffn_grads = ffn_backward(
        normed_two,
        grad_mlp,
        up_mat,
        down_mat,
        up_a_sel,
        up_b_sel,
        down_a_sel,
        down_b_sel,
        rank_up,
        preact,
        hidden,
        rank_down,
    )
    grad_residual = grad_out + norm_back(residual, gain_two, ffn_grad_in)
    grad_attn = (scale_one * grad_residual).astype(jnp.bfloat16)
    full_grad_attn = lax.all_gather(grad_attn, "tensor", axis=1, tiled=True)
    grad_rank_out = product("std,sdr->str", full_grad_attn, out_b_sel).astype(jnp.bfloat16)
    grad_mixed = (
        product("std,fd->stf", full_grad_attn, w_out)
        + product("str,srf->stf", grad_rank_out, out_a_sel)
    ).astype(jnp.bfloat16)
    grad_out_a = product("str,stf->srf", grad_rank_out, mixed)
    grad_out_b = precise("std,str->sdr", full_grad_attn, rank_out)

    def attend_back(slot_items):
        slot_block, valid_keys, log_rows, grad_rows = slot_items
        queries = split_heads(slot_block[0])
        keyrows = split_heads(slot_block[1])
        values = split_heads(slot_block[2])
        scores = masked_scores(queries, keyrows, valid_keys)
        soft = jnp.exp(scores - log_rows[:, :, None])
        soft_low = soft.astype(jnp.bfloat16)
        grad_heads = split_heads(grad_rows)
        grad_soft = product("qhe,khe->hqk", grad_heads, values)
        grad_values = product("hqk,qhe->khe", soft_low, grad_heads)
        grad_scores = (
            soft * (grad_soft - jnp.sum(soft * grad_soft, axis=-1, keepdims=True))
        ).astype(jnp.bfloat16)
        grad_queries = product("hqk,khe->qhe", grad_scores, keyrows) * scale_attn
        grad_keys = product("hqk,qhe->khe", grad_scores, queries) * scale_attn
        return (
            jnp.stack([grad_queries, grad_keys, grad_values])
            .reshape(3, seq_len, -1)
            .astype(jnp.bfloat16)
        )

    grad_projected = lax.map(attend_back, (projected, key_valid, log_total, grad_mixed))
    grad_qkv_b = product("sctf,str->scfr", grad_projected, rank_qkv)
    grad_rank_qkv = product("sctf,scfr->str", grad_projected, qkv_b_sel)
    grad_one_terms = product("sctf,dcf->std", grad_projected, w_qkv) + precise(
        "str,srd->std", grad_rank_qkv, qkv_a_sel
    )
    grad_qkv_a = precise("str,std->srd", grad_rank_qkv, full_one)
    grad_normed_one = lax.psum_scatter(grad_one_terms, "tensor", scatter_dimension=1, tiled=True)
    grad_tokens = grad_residual + norm_back(inputs, gain_one, grad_normed_one)
    onehot_wide = onehot.astype(jnp.float32)

    def stack_slots(slot_grads):
        return jnp.einsum("sn,s...->n...", onehot_wide, slot_grads, precision=HIGHEST)

    grad_up_a, grad_up_b, grad_down_a, grad_down_b = ffn_grads
    sum_qkv_b, sum_out_a = lax.psum((stack_slots(grad_qkv_b), stack_slots(grad_out_a)), "dp")
    joint_sums = lax.psum(
        (
            stack_slots(grad_qkv_a),
            stack_slots(grad_out_b),
            stack_slots(grad_up_a),
            stack_slots(grad_up_b),
            stack_slots(grad_down_a),
            stack_slots(grad_down_b),
        ),
        ("dp", "tensor"),
    )
    sum_qkv_a, sum_out_b, sum_up_a, up_b_whole, down_a_whole, sum_down_b = joint_sums
    width_local = w_up.shape[1]
    first_col = lax.axis_index("tensor") * width_local
    sum_up_b = lax.dynamic_slice_in_dim(up_b_whole, first_col, width_local, 1)
    sum_down_a = lax.dynamic_slice_in_dim(down_a_whole, first_col, width_local, 2)
    return (
        layer_out,
        grad_tokens,
        sum_qkv_a,
        sum_qkv_b,
        sum_out_a,
        sum_out_b,
        sum_up_a,
        sum_up_b,
        sum_down_a,
        sum_down_b,
    )


F32 = jnp.float32
BF = jnp.bfloat16
LOG2E = 1.4426950408889634
PARTS = 8
PAD = 128
FLIP = [(0, 1), (1, 0)]
SWAP = [(1, 2), (2, 1)]


def dotg(a, b, ca, cb):
    return lax.dot_general(a, b, (((ca,), (cb,)), ((), ())), preferred_element_type=F32)


def pad_rows(table):
    rank, width = table.shape
    return jnp.concatenate([table, jnp.zeros((PAD - rank, width), table.dtype)], axis=0)


def pad_twice(table):
    rank, width = table.shape
    return jnp.concatenate([table, table, jnp.zeros((PAD - 2 * rank, width), table.dtype)], axis=0)


def two_terms(wide, rank):
    high = wide.astype(BF).astype(F32)
    return (high + pltpu.roll(wide - high, rank, 1)).astype(BF)


def three_terms(wide):
    high = wide.astype(BF)
    rest = wide - high.astype(F32)
    middle = rest.astype(BF)
    return high, middle, (rest - middle.astype(F32)).astype(BF)


def whole():
    return pl.BlockSpec(memory_space=pltpu.VMEM)


def in_place():
    return pl.BlockSpec(memory_space=pl.ANY)


def scalars():
    return pl.BlockSpec(memory_space=pltpu.SMEM)


def params(mib=58, **more):
    return pltpu.CompilerParams(vmem_limit_bytes=mib * 2**20, **more)


def cost(flops, nbytes):
    return pl.CostEstimate(flops=int(flops * 0.25), bytes_accessed=int(nbytes * 0.025), transcendentals=0)


def norm_stats(values):
    average = jnp.mean(values, axis=-1, keepdims=True)
    centred = values - average
    scale = lax.rsqrt(jnp.mean(centred * centred, axis=-1, keepdims=True) + epsilon)
    return centred * scale, scale


def norm_grad(unit, scale, grad):
    return scale * (
        grad
        - jnp.mean(grad, axis=-1, keepdims=True)
        - unit * jnp.mean(grad * unit, axis=-1, keepdims=True)
    )


def row_mask(scal, rows):
    at = lax.broadcasted_iota(jnp.int32, (rows, 1), 0) + scal[1] * rows
    return (at < scal[0]).astype(F32)


def choose(scal, here, swapped, target, sem):
    @pl.when(scal[3] != 0)
    def _():
        pltpu.make_async_copy(here, target, sem).start()

    @pl.when(scal[3] == 0)
    def _():
        pltpu.make_async_copy(swapped, target, sem).start()

    return pltpu.make_async_copy(here, target, sem)


def fetch(arrays, nears, target, sem, part_at, axis, size):
    copies = []
    parts = len(nears)
    for number, near in enumerate(nears):
        first = pl.multiple_of(((part_at % parts) ^ near) * size, size)
        place = target.at[:, pl.ds(first, size)] if axis == 1 else target.at[pl.ds(first, size)]
        copies.append(pltpu.make_async_copy(arrays[number // 2].at[number % 2], place, sem.at[near]))
    for copy in copies:
        copy.start()
    return copies


def qkv_local_kernel(scal, here, swapped, gain, w, qa, qb, tok, n1, rank, queries, rest, low, sem):
    step = pl.program_id(0)

    @pl.when(step == 0)
    def _():
        choose(scal, here, swapped, tok, sem.at[0]).wait()
        unit, _ = norm_stats(tok[...].astype(F32))
        normed = (unit * gain[...]).astype(BF)
        n1[...] = normed
        ranked = dotg(normed, pad_rows(qa[...]), 1, 1).astype(BF)
        rank[...] = ranked
        low[...] = ranked

    out = (dotg(n1[...], w[0], 1, 0) + dotg(low[...], pad_rows(qb[...]), 1, 0)).astype(BF)

    @pl.when(step < 2)
    def _():
        rest[0] = out

    @pl.when(step == 2)
    def _():
        queries[...] = out


def qkv_local(scal, tok, swapped, gain, w, qa, qb):
    rows, width = tok.shape
    third = w.shape[2]
    rank = qa.shape[0]
    fixed = lambda c: (0, 0)
    return pl.pallas_call(
        qkv_local_kernel,
        grid=(3,),
        in_specs=[
            scalars(),
            in_place(),
            in_place(),
            pl.BlockSpec((1, width), fixed),
            pl.BlockSpec((1, width, third), lambda c: ((c + 1) % 3, 0, 0)),
            pl.BlockSpec((rank, width), fixed),
            pl.BlockSpec((rank, third), lambda c: (0, (c + 1) % 3)),
        ],
        out_specs=[
            pl.BlockSpec((rows, width), fixed),
            pl.BlockSpec((rows, width), fixed),
            pl.BlockSpec((rows, PAD), fixed),
            pl.BlockSpec((rows, third), fixed),
            pl.BlockSpec((1, rows, third), lambda c: (jnp.minimum(c, 1), 0, 0)),
        ],
        out_shape=[
            jax.ShapeDtypeStruct((rows, width), BF),
            jax.ShapeDtypeStruct((rows, width), BF),
            jax.ShapeDtypeStruct((rows, PAD), BF),
            jax.ShapeDtypeStruct((rows, third), BF),
            jax.ShapeDtypeStruct((2, rows, third), BF),
        ],
        scratch_shapes=[pltpu.VMEM((rows, PAD), BF), pltpu.SemaphoreType.DMA((1,))],
        compiler_params=params(dimension_semantics=("arbitrary",)),
        cost_estimate=cost(1e-7 * 1e15, 1e5),
        name="qkv_local",
    )(scal, tok, swapped, gain, w, qa, qb)


def qkv_other_kernel(nears, scal, n1, rank, qb, *rest):
    arrays, (queries, out, w, sem) = rest[: len(nears) // 2], rest[len(nears) // 2 :]
    third = w.shape[2]
    copies = fetch(arrays, nears, w, sem, scal[2], 1, arrays[0].shape[2])
    for copy in copies:
        copy.wait()
    for c in (1, 2, 0):
        at = slice(c * third, (c + 1) * third)
        terms = (dotg(n1[...], w[c], 1, 0) + dotg(rank[...], pad_rows(qb[:, at]), 1, 0)).astype(BF)
        if c == 0:
            queries[...] = terms
        else:
            out[c - 1] = terms


def qkv_other(scal, n1, rank, qb, half):
    rows, width = n1.shape
    arrays, nears = half.pairs, half.names
    third = arrays[0].shape[3]
    return pl.pallas_call(
        functools.partial(qkv_other_kernel, nears),
        in_specs=[scalars(), whole(), whole(), whole()] + [in_place()] * len(arrays),
        out_specs=[whole()] * 3,
        out_shape=[
            jax.ShapeDtypeStruct((rows, third), BF),
            jax.ShapeDtypeStruct((2, rows, third), BF),
            jax.ShapeDtypeStruct((3, width, third), BF),
        ],
        scratch_shapes=[pltpu.SemaphoreType.DMA((PARTS,))],
        compiler_params=params(),
        cost_estimate=cost(7e-6 * 1e15, 10e6),
        name="qkv_other",
    )(scal, n1, rank, qb, *arrays)


def lane_numbers(rows):
    return lax.broadcasted_iota(jnp.int32, (rows, 2 * HD), 1)


def key_fill(scal, rows, other, ones):
    side = 1 - scal[1] if other else scal[1]
    lanes = lane_numbers(rows) % HD
    at = lax.broadcasted_iota(jnp.int32, (rows, 2 * HD), 0) + side * rows
    bias = jnp.where(at < jnp.maximum(scal[0], 1), 0.0, masked_score)
    return jnp.where(lanes < ones, 1.0, jnp.where(lanes == ones, bias, 0.0)).astype(BF)


def lane_terms(wide, rows, with_one):
    lanes = lane_numbers(rows) % HD
    first, second, third = three_terms(wide)
    filled = jnp.where(lanes == 2, third, jnp.full_like(third, 0.0))
    if with_one:
        filled = jnp.where(lanes == 3, jnp.full_like(third, 1.0), filled)
    return jnp.where(lanes == 0, first, jnp.where(lanes == 1, second, filled))


def attend_kernel(scal, q_ref, k_ref, v_ref, ko_ref, vo_ref, out, log_out, qx, kx, vt):
    rows = q_ref.shape[0]
    queries = (q_ref[...].astype(F32) * HD**-0.5).astype(BF)
    lanes = lane_numbers(rows)
    low_half = lanes < HD
    ones = (lanes % HD == 0).astype(BF)
    fills = [key_fill(scal, rows, side == 1, 0) for side in range(2)]
    for head in range(2):
        own = low_half if head == 0 else ~low_half
        qx[head] = jnp.where(own, queries, ones)
        for side, ref in enumerate((k_ref, ko_ref)):
            kx[head, side * rows : (side + 1) * rows] = jnp.where(own, ref[0], fills[side])
    for side, ref in enumerate((v_ref, vo_ref)):
        at = slice(side * rows, (side + 1) * rows)
        turned = ref[0].T
        for head in range(2):
            vt[head, 0:HD, at] = turned[head * HD : (head + 1) * HD]
            vt[head, HD : HD + 16, at] = jnp.ones((16, rows), BF)

    def scores(head):
        return dotg(kx[head], qx[head], 1, 1)

    ahead = scores(0)
    mixed, logs = [], []
    for head in range(2):
        now = ahead
        if head == 0:
            ahead = scores(1)
        top = jnp.max(now, axis=0, keepdims=True)
        soft = jnp.exp(now - top).astype(BF)
        terms = dotg(vt[head], soft, 1, 0)
        total = terms[HD : HD + 1]
        mixed.append(terms[0:HD] / total)
        logs.append(jnp.broadcast_to(top + jnp.log(total), (HD, total.shape[1])))
    out[...] = jnp.concatenate(mixed, axis=0).T.astype(BF)
    log_out[...] = jnp.concatenate([logs[1], logs[0]], axis=0).T


def attend(scal, queries, own, other):
    _, rows, width = own.shape
    pairs = width // (2 * HD)
    take = lambda c: pl.BlockSpec((1, rows, 2 * HD), lambda p: (c, 0, p))
    flat = pl.BlockSpec((rows, 2 * HD), lambda p: (0, p))
    return pl.pallas_call(
        attend_kernel,
        grid=(pairs,),
        in_specs=[scalars(), flat, take(0), take(1), take(0), take(1)],
        out_specs=[flat, flat],
        out_shape=[jax.ShapeDtypeStruct((rows, width), BF), jax.ShapeDtypeStruct((rows, width), F32)],
        scratch_shapes=[
            pltpu.VMEM((2, rows, 2 * HD), BF),
            pltpu.VMEM((2, 2 * rows, 2 * HD), BF),
            pltpu.VMEM((2, HD + 16, 2 * rows), BF),
        ],
        compiler_params=params(dimension_semantics=("arbitrary",)),
        cost_estimate=cost(16e-6 * 1e15, 6e6),
        name="attend",
    )(scal, queries, own, own, other, other)


def attend_back_kernel(
    scal, q_ref, k_ref, v_ref, ko_ref, vo_ref, mixed_ref, grad_ref, log_ref, queries_out, own_out, other_out,
    qx, gx, qm, gm, kx, vx, kt,
):
    rows = q_ref.shape[0]
    queries, grad = q_ref[...], grad_ref[...]
    zero = jnp.zeros_like(queries)
    low_half = lane_numbers(rows) < HD
    scaled = (queries.astype(F32) * HD**-0.5).astype(BF)
    weighed = grad.astype(F32) * mixed_ref[...].astype(F32)
    high = weighed.astype(BF)
    pair = jnp.concatenate([high, (weighed - high.astype(F32)).astype(BF)], axis=1)
    down = lax.broadcasted_iota(jnp.int32, (4 * HD, 2 * HD), 0) // HD % 2
    across = lax.broadcasted_iota(jnp.int32, (4 * HD, 2 * HD), 1) // HD
    sums = dotg(pair, (down != across).astype(BF), 1, 0)
    query_fill = lane_terms(-log_ref[...], rows, True)
    grad_fill = lane_terms(-sums, rows, False)
    fills = [key_fill(scal, rows, side == 1, 3) for side in range(2)]
    value_fill = (lane_numbers(rows) % HD < 3).astype(BF)
    for head in range(2):
        own = low_half if head == 0 else ~low_half
        qx[head] = jnp.where(own, scaled, query_fill)
        gx[head] = jnp.where(own, grad, grad_fill)
        qm[head] = jnp.where(own, queries, zero)
        gm[head] = jnp.where(own, grad, zero)
        for side, (key_ref, value_ref) in enumerate(((k_ref, v_ref), (ko_ref, vo_ref))):
            at = slice(side * rows, (side + 1) * rows)
            kx[head, at] = jnp.where(own, key_ref[0], fills[side])
            vx[head, at] = jnp.where(own, value_ref[0], value_fill)
    for side, ref in enumerate((k_ref, ko_ref)):
        kt[:, side * rows : (side + 1) * rows] = ref[0].T
    steps = [(side, head) for side in range(2) for head in range(2)]

    def first(side, head):
        at = slice(side * rows, (side + 1) * rows)
        return dotg(kx[head, at], qx[head], 1, 1), dotg(vx[head, at], gx[head], 1, 1)

    ahead = first(*steps[0])
    grad_queries = [0.0, 0.0]
    kept = None
    for number, (side, head) in enumerate(steps):
        scores, grad_soft = ahead
        if number + 1 < len(steps):
            ahead = first(*steps[number + 1])
        soft = jnp.exp(scores)
        grad_scores = (soft * grad_soft).astype(BF)
        values = dotg(soft.astype(BF), gm[head], 1, 0)
        keys = dotg(grad_scores, qm[head], 1, 0)
        at = slice(side * rows, (side + 1) * rows)
        grad_queries[head] += dotg(kt[head * HD : (head + 1) * HD, at], grad_scores, 1, 0)
        if head == 0:
            kept = (keys, values)
        else:
            keys = ((kept[0] + keys) * HD**-0.5).astype(BF)
            values = (kept[1] + values).astype(BF)
            out = own_out if side == 0 else other_out
            out[0], out[1] = keys, values
    queries_out[...] = (jnp.concatenate(grad_queries, axis=0).T * HD**-0.5).astype(BF)


def attend_back(scal, queries, own, other, mixed, grad, logs, piece, pieces):
    _, rows, width = own.shape
    width = width // pieces
    pairs = width // (2 * HD)
    skip = piece * pairs
    take = lambda c: pl.BlockSpec((1, rows, 2 * HD), lambda p: (c, 0, p + skip))
    flat = pl.BlockSpec((rows, 2 * HD), lambda p: (0, p + skip))
    both = jax.ShapeDtypeStruct((2, rows, width), BF)
    return pl.pallas_call(
        attend_back_kernel,
        grid=(pairs,),
        in_specs=[scalars(), flat, take(0), take(1), take(0), take(1), flat, flat, flat],
        out_specs=[
            pl.BlockSpec((rows, 2 * HD), lambda p: (0, p)),
            pl.BlockSpec((2, rows, 2 * HD), lambda p: (0, 0, p)),
            pl.BlockSpec((2, rows, 2 * HD), lambda p: (0, 0, p)),
        ],
        out_shape=[jax.ShapeDtypeStruct((rows, width), BF), both, both],
        scratch_shapes=[pltpu.VMEM((2, rows, 2 * HD), BF)] * 4
        + [pltpu.VMEM((2, 2 * rows, 2 * HD), BF)] * 2
        + [pltpu.VMEM((2 * HD, 2 * rows), BF)],
        compiler_params=params(dimension_semantics=("arbitrary",)),
        cost_estimate=cost(26e-6 / pieces * 1e15, 9e6),
        name="attend_back",
    )(scal, queries, own, own, other, other, mixed, grad, logs)


def branch_kernel(nears, scal, mix_a, mix_b, tok, w_a, oa_a, oa_b, obs, scale_one, gain_two, uas, *rest):
    arrays = rest[: len(nears) // 2]
    residual, n2, rank_out, rank_up, w_b, sem = rest[len(nears) // 2 :]
    rank = oa_a.shape[0]
    ob, ua = obs[scal[4]], uas[scal[4]]

    @pl.when(pl.program_id(0) == 0)
    def _():
        for copy in fetch(arrays, nears, w_b, sem, scal[2], 0, arrays[0].shape[1]):
            copy.wait()

    ranked = dotg(mix_a[...], pad_rows(oa_a[...]), 1, 1) + dotg(mix_b[...], pad_rows(oa_b[:, -oa_a.shape[1] :]), 1, 1)
    ranked = two_terms(ranked, rank)
    rank_out[...] = ranked
    terms = dotg(mix_a[...], w_a[...], 1, 0) + dotg(mix_b[...], w_b[...], 1, 0)
    terms = terms + dotg(ranked, pad_twice(ob), 1, 0)
    total = tok[...].astype(F32) + scale_one[...] * terms
    residual[...] = total.astype(BF)
    unit, _ = norm_stats(total)
    normed = (unit * gain_two[...]).astype(BF)
    n2[...] = normed
    rank_up[...] = dotg(normed, pad_rows(ua), 1, 1).astype(BF)


def blocked(rows, width):
    return pl.BlockSpec((rows, width), lambda step: (step, 0))


def fixed_block(*shape):
    return pl.BlockSpec(shape, lambda step: (0,) * len(shape))


def branch(scal, mix_a, mix_b, tok, w_a, half, oa_a, oa_b, ob, scale_one, gain_two, ua):
    rows, width = tok.shape
    heads = mix_a.shape[1]
    block = rows // 2
    arrays, nears = half.pairs, half.names
    return pl.pallas_call(
        functools.partial(branch_kernel, nears),
        grid=(2,),
        in_specs=[scalars(), blocked(block, heads), blocked(block, heads), blocked(block, width)]
        + [fixed_block(*array.shape) for array in (w_a, oa_a, oa_b, ob, scale_one, gain_two, ua)]
        + [in_place()] * len(arrays),
        out_specs=[blocked(block, width), blocked(block, width), blocked(block, PAD), blocked(block, PAD)]
        + [fixed_block(*w_a.shape)],
        out_shape=[
            jax.ShapeDtypeStruct((rows, width), BF),
            jax.ShapeDtypeStruct((rows, width), BF),
            jax.ShapeDtypeStruct((rows, PAD), BF),
            jax.ShapeDtypeStruct((rows, PAD), BF),
            jax.ShapeDtypeStruct(w_a.shape, BF),
        ],
        scratch_shapes=[pltpu.SemaphoreType.DMA((PARTS,))],
        compiler_params=params(dimension_semantics=("arbitrary",)),
        cost_estimate=cost(8e-6 * 1e15, 16e6),
        name="branch",
    )(scal, mix_a, mix_b, tok, w_a, oa_a, oa_b, ob, scale_one, gain_two, ua, *arrays)


def mlp_kernel(nears, counts, step, more, *refs):
    scal, n2, rank_up, ub, da = refs[:5]
    ups, downs, rest = refs[5 : 5 + counts[0]], refs[5 + counts[0] : 5 + sum(counts)], refs[5 + sum(counts) :]
    if nears is None:
        cot, scale_two, dbs, grad_mlp, grad_rank = rest[:5]
        earlier, rest = (), rest[5:]
        ub, da, db = (table.at[scal[4]] for table in (ub, da, dbs))
    else:
        grad_mlp, grad_rank = rest[:2]
        earlier, rest = rest[2 : 2 + more], rest[2 + more :]
    m_out, g_out, rd_out, gru_out, gub_out, gda_out = rest[:6]
    wu, wd, ubs, das, hidden, grad_pre, sem = rest[6:]
    width = wu.shape[1]
    rank = ub.shape[0]
    size = gub_out.shape[1] // PARTS
    pieces = width // size
    chunks = width // step
    waits = [[] for _ in range(chunks)]
    for piece in range(pieces):
        at = pl.ds(piece * size, size)
        if nears is None:
            sources = ups[0].at[:, at], downs[0].at[at]
        else:
            last = counts[0] - 1
            sources = ups[piece] if piece < last else ups[last].at[piece - last], downs[piece]
        for which, (source, target) in enumerate(zip(sources, (wu.at[:, at], wd.at[at]))):
            copy = pltpu.make_async_copy(source, target, sem.at[which, piece])
            copy.start()
            waits[piece * size // step].append(copy)
    def place(piece, first=0):
        if nears is None:
            return pl.ds(piece * size, size)
        return pl.ds(pl.multiple_of((scal[2] ^ nears[piece]) * size + first, size), size)

    if nears is None:
        grad_low = (scale_two[...] * (cot[...].astype(F32) * row_mask(scal, cot.shape[0]))).astype(BF)
        grad_mlp[...] = grad_low
        grad_rank[...] = dotg(grad_low, pad_rows(db[...]), 1, 1).astype(BF)
    ubs[...] = jnp.zeros_like(ubs)
    das[...] = jnp.zeros_like(das)
    for piece in range(pieces):
        at = slice(piece * size, (piece + 1) * size)
        ubs[0:rank, at] = ub[:, place(piece)]
        das[0:rank, at] = da[:, place(piece, da.shape[1] // 2)]
    up_turned = rank_up[...].T[0:rank]
    grad_turned = grad_rank[...].T[0:rank]

    def first(k):
        for copy in waits[k]:
            copy.wait()
        at = slice(k * step, (k + 1) * step)
        return (
            dotg(n2[...], wu[:, at], 1, 0) + dotg(rank_up[...], ubs[:, at], 1, 0),
            dotg(grad_mlp[...], wd[at, :], 1, 1) + dotg(grad_rank[...], das[:, at], 1, 0),
        )

    ahead = first(0)
    for k in range(chunks):
        at = slice(k * step, (k + 1) * step)
        preact, grad_hidden = ahead
        if k + 1 < chunks:
            ahead = first(k + 1)
        cdf = 0.5 * (1.0 + lax.erf(preact * 0.7071067811865476))
        hidden[:, at] = (preact * cdf).astype(BF)
        slope = cdf + preact * jnp.exp(-0.5 * preact * preact) * 0.3989422804014327
        grad_pre[:, at] = (grad_hidden * slope).astype(BF)
    ranked = dotg(hidden[...], das[...], 1, 1)
    grad_ranked = dotg(grad_pre[...], ubs[...], 1, 1)
    if more:
        ranked, grad_ranked = ranked + earlier[2][...], grad_ranked + earlier[3][...]
    rd_out[...] = ranked
    gru_out[...] = grad_ranked
    for piece in range(pieces):
        at = slice(piece * size, (piece + 1) * size)
        gub_out[:, place(piece)] = dotg(up_turned, grad_pre[:, at], 1, 0)
        gda_out[:, place(piece)] = dotg(grad_turned, hidden[:, at], 1, 0)
    for at in (slice(k, k + step) for k in range(0, wu.shape[0], step)):
        terms = dotg(hidden[...], wd[:, at], 1, 0)
        grad_terms = dotg(grad_pre[...], wu[at, :], 1, 1)
        if more:
            terms = terms + earlier[0][:, at].astype(F32)
            grad_terms = grad_terms + earlier[1][:, at].astype(F32)
        m_out[:, at] = terms.astype(BF)
        g_out[:, at] = grad_terms.astype(BF)


def mlp(scal, n2, rank_up, ub, da, ups, downs, grads, nears=None, earlier=()):
    rows, width = n2.shape
    rank, half = ub.shape[-2:]
    half = half if nears is None else half // 2
    units = half if nears is None else len(nears) * half // PARTS
    step = min(512, units)
    sums = jax.ShapeDtypeStruct((rows, width), BF)
    ranked = jax.ShapeDtypeStruct((rows, PAD), F32)
    table = jax.ShapeDtypeStruct((rank, half), F32)
    low = jax.ShapeDtypeStruct((rows, width), BF)
    first = [low, jax.ShapeDtypeStruct((rows, PAD), BF)] if nears is None else []
    return pl.pallas_call(
        functools.partial(mlp_kernel, nears, (len(ups), len(downs)), step, len(earlier)),
        in_specs=[scalars()]
        + [whole()] * 4
        + [in_place()] * (len(ups) + len(downs))
        + [whole()] * (len(grads) + len(earlier)),
        out_specs=[whole()] * (len(first) + 6),
        out_shape=first + [sums, sums, ranked, ranked, table, table],
        scratch_shapes=[
            pltpu.VMEM((width, units), BF),
            pltpu.VMEM((units, width), BF),
            pltpu.VMEM((PAD, units), BF),
            pltpu.VMEM((PAD, units), BF),
            pltpu.VMEM((rows, units), BF),
            pltpu.VMEM((rows, units), BF),
            pltpu.SemaphoreType.DMA((2, PARTS)),
        ],
        compiler_params=params(),
        cost_estimate=cost(25e-6 * units / half * 1e15, 20e6),
        name="mlp",
    )(scal, n2, rank_up, ub, da, *ups, *downs, *grads, *earlier)


def middle_kernel(
    scal, residual, m_in, g_in, rd, gru, cot, mix_a, mix_b, rank_out, n2, grad_mlp,
    dbs, uas, scale_two, gain_two, scale_one, w_a, w_b, oa_a, oa_b, obs,
    layer, grad_res, grad_a, grad_b, goa_a, goa_b, gob, gua, gdb,
):
    step = pl.program_id(0)
    rows = residual.shape[0]
    db, ua, ob = dbs[scal[4]], uas[scal[4]], obs[scal[4]]
    rank = db.shape[0]
    at = lax.broadcasted_iota(jnp.int32, (rows, 1), 0) + (scal[1] * pl.num_programs(0) + step) * rows
    valid = (at < scal[0]).astype(F32)
    down = two_terms(rd[...], rank)
    up = two_terms(gru[...], rank)

    def add(out, terms):
        @pl.when(step == 0)
        def _():
            out[...] = terms

        @pl.when(step > 0)
        def _():
            out[...] += terms

    def turned(terms, right):
        both = dotg(terms.T[0 : 2 * rank], right, 1, 0)
        return both[0:rank] + both[rank : 2 * rank]

    branch_out = m_in[...].astype(F32) + dotg(down, pad_twice(db), 1, 0)
    total = residual[...].astype(F32)
    layer[...] = ((total + scale_two[...] * branch_out) * valid).astype(BF)
    add(gua, turned(up, n2[...]))
    add(gdb, turned(down, grad_mlp[...]))
    unit, scale = norm_stats(total)
    grad_normed = (g_in[...].astype(F32) + dotg(up, pad_twice(ua), 1, 0)) * gain_two[...]
    grad_total = cot[...].astype(F32) * valid + norm_grad(unit, scale, grad_normed)
    grad_res[...] = grad_total.astype(BF)
    grad_attn = (scale_one[...] * grad_total).astype(BF)
    grad_rank = dotg(grad_attn, pad_rows(ob), 1, 1).astype(BF)
    grad_a[...] = (
        dotg(grad_attn, w_a[...], 1, 1) + dotg(grad_rank, pad_rows(oa_a[...]), 1, 0)
    ).astype(BF)
    grad_b[...] = (
        dotg(grad_attn, w_b[...], 1, 1) + dotg(grad_rank, pad_rows(oa_b[:, -oa_a.shape[1] :]), 1, 0)
    ).astype(BF)
    rank_turned = grad_rank.T[0:rank]
    add(goa_a, dotg(rank_turned, mix_a[...], 1, 0))
    add(goa_b, dotg(rank_turned, mix_b[...], 1, 0))
    add(gob, turned(rank_out[...], grad_attn))


def middle(scal, by_rows, others, blocks=1):
    rows, width = by_rows[0].shape
    block = rows // blocks
    heads = by_rows[6].shape[1]
    rank = others[0].shape[1]
    part = jax.ShapeDtypeStruct((rows, heads), BF)
    table = jax.ShapeDtypeStruct((rank, width), F32)
    half_table = jax.ShapeDtypeStruct((rank, heads), F32)
    return pl.pallas_call(
        middle_kernel,
        grid=(blocks,),
        in_specs=[scalars()]
        + [blocked(block, array.shape[1]) for array in by_rows]
        + [fixed_block(*array.shape) for array in others],
        out_specs=[blocked(block, width), blocked(block, width), blocked(block, heads), blocked(block, heads)]
        + [fixed_block(*shape) for shape in ((rank, heads),) * 2 + ((rank, width),) * 3],
        out_shape=[jax.ShapeDtypeStruct((rows, width), BF)] * 2
        + [part, part, half_table, half_table, table, table, table],
        compiler_params=params(dimension_semantics=("arbitrary",)),
        cost_estimate=cost(9e-6 * 1e15, 20e6),
        name="middle",
    )(scal, *by_rows, *others)


def columns_of(pieces):
    first = 0
    for piece in pieces:
        yield piece, slice(first, first + piece.shape[-1])
        first += piece.shape[-1]


def qkv_tables_kernel(counts, *refs):
    sides = []
    for count in counts:
        sides.append((refs[:count], refs[count : 2 * count], refs[2 * count : 3 * count]))
        refs = refs[3 * count :]
    scal, qb_a, qb_b, n1, rank_in, total_a, total_b, rank_out, kept, sent, gqb_a, gqb_b, gqa = refs
    rank = qb_a.shape[0]
    third = qb_a.shape[1] // 3
    rank_turned = rank_in[...].T[0:rank]
    ranked = None
    for side, qb, total, table in zip(sides, (qb_a, qb_b), (total_a, total_b), (gqb_a, gqb_b)):
        queries, owns, gots = side
        for (piece, at), own, got in zip(columns_of(queries), owns, gots):
            for c in range(3):
                if c == 0:
                    grad = piece[...]
                else:
                    grad = (own[c - 1].astype(F32) + got[c - 1].astype(F32)).astype(BF)
                    total[c - 1, :, at] = grad
                place = slice(c * third + at.start, c * third + at.stop)
                table[:, place] = dotg(rank_turned, grad, 1, 0)
                terms = dotg(grad, pad_rows(qb[:, place]), 1, 1)
                ranked = terms if ranked is None else ranked + terms
    ranked = two_terms(ranked, rank)
    rank_out[...] = ranked
    both = dotg(ranked.T[0 : 2 * rank], n1[...], 1, 0)
    gqa[...] = both[0:rank] + both[rank : 2 * rank]
    first = 0
    for table in (gqb_a, gqa, gqb_b):
        half = table.shape[1] // 2
        at = slice(first, first + half)
        kept[:, at] = table[:, pl.ds(pl.multiple_of(scal[1] * half, half), half)]
        sent[:, at] = table[:, pl.ds(pl.multiple_of((1 - scal[1]) * half, half), half)].astype(BF)
        first += half


def qkv_tables(scal, side_a, side_b, qb_a, qb_b, n1, rank_in):
    rows, width = n1.shape
    rank, columns = qb_a.shape
    pieces = [piece for side in (side_a, side_b) for group in side for piece in group]
    total = jax.ShapeDtypeStruct((2, rows, columns // 3), BF)
    share = columns + width // 2
    return pl.pallas_call(
        functools.partial(qkv_tables_kernel, (len(side_a[0]), len(side_b[0]))),
        in_specs=[whole()] * len(pieces) + [scalars()] + [whole()] * 4,
        out_specs=[whole()] * 5,
        out_shape=[total, total, jax.ShapeDtypeStruct((rows, PAD), BF)]
        + [jax.ShapeDtypeStruct((rank, share), F32), jax.ShapeDtypeStruct((rank, share), BF)],
        scratch_shapes=[pltpu.VMEM((rank, columns), F32)] * 2 + [pltpu.VMEM((rank, width), F32)],
        compiler_params=params(),
        cost_estimate=cost(7e-6 * 1e15, 14e6),
        name="qkv_tables",
    )(*pieces, scal, qb_a, qb_b, n1, rank_in)


def qkv_rows_kernel(count_a, count_b, *refs):
    grads_a, grads_b, refs = refs[:count_a], refs[count_a : count_a + count_b], refs[count_a + count_b :]
    w_a, w_b, ranked, qa, tok, gain, grad_res, out = refs
    grad = dotg(ranked[...], pad_twice(qa[...]), 1, 0)
    for grads, w in ((grads_a, w_a), (grads_b, w_b)):
        for piece, at in columns_of(grads[:-1]):
            grad = grad + dotg(piece[...], w[0, :, at], 1, 1)
        for c in (1, 2):
            grad = grad + dotg(grads[-1][c - 1], w[c], 1, 1)
    unit, scale = norm_stats(tok[...].astype(F32))
    out[...] = (grad_res[...].astype(F32) + norm_grad(unit, scale, grad * gain[...])).astype(BF)


def qkv_rows(block_at, blocks, grads_a, grads_b, w_a, w_b, ranked, qa, tok, gain, grad_res):
    rows, width = tok.shape
    block = rows // blocks
    flat = lambda array: pl.BlockSpec((block, array.shape[1]), lambda step: (block_at, 0))
    deep = lambda array: pl.BlockSpec((2, block, array.shape[2]), lambda step: (0, block_at, 0))
    specs = [flat(array) if array.ndim == 2 else deep(array) for array in grads_a + grads_b]
    return pl.pallas_call(
        functools.partial(qkv_rows_kernel, len(grads_a), len(grads_b)),
        grid=(1,),
        in_specs=specs
        + [whole(), whole(), flat(ranked), whole(), flat(tok), whole(), flat(grad_res)],
        out_specs=whole(),
        out_shape=jax.ShapeDtypeStruct((block, width), BF),
        compiler_params=params(),
        cost_estimate=cost(12e-6 / blocks * 1e15, 16e6 / blocks),
        name="qkv_rows",
    )(*grads_a, *grads_b, w_a, w_b, ranked, qa, tok, gain, grad_res)


def gather_kernel(has_ids, flag, *refs):
    ids, (own, got, out, ids_out, total) = refs[0], refs[has_ids:]
    columns = out.shape[2]
    half = own.shape[0]
    total[...] = jnp.zeros_like(total)

    def add(first, images):
        for image in range(half):
            if has_ids:
                adapter = ids[first + image]
            else:
                note = images[image, 0:8, columns : columns + PAD].astype(F32)
                adapter = jnp.max(note).astype(jnp.int32)
            ids_out[first + image] = adapter
            total[adapter] += images[image, :, 0:columns].astype(F32)

    @pl.when(flag[0] == 0)
    def _():
        add(0, own)
        add(half, got)

    @pl.when(flag[0] != 0)
    def _():
        add(0, got)
        add(half, own)

    out[...] = total[...].astype(BF)


def gather_images(flag, ids, pair, adapters, columns):
    count, rank, _ = pair[0].shape
    given = [] if ids is None else [ids]
    return pl.pallas_call(
        functools.partial(gather_kernel, len(given)),
        in_specs=[scalars()] * (1 + len(given)) + [whole()] * 2,
        out_specs=[whole(), scalars()],
        out_shape=[
            jax.ShapeDtypeStruct((adapters, rank, columns), BF),
            jax.ShapeDtypeStruct((2 * count,), jnp.int32),
        ],
        scratch_shapes=[pltpu.VMEM((adapters, rank, columns), F32)],
        compiler_params=params(),
        cost_estimate=cost((20e-6 if ids is None else 1e-6) * 1e15, 1e6),
        name="gather_images",
    )(flag.astype(jnp.int32)[None], *given, *pair)


def finish_kernel(cut, spans, places, core, own, other, *outs):
    def write(low, high):
        for (shared, start, stop), (number, index) in zip(spans, places):
            first = cut if shared else 0
            half = own.shape[2] - cut if shared else cut
            out = outs[number] if index is None else outs[number].at[:, index]
            middle = min(max(half - start, 0), stop - start)
            if middle > 0:
                out[:, :, 0:middle] = low[:, :, first + start : first + start + middle].astype(F32)
            if middle < stop - start:
                begin = first + start + middle - half
                out[:, :, middle : stop - start] = high[:, :, begin : first + stop - half].astype(F32)

    @pl.when(core[0] == 0)
    def _():
        write(own, other)

    @pl.when(core[0] != 0)
    def _():
        write(other, own)


def finish(core, cut, spans, places, own, other, shapes, seconds=1e-6):
    return pl.pallas_call(
        functools.partial(finish_kernel, cut, spans, places),
        in_specs=[scalars(), whole(), whole()],
        out_specs=[whole()] * len(shapes),
        out_shape=[jax.ShapeDtypeStruct(shape, F32) for shape in shapes],
        compiler_params=params(),
        cost_estimate=cost(seconds * 1e15, 1e6),
        name="finish",
    )(core, own, other)


def swap(rows):
    return lax.ppermute(rows, ("core", "tensor"), SWAP)


def flip(axis):
    return lambda array: lax.ppermute(array, axis, FLIP)


def after(value, *others):
    return lax.optimization_barrier((value, others))[0]


class OtherHalf:
    BITS = {"core": 1, "x": 2, "zb": 4}

    def __init__(self, local, axis, part_at, count):
        size = local.shape[axis] // count
        self.mine = lax.dynamic_slice_in_dim(local, (part_at % count) * size, size, axis)
        self.parts = {}
        self.nears = tuple(range(0, count, 2))

    def over_tensor(self, *others):
        self.parts[0] = flip("tensor")(after(self.mine, *others) if others else self.mine)

    def hop(self, near, axis, *others):
        part = after(self.parts[near], *others) if others else self.parts[near]
        self.parts[near ^ self.BITS[axis]] = flip(axis)(part)

    def last_hop(self):
        over_zb, over_x = jnp.split(self.parts[2], 2, axis=1)[0], jnp.split(self.parts[4], 2, axis=1)[1]
        self.parts[6] = jnp.concatenate([flip("zb")(over_zb), flip("x")(over_x)], axis=1)

    def pairs_over_cores(self, *others):
        parts = after(self.parts, *others) if others else self.parts
        even = [jnp.stack([parts[a], parts[b]]) for a, b in zip(self.nears[::2], self.nears[1::2])]
        self.pairs = even + [flip("core")(array) for array in even]
        self.names = self.nears + tuple(near + 1 for near in self.nears)


def half_columns(array, index):
    size = array.shape[1] // 2
    return lax.dynamic_slice_in_dim(array, index * size, size, 1)


def by_index(index, own, other, axis):
    return jnp.where(
        index == 0, jnp.concatenate([own, other], axis=axis), jnp.concatenate([other, own], axis=axis)
    )


class Sum:
    def __init__(self, kept, sent, cut, adapter, core, tensor):
        self.core, self.tensor, self.adapter = core, tensor, adapter
        self.kept, self.sent, self.cut = kept, sent, cut

    @staticmethod
    def shares(near, shared, far, core):
        def share(index):
            return jnp.concatenate([half_columns(array, index) for array in (near, shared, far)], axis=1)

        return share(core), share(1 - core).astype(BF)

    def over_cores(self):
        total = (self.kept + flip("core")(self.sent).astype(F32)).astype(BF)
        cut, columns = self.cut, total.shape[1] - self.cut
        note = []
        if self.adapter is not None:
            note = [jnp.broadcast_to(self.adapter.astype(BF), (total.shape[0], PAD))]
        self.mine = jnp.concatenate([total[:, :columns]] + note, axis=1)
        self.send = jnp.concatenate([total[:, columns:], total[:, cut:columns]] + note, axis=1)
        self.columns = columns

    def start_pair(self):
        self.flag, self.pair = self.tensor, (self.mine[None], flip("tensor")(self.send)[None])

    def start(self, name):
        self.images = by_index(self.flag, *self.pair, 0)
        if lax.axis_size(name) == 2:
            self.flag, self.pair = lax.axis_index(name), (self.images, flip(name)(self.images))
        else:
            images = lax.all_gather(self.images, name, axis=0, tiled=True)
            half = images.shape[0] // 2
            self.flag, self.pair = jnp.zeros((), jnp.int32), (images[:half], images[half:])

    def arrive(self, *others):
        self.pair = (self.pair[0], after(self.pair[1], *others))

    def over_adapters(self, ids, adapters):
        self.dense, ids = gather_images(self.flag, ids, self.pair, adapters, self.columns)
        self.other = flip("core")(self.dense)
        return ids

    def finish(self, spans, places, shapes, *seconds):
        core = self.core.astype(jnp.int32)[None]
        return finish(core, self.cut, spans, places, self.dense, self.other, shapes, *seconds)


def quad_body(
    tokens, cotangent, lengths, adapter_ids, gain_one, gain_two, scale_one, scale_two, w_qkv, w_out, w_up, w_down,
    qkv_a, qkv_b, out_a, out_b, up_a, up_b, down_a, down_b,
):
    core, tensor = lax.axis_index("core"), lax.axis_index("tensor")
    part_at = lax.axis_index("zb") * 4 + lax.axis_index("x") * 2 + core
    adapters, rank, width = qkv_a.shape
    third = w_qkv.shape[2]
    units = w_up.shape[1]

    w3 = jnp.swapaxes(w_qkv, 0, 1)
    half_qkv = OtherHalf(w3, 1, part_at, PARTS)
    half_out = OtherHalf(w_out, 0, part_at, 4)
    half_up = OtherHalf(w_up, 1, part_at, PARTS)
    half_down = OtherHalf(w_down, 0, part_at, PARTS)
    half_qkv.over_tensor()
    tok_here = tokens[0]
    tok_swapped = swap(tok_here)
    facts = jnp.stack([lengths[0], adapter_ids[0]])
    facts_other = flip("core")(facts)
    mine = jnp.where(core == tensor, facts, facts_other)
    theirs = jnp.where(core == tensor, facts_other, facts)
    length, adapter, adapter_other = mine[0], mine[1], theirs[1]
    scal = jnp.stack([length, core, part_at, core == tensor, adapter]).astype(jnp.int32)

    qkv_b, out_b, up_b, down_b = (jnp.swapaxes(table, -1, -2) for table in (qkv_b, out_b, up_b, down_b))
    pick = lambda table, index: lax.dynamic_index_in_dim(table, index, 0, False)
    flat = lambda table: jnp.swapaxes(table, 0, 1).reshape(rank, 3 * third)
    half_qkv.parts[0] = after(half_qkv.parts[0], half_out.mine, half_up.mine, half_down.mine)
    half_qkv.hop(0, "x")
    half_qkv.hop(0, "zb")
    packed_first = jnp.concatenate([flat(pick(qkv_b, adapter_other)), pick(out_a, adapter_other)], axis=1)
    qa, oa = pick(qkv_a, adapter), pick(out_a, adapter)
    qb = flat(pick(qkv_b, adapter))
    gain_one, gain_two, scale_one, scale_two = (v.reshape(1, width) for v in (gain_one, gain_two, scale_one, scale_two))

    other_tables = flip("tensor")(packed_first)
    half_up.over_tensor(half_qkv.parts[4])
    half_qkv.last_hop()
    half_qkv.parts[6] = after(half_qkv.parts[6], scal, qa, qb, other_tables, half_up.mine)
    tok_swapped = after(tok_swapped, half_qkv.parts[2], half_qkv.parts[4], other_tables, scal, half_out.mine, half_down.mine)
    tok, n1, rank_qkv, q_a, own_a = qkv_local(scal, tok_here, tok_swapped, gain_one, w3, qa, qb)
    half_qkv.pairs_over_cores()
    kv_a = flip("core")(own_a)
    later_other = after(adapter_other, n1)
    packed = jnp.concatenate([pick(table, later_other) for table in (up_b, down_a)], axis=1)
    q_b, own_b, w3_other = qkv_other(scal, after(n1, half_up.parts[0], packed), rank_qkv, other_tables, half_qkv)
    kv_b = flip("core")(own_b)
    half_out.over_tensor(own_b)
    half_up.hop(0, "x", own_b)
    half_up.hop(0, "zb", own_b)
    cot_swapped = swap(after(cotangent[0], own_b))
    mix_a, logs_a = attend(scal, after(q_a, own_b), own_a, kv_a)
    half_out.hop(0, "x", mix_a)
    half_up.hop(4, "x", mix_a)
    half_down.over_tensor(mix_a)
    mix_b, logs_b = attend(scal, after(q_b, mix_a, half_up.parts[2], half_up.parts[4]), own_b, kv_b)
    half_out.pairs_over_cores(mix_b)
    half_down.hop(0, "x", mix_b)
    half_down.hop(0, "zb", mix_b)
    residual, n2, rank_out, rank_up, out_other = branch(
        scal, after(mix_a, half_up.parts[6], half_down.parts[0]), mix_b, tok, w_out, half_out, oa, other_tables, out_b, scale_one, gain_two, up_a
    )
    half_down.hop(2, "zb", n2)
    other_units = flip("tensor")(after(packed, mix_b))
    evens = (0, 2, 4, 6)
    ups = after([half_up.parts[near] for near in evens], mix_b)
    ups_odd = flip("core")(jnp.stack(ups))
    for near in evens[:3]:
        half_down.hop(near, "core", n2)
    cot = jnp.where(core == tensor, cotangent[0], cot_swapped)
    grad_mlp, grad_rank, m, g, rd, gru, gub_a, gda_a = mlp(
        scal, after(n2, half_down.parts[2], half_down.parts[4], other_units), rank_up, up_b, down_a, [w_up], [w_down],
        [cot, scale_two, down_b],
    )
    half_down.hop(6, "core", m)
    nears = evens + tuple(near + 1 for near in evens)
    m, g, rd, gru, gub_b, gda_b = mlp(
        scal, n2, rank_up, other_units, other_units, [*ups, ups_odd], [half_down.parts[near] for near in nears],
        [grad_mlp, grad_rank], nears, (m, g, rd, gru),
    )
    layer, grad_res, grad_a, grad_b, goa_a, goa_b, gob, gua, gdb = middle(
        scal,
        (residual, m, g, rd, gru, cot, mix_a, mix_b, rank_out, n2, grad_mlp),
        (down_b, up_a, scale_two, gain_two, scale_one, w_out, out_other, oa, other_tables, out_b),
    )
    shares = Sum.shares(
        jnp.concatenate([goa_a, gub_a, gda_a], axis=1),
        jnp.concatenate([gob, gua, gdb], axis=1),
        jnp.concatenate([goa_b, gub_b, gda_b], axis=1),
        core,
    )
    early = Sum(*shares, third // 2 + units, adapter, core, tensor)
    early.over_cores()

    def back(queries, own, kv, mixed, grad, logs, piece, pieces, *others):
        return attend_back(scal, after(queries, *others), own, kv, mixed, grad, logs, piece, pieces)

    def exchanged(back, *others):
        return back[0], back[1], flip("core")(after(back[2], *others) if others else back[2])


    side_a = (q_a, own_a, kv_a, mix_a, grad_a, logs_a)
    side_b = (q_b, own_b, kv_b, mix_b, grad_b, logs_b)
    early.start_pair()
    back_1 = back(*side_a, 0, 2, early.send)
    early.arrive(back_1[0])
    early.start("hi")
    back_1 = exchanged(back_1, early.images)
    layer_swapped = swap(after(layer, back_1[0]))
    back_2 = back(*side_a, 1, 2, early.images)
    early.arrive(back_2[0])
    early.start("zb")
    back_2 = exchanged(back_2, early.images)
    back_3 = back(*side_b, 0, 2, early.images)
    early.arrive(back_3[0])
    early.start("x")
    back_3 = exchanged(back_3, early.images)
    back_4 = exchanged(back(*side_b, 1, 2, early.images, layer_swapped))
    kv_sum_a, kv_sum_b, ranked, kept, sent = qkv_tables(
        scal,
        [list(pair) for pair in zip(back_1, back_2)],
        [list(pair) for pair in zip(back_3, back_4)],
        qb, other_tables, n1, rank_qkv,
    )
    early.arrive(kept)
    late = Sum(kept, after(sent, early.pair[1]), 3 * third // 2, None, core, tensor)
    late.over_cores()
    late.start_pair()
    early.arrive(late.send)
    ids = early.over_adapters(None, adapters)
    late.arrive(early.dense)
    late.start("hi")
    grad_rows = qkv_rows(
        0, 1, [back_1[0], back_2[0], kv_sum_a], [back_3[0], back_4[0], kv_sum_b],
        after(w3, late.images), w3_other, ranked, qa, tok, gain_one, grad_res,
    )
    late.arrive(grad_rows)
    grad_rows_swapped = swap(after(grad_rows, late.pair[1]))
    early.other = after(early.other, grad_rows)
    late.start("zb")
    late.start("x")
    late.arrive(grad_rows_swapped)
    in_place_already = core == tensor
    grad_tokens = jnp.where(in_place_already, grad_rows, grad_rows_swapped).astype(F32)
    layer_out = jnp.where(in_place_already, layer, layer_swapped)
    late.over_adapters(ids, adapters)
    ends = (0, third, third + units, third + 2 * units)
    spans = [(False, ends[k], ends[k + 1]) for k in range(3)] + [(True, k * width, (k + 1) * width) for k in range(3)]
    widths = (third, units, units, width, width, width)
    sum_oa, sum_ub, sum_da, sum_ob, sum_ua, sum_db = early.finish(
        spans, [(k, None) for k in range(6)], [(adapters, rank, size) for size in widths], 20e-6
    )
    sum_qb, sum_qa = late.finish(
        [(False, c * third, (c + 1) * third) for c in range(3)] + [(True, 0, width)],
        [(0, c) for c in range(3)] + [(1, None)],
        [(adapters, 3, rank, third), (adapters, rank, width)],
    )
    turn = lambda table: jnp.swapaxes(table, -1, -2)
    return (
        layer_out[None],
        grad_tokens[None],
        sum_qa,
        turn(sum_qb),
        sum_oa,
        turn(sum_ob),
        sum_ua,
        turn(sum_ub),
        sum_da,
        turn(sum_db),
    )


def solution(mesh):
    groups, split = mesh.shape["dp"], mesh.shape["tensor"]
    if split == 2 and groups % 8 == 0:
        mesh = Mesh(mesh.devices.reshape(groups // 8, 2, 2, 2, 2), ("hi", "zb", "x", "core", "tensor"))
        dp, body = ("hi", "zb", "x", "core"), quad_body
    else:
        dp, body = "dp", plain_body
    slots = P(dp, "tensor", None)
    in_specs = (
        slots, slots, P(dp), P(dp), P(), P(), P(), P(),
        P(None, None, "tensor"), P("tensor", None), P(None, "tensor"), P("tensor", None),
        P(), P(None, None, "tensor", None), P(None, None, "tensor"), P(),
        P(), P(None, "tensor", None), P(None, None, "tensor"), P(),
    )
    out_specs = (
        slots, slots, P(), P(None, None, "tensor", None), P(None, None, "tensor"), P(),
        P(), P(None, "tensor", None), P(None, None, "tensor"), P(),
    )
    return jax.shard_map(body, mesh=mesh, in_specs=in_specs, out_specs=out_specs, check_vma=False)
```
